128 devices in a mesh: seq: 16 (over x, y_lo, core), tp: 8 (over y_hi, z).
Axes of the slice: x: 4, y: 4 (y_hi: 2, y_lo: 2; y = y_hi * 2 + y_lo), z: 4, core: 2. Of those that a mesh axis runs over, the one named last changes fastest.
Arguments:
- query_proj: bfloat16 [2560, 4096], P('seq', 'tp'), may hold values from -6 to 6
- key_proj: bfloat16 [2560, 4096], P('seq', 'tp'), may hold values from -6 to 6
- value_proj: bfloat16 [2560, 4096], P('seq', 'tp'), may hold values from -6 to 6
- query_tan: bfloat16 [2560, 4096], P('seq', 'tp'), may hold values from -6 to 6
- key_tan: bfloat16 [2560, 4096], P('seq', 'tp'), may hold values from -6 to 6
- value_tan: bfloat16 [2560, 4096], P('seq', 'tp'), may hold values from -6 to 6
- out_weight: bfloat16 [4096, 4096], P('tp'), may hold values from -0.09375 to 0.09375
- noisy_latent: bfloat16 [2560, 4096], P(('seq', 'tp')), may hold values from -20 to 20
- latent_velocity: bfloat16 [2560, 4096], P(('seq', 'tp')), may hold values from -20 to 20
- time_index: int32 [16], replicated, may hold values from 0 to 63
- frame_lengths: int32 [16], replicated, may hold values from 1 to 320, 2560 in all
Outputs:
- grad_query: bfloat16 [2560, 4096], P('seq', 'tp')
- grad_key: bfloat16 [2560, 4096], P('seq', 'tp')
- grad_value: bfloat16 [2560, 4096], P('seq', 'tp')
- grad_out_proj: bfloat16 [4096, 4096], P('tp', 'seq')
The draws below stay inside these ranges and needn't reach their ends.
All inputs are finite; a program needn't handle non-finite values.
Results may differ from the reference program's by a relative error of at most 0.025.
Values may be sent and summed in bfloat16 or wider, within the bound.
A program may use at most 64 MiB of HBM per device.

```python
import math
import jax
import jax.numpy as jnp
import numpy as np
from jax import lax

DMODEL = 4096
HEADS = 32
HEAD_DIM = 128
TSTEPS = 64
FRAMES = 16
TOKENS = 2560


def field_scales(row_key, column_key):
    row_index = jnp.arange(TOKENS, dtype=jnp.float32)
    rising = 1.0 + 2.0 * row_index / (TOKENS - 1)
    row_scale = jnp.exp(jax.random.uniform(row_key, (TOKENS,), jnp.float32, 0.0, math.log(10.0)))
    column_scale = jnp.exp(jax.random.uniform(column_key, (DMODEL,), jnp.float32, 0.0, math.log(10.0)))
    return (rising, row_scale, column_scale)


def draw_query_proj(key, part):
    key = jax.random.fold_in(key, 3)
    base = jnp.clip(1.5 * jax.random.normal(key, (TOKENS, DMODEL), jnp.float32), -6.0, 6.0)
    return base.astype(jnp.bfloat16)


def draw_key_proj(key, part):
    key = jax.random.fold_in(key, 4)
    base = jnp.clip(1.5 * jax.random.normal(key, (TOKENS, DMODEL), jnp.float32), -6.0, 6.0)
    return base.astype(jnp.bfloat16)


def draw_noisy_latent(key, part):
    key = jax.random.fold_in(key, 5)
    pieces = jax.random.split(key, 3)
    rising, row_scale, column_scale = field_scales(pieces[1], pieces[2])
    core = jnp.clip(jax.random.normal(pieces[0], (TOKENS, DMODEL), jnp.float32), -5.0, 5.0)
    return (0.01 * core * rising[:, None] * row_scale[:, None] * column_scale[None, :]).astype(jnp.bfloat16)


def draw_latent_velocity(key, part):
    key = jax.random.fold_in(key, 6)
    pieces = jax.random.split(key, 3)
    rising, row_scale, column_scale = field_scales(pieces[1], pieces[2])
    core = jnp.clip(jax.random.normal(pieces[0], (TOKENS, DMODEL), jnp.float32), -5.0, 5.0)
    return (0.01 * core * rising[:, None] * row_scale[:, None] * column_scale[None, :]).astype(jnp.bfloat16)


def touch_ends(entries, rng, smallest, top_value):
    shape = entries.shape
    spot = [jax.random.randint(jax.random.fold_in(rng, axis), (), 0, shape[axis]) for axis in range(len(shape))]
    entries = entries.at[tuple(spot)].set(smallest)
    longest = shape.index(max(shape))
    spot[longest] = (spot[longest] + 1) % shape[longest]
    return entries.at[tuple(spot)].set(top_value)


def steps_of(stream_key, dims, shards, low, largest):
    level = 1.0
    for position, parts in shards:
        steps = jax.random.uniform(jax.random.fold_in(jax.random.fold_in(stream_key, 6), position), (parts,), jnp.float32, low / len(shards), largest / len(shards))
        level = level * jnp.repeat(jnp.exp(steps), dims[position] // parts).reshape((-1,) + (1,) * (len(dims) - 1 - position))
    return level


def profile(number_of, total, most, slope):
    portions = [(1 << 20) // math.isqrt(grade ** slope) + 1 for grade in range(2, number_of + 1)]
    rest, given = total - most - (number_of - 1), [1] * (number_of - 1)
    while rest > 0:
        candidates = [i for i in range(number_of - 1) if given[i] < most]
        pool, budget = sum([portions[i] for i in candidates]), rest
        for i in candidates:
            extra = min(most - given[i], max(1, budget * portions[i] // pool), rest)
            given[i] = given[i] + extra
            rest = rest - extra
    return np.array([most] + given)


def uneven(stream_key, number_of, total, reach, skew):
    if number_of == 2:
        one = jax.random.randint(stream_key, (), max(1, total - reach), min(reach, total - 1) + 1)
        return jnp.stack([one, total - one])
    lengths = jnp.asarray(profile(number_of, total, reach, skew), jnp.int32)
    pairs = (number_of - 1) // 2
    source_of, receiver = lengths[1:1 + 2 * pairs:2], lengths[2:2 + 2 * pairs:2]
    margin = jnp.minimum(source_of - 1, reach - receiver)
    passed = jax.random.randint(jax.random.fold_in(stream_key, 1), (pairs,), 0, 1 << 20) % (margin + 1)
    lengths = lengths.at[1:1 + 2 * pairs:2].set(source_of - passed).at[2:2 + 2 * pairs:2].set(receiver + passed)
    return lengths[jax.random.permutation(jax.random.fold_in(stream_key, 2), number_of)]


def scatter_about(rng, dims, deviation, limit, cuts=(), kind=jnp.bfloat16):
    values = jax.random.normal(rng, dims, jnp.float32) * deviation
    if len(cuts) > 0:
        values = steps_of(rng, dims, cuts, -0.22, 0.18) * values
    return jnp.clip(values, min=-limit, max=limit).astype(kind)


def setup_inputs(seed: int = 0) -> dict:
    keys = jax.random.split(jax.random.key(seed), 12)
    query_proj = draw_query_proj(jax.random.fold_in(keys[11], 71), 0)
    key_proj = draw_key_proj(jax.random.fold_in(keys[11], 71), 0)
    value_proj = scatter_about(keys[2], (TOKENS, DMODEL), 1.0, 6.0, ((0, 16), (1, 8)))
    query_tan = scatter_about(keys[3], (TOKENS, DMODEL), 1.0, 6.0, ((0, 16), (1, 8)))
    key_tan = scatter_about(keys[4], (TOKENS, DMODEL), 1.0, 6.0, ((0, 16), (1, 8)))
    value_tan = scatter_about(keys[5], (TOKENS, DMODEL), 1.0, 6.0, ((0, 16), (1, 8)))
    out_weight = scatter_about(keys[6], (DMODEL, DMODEL), DMODEL ** -0.5, 0.09375, ((0, 8),))
    noisy_latent = draw_noisy_latent(jax.random.fold_in(keys[11], 71), 0)
    latent_velocity = draw_latent_velocity(jax.random.fold_in(keys[11], 71), 0)
    time_index = touch_ends(jax.random.randint(keys[9], (FRAMES,), 0, TSTEPS), jax.random.fold_in(keys[9], 1), 0, TSTEPS - 1).astype(jnp.int32)
    frame_lengths = uneven(keys[10], FRAMES, TOKENS, TOKENS // 8, 2).astype(jnp.int32)
    return {"query_proj": query_proj, "key_proj": key_proj, "value_proj": value_proj, "query_tan": query_tan, "key_tan": key_tan, "value_tan": value_tan, "out_weight": out_weight, "noisy_latent": noisy_latent, "latent_velocity": latent_velocity, "time_index": time_index, "frame_lengths": frame_lengths}


def reference(query_proj, key_proj, value_proj, query_tan, key_tan, value_tan, out_weight, noisy_latent, latent_velocity, time_index, frame_lengths):
    scale = 1.0 / math.sqrt(HEAD_DIM)
    highest = lax.Precision.HIGHEST
    frame_ends = jnp.cumsum(frame_lengths).astype(jnp.int32)
    positions = jnp.arange(TOKENS, dtype=jnp.int32)
    frames = lax.optimization_barrier(jnp.sum((positions[:, None] >= frame_ends[None, :]).astype(jnp.int32), axis=1))
    allowed = frames[None, :] <= frames[:, None]

    def per_head(array):
        return jnp.transpose(array.reshape(TOKENS, HEADS, HEAD_DIM), (1, 0, 2))

    def merged(array):
        return jnp.transpose(array, (1, 0, 2)).reshape(TOKENS, DMODEL)

    def probabilities(query_head, key_head):
        scores = scale * jnp.dot(query_head, key_head.T, preferred_element_type=jnp.float32)
        masked = jnp.where(allowed, scores, -1e+30)
        top = lax.optimization_barrier(jnp.max(masked, axis=1, keepdims=True))
        weights = jnp.where(allowed, jnp.exp(masked - top), 0.0)
        return weights / lax.optimization_barrier(jnp.sum(weights, axis=1, keepdims=True))

    def head_forward(members):
        query_head, key_head, value_head, query_dot, key_dot, value_dot = members
        probs = probabilities(query_head, key_head)
        score_tan = scale * (jnp.dot(query_dot, key_head.T, preferred_element_type=jnp.float32) + jnp.dot(query_head, key_dot.T, preferred_element_type=jnp.float32))
        weighted = probs * score_tan
        value_wide = value_head.astype(jnp.float32)
        attn = jnp.dot(probs, value_wide, precision=highest, preferred_element_type=jnp.float32)
        mean_tan = lax.optimization_barrier(jnp.sum(weighted, axis=1, keepdims=True))
        attn_tan = jnp.dot(weighted, value_wide, precision=highest, preferred_element_type=jnp.float32) + jnp.dot(probs, value_dot.astype(jnp.float32), precision=highest, preferred_element_type=jnp.float32) - mean_tan * attn
        return (attn.astype(jnp.bfloat16), attn_tan.astype(jnp.bfloat16))
    attn_heads, tan_heads = lax.map(head_forward, (per_head(query_proj), per_head(key_proj), per_head(value_proj), per_head(query_tan), per_head(key_tan), per_head(value_tan)))
    attn_out = merged(attn_heads)
    attn_tan = merged(tan_heads)
    branch = jnp.dot(attn_out, out_weight, preferred_element_type=jnp.float32)
    branch_tan = jnp.dot(attn_tan, out_weight, preferred_element_type=jnp.float32)
    frame_hits = (frames[:, None] == jnp.arange(FRAMES, dtype=jnp.int32)[None, :]).astype(jnp.float32)
    levels = lax.optimization_barrier(jnp.sum(frame_hits * time_index[None, :].astype(jnp.float32), axis=1, keepdims=True))
    angle = (levels + 0.5) * (math.pi / (2 * TSTEPS))
    cosine = jnp.cos(angle)
    sine = jnp.sin(angle)
    target = -(cosine * cosine) * (0.5 * branch - latent_velocity.astype(jnp.float32)) - sine * cosine * (noisy_latent.astype(jnp.float32) + 0.5 * branch_tan)
    mean_square = jnp.mean(target * target)
    cotangent = (-target * lax.rsqrt(mean_square + 1e-05)).astype(jnp.bfloat16)
    grad_attn = jnp.dot(cotangent, out_weight.T, preferred_element_type=jnp.float32).astype(jnp.bfloat16)
    grad_out_proj = jnp.dot(attn_out.T, cotangent, preferred_element_type=jnp.float32).astype(jnp.bfloat16)

    def head_backward(members):
        query_head, key_head, value_head, grad_head, attn_head = members
        probs = probabilities(query_head, key_head)
        probs16 = probs.astype(jnp.bfloat16)
        value_grad = jnp.dot(probs16.T, grad_head, preferred_element_type=jnp.float32)
        prob_grad = jnp.dot(grad_head, value_head.T, preferred_element_type=jnp.float32)
        dterm = lax.optimization_barrier(jnp.sum(grad_head.astype(jnp.float32) * attn_head.astype(jnp.float32), axis=1, keepdims=True))
        score_grad = (probs * (prob_grad - dterm)).astype(jnp.bfloat16)
        query_grad = scale * jnp.dot(score_grad, key_head, preferred_element_type=jnp.float32)
        key_grad = scale * jnp.dot(score_grad.T, query_head, preferred_element_type=jnp.float32)
        return (query_grad.astype(jnp.bfloat16), key_grad.astype(jnp.bfloat16), value_grad.astype(jnp.bfloat16))
    query_grads, key_grads, value_grads = lax.map(head_backward, (per_head(query_proj), per_head(key_proj), per_head(value_proj), per_head(grad_attn), attn_heads))
    return (merged(query_grads), merged(key_grads), merged(value_grads), grad_out_proj)
```

```python
import math

import jax
import jax.numpy as jnp
from jax import lax
from jax.experimental import pallas as pl
from jax.experimental.pallas import tpu as pltpu
from jax.sharding import PartitionSpec as P

HD = 128
TSTEPS = 64
FRAMES = 16
ROWS = 160
UNIT = 320
NCHIP = 8
NQ = 640
SCALE = 1.0 / math.sqrt(HD)
MESH = pl.DeviceIdType.MESH
F32 = jnp.float32
BF16 = jnp.bfloat16


def dot_nt(a, b):
    return lax.dot_general(a, b, (((1,), (1,)), ((), ())), preferred_element_type=F32)


def dot_nn(a, b):
    return lax.dot_general(a, b, (((1,), (0,)), ((), ())), preferred_element_type=F32)


def dot_tn(a, b):
    return lax.dot_general(a, b, (((0,), (0,)), ((), ())), preferred_element_type=F32)


def kernel(
    frame_ref,
    time_ref,
    q_ref,
    k_ref,
    v_ref,
    qd_ref,
    kd_ref,
    vd_ref,
    w_hbm,
    noisy_ref,
    vel_ref,
    dq_out,
    dk_out,
    dv_out,
    gw_out,
    ms_out,
    w,
    kk,
    vv,
    qq,
    sbuf,
    stbuf,
    p16,
    acc1,
    acc2,
    ublk,
    uown,
    at_own,
    at,
    negb,
    part,
    rs_rx,
    cot,
    g_tx,
    g,
    dqt,
    dq_tx,
    dq_rx,
    dkv,
    sib_rx,
    dkv_tx,
    dkv_rx,
    tw,
    sq_tp,
    sq_seq,
    wsem,
    kv_send,
    kv_recv,
    fw_send,
    fw_recv,
    q_send,
    q_recv,
    u_send,
    u_recv,
    at_send,
    at_recv,
    atf_send,
    atf_recv,
    rs_send,
    rs_recv,
    t_send,
    t_recv,
    g_send,
    g_recv,
    tw_send,
    tw_recv,
    dq_send,
    dq_recv,
    sib_send,
    sib_recv,
    dkv_send,
    dkv_recv,
    sqt_send,
    sqt_recv,
    sqs_send,
    sqs_recv,
):
    s = lax.axis_index("seq")
    t = lax.axis_index("tp")
    x = s // 4
    y = (s // 2) % 2
    c = s % 2
    m = s // 2
    yh = t // 4
    z = t % 4
    j = s % 4
    head = x

    chips = [(dx, dy) for dx in (2, 1, 3, 0) for dy in (1, 0)]
    far_chips = [d for d in chips if d != (0, 0)]
    tps = [(a, b) for a in (1, 0) for b in (2, 1, 3, 0) if a or b]

    def chip_at(dx, dy):
        return lax.rem(x + dx, 4), lax.rem(y + dy, 2)

    def chip_dev(dx, dy):
        cx, cy = chip_at(dx, dy)
        return cx * 4 + cy * 2 + c

    def tp_at(dyh, dz):
        return lax.rem(yh + dyh, 2) * 4 + lax.rem(z + dz, 4)

    def tp_from(dyh, dz):
        return lax.rem(yh + 2 - dyh, 2) * 4 + lax.rem(z + 4 - dz, 4)

    def remote(src, dst, ssem, rsem, dev):
        return pltpu.make_async_remote_copy(
            src_ref=src, dst_ref=dst, send_sem=ssem, recv_sem=rsem, device_id=dev, device_id_type=MESH
        )

    def lanes(index, width):
        return pl.ds(pl.multiple_of(index * width, width), width)

    def wait_for(ref, sem):
        pltpu.make_async_copy(ref, ref, sem).wait()

    wload = pltpu.make_async_copy(w_hbm, w, wsem)
    wload.start()

    barrier = pltpu.get_barrier_semaphore()
    sibling = s + 1 - 2 * c
    for d in range(1, 16):
        pl.semaphore_signal(barrier, inc=1, device_id=(lax.rem(s + d, 16), t), device_id_type=MESH)
    for dyh, dz in tps:
        pl.semaphore_signal(barrier, inc=1, device_id=(s, tp_at(dyh, dz)), device_id_type=MESH)
    pl.semaphore_wait(barrier, 22)

    kv_src = (k_ref, kd_ref, v_ref, vd_ref)
    kv_dst = ((kk, 0), (kk, 1), (vv, 0), (vv, 1))

    def kv_copy(a, i, dx, dy):
        hx, hy = chip_at(dx, dy)
        buf, half = kv_dst[a]
        return remote(
            kv_src[a].at[:, lanes(hx, HD)],
            buf.at[m, c, :, half * HD : (half + 1) * HD],
            kv_send.at[a, i],
            kv_recv.at[a],
            (hx * 4 + hy * 2 + c, t),
        )

    def kv_local(a):
        buf, half = kv_dst[a]
        return pltpu.make_async_copy(
            kv_src[a].at[:, lanes(x, HD)],
            buf.at[m, c, :, half * HD : (half + 1) * HD],
            kv_recv.at[a],
        )

    def to_heads(src_of, dst, send, recv, slot, act):
        qj = jnp.where(m < 4, m, 7 - m)
        qu = m // 4
        for dx in range(4):
            hx = lax.rem(x + dx, 4)
            dev = hx * 4 + qj
            if dx:
                copy = remote(src_of(hx), dst(qu), send.at[slot, dx], recv, (dev, t))
                copy.start() if act == "start" else copy.wait_send()
            else:

                @pl.when(dev != s)
                def _():
                    copy = remote(src_of(hx), dst(qu), send.at[slot, dx], recv, (dev, t))
                    copy.start() if act == "start" else copy.wait_send()

                if act == "start":

                    @pl.when(dev == s)
                    def _():
                        pltpu.make_async_copy(src_of(hx), dst(qu), recv).start()

    def to_owners(src, dst, send, recv, act):
        for u in range(2):
            um = j if u == 0 else 7 - j
            for core in range(2):
                dev = um * 2 + core

                @pl.when(dev != s)
                def _():
                    copy = remote(src.at[u, core], dst, send.at[u, core], recv, (dev, t))
                    copy.start() if act == "start" else copy.wait_send()

                if act == "start":

                    @pl.when(dev == s)
                    def _():
                        pltpu.make_async_copy(src.at[u, core], dst, recv).start()

    def q_moves(act):
        for a, ref in ((1, q_ref), (0, qd_ref)):
            to_heads(
                lambda hx, ref=ref: ref.at[:, lanes(hx, HD)],
                lambda qu, a=a: qq.at[qu, c, :, a * HD : (a + 1) * HD],
                q_send,
                q_recv,
                a,
                act,
            )

    def kv_start(a):
        kv_local(a).start()
        for i, (dx, dy) in enumerate(far_chips):
            kv_copy(a, i, dx, dy).start()

    kv_start(0)
    q_moves("start")
    kv_start(1)
    kv_start(2)
    kv_start(3)

    ends = []
    total = 0
    for f in range(FRAMES):
        total = total + frame_ref[f]
        ends.append(total)
    times = [time_ref[f] for f in range(FRAMES)]

    def frame_facts(pos):
        kend = jnp.zeros(pos.shape, jnp.int32) + ends[FRAMES - 1]
        level = jnp.zeros(pos.shape, jnp.int32) + times[FRAMES - 1]
        for f in range(FRAMES - 2, -1, -1):
            inside = pos < ends[f]
            kend = jnp.where(inside, ends[f], kend)
            level = jnp.where(inside, times[f], level)
        angle = (level.astype(F32) + 0.5) * (math.pi / (2 * TSTEPS))
        return kend, jnp.cos(angle), jnp.sin(angle)

    lane = lax.broadcasted_iota(jnp.int32, (1, NQ), 1)
    qpos = jnp.where(lane < UNIT, UNIT * j + lane, UNIT * (7 - j) + lane - UNIT)
    kend, cosq, sinq = frame_facts(qpos)

    rpos = s * ROWS + t * 20 + lax.broadcasted_iota(jnp.int32, (20, 1), 0)
    _, cosr, sinr = frame_facts(rpos)
    negb[...] = jnp.zeros_like(negb)
    negb[0:20, :] = sinr * cosr * noisy_ref[...].astype(F32) - cosr * cosr * vel_ref[...].astype(F32)

    def fw_copy(a):
        buf, half = kv_dst[a]
        view = buf.at[:, c, :, half * HD : (half + 1) * HD]
        return remote(view, view, fw_send.at[a], fw_recv.at[a], (sibling, t))

    def kv_forward(a):
        buf, half = kv_dst[a]
        wait_for(buf.at[:, c, :, half * HD : (half + 1) * HD], kv_recv.at[a])
        fw_copy(a).start()

    def kv_arrived(a):
        fw_copy(a).wait_recv()

    n0 = j + 2
    n1 = jnp.minimum(9 - j, 8)

    def over_keys(body, carry):
        carry = lax.fori_loop(0, n0, lambda i, st: body(i, st, 0), carry)
        return lax.fori_loop(n0, n1, lambda i, st: body(i, st, 256), carry)

    def put(row, lo, part_row):
        if lo == 0:
            return part_row
        return jnp.concatenate([row[:, :lo], part_row], axis=1)

    kv_forward(0)
    wait_for(qq, q_recv)
    kv_arrived(0)

    def chunk(buf, i):
        return buf[i].reshape(UNIT, buf.shape[-1])

    def pass1(i, top, lo):
        keys = kk[i, :, :, :HD].reshape(UNIT, HD)
        queries = qq[...].reshape(NQ, 2 * HD)[lo:, HD:]
        sc = dot_nt(keys, queries) * SCALE
        kpos = i * UNIT + lax.broadcasted_iota(jnp.int32, (UNIT, 1), 0)
        sc = jnp.where(kpos < kend[:, lo:], sc, -1e30)
        sbuf[i, :, lo:] = sc
        return put(top, lo, jnp.maximum(top[:, lo:], jnp.max(sc, axis=0, keepdims=True)))

    top = over_keys(pass1, jnp.full((1, NQ), -1e30, F32))

    kv_forward(1)
    kv_forward(2)
    kv_forward(3)
    kv_arrived(1)

    def pass2(i, state, lo):
        den, tan = state
        st = dot_nt(chunk(kk, i), qq[...].reshape(NQ, 2 * HD)[lo:]) * SCALE
        p = jnp.exp(sbuf[i, :, lo:] - top[:, lo:])
        sbuf[i, :, lo:] = p
        stbuf[i, :, lo:] = st
        den = put(den, lo, den[:, lo:] + jnp.sum(p, axis=0, keepdims=True))
        tan = put(tan, lo, tan[:, lo:] + jnp.sum(p * st, axis=0, keepdims=True))
        return den, tan

    row0 = jnp.zeros((1, NQ), F32)
    den, tan = over_keys(pass2, (row0, row0))
    inv = 1.0 / den
    mean = tan * inv
    kv_arrived(2)
    kv_arrived(3)

    acc1[...] = jnp.zeros_like(acc1)
    acc2[...] = jnp.zeros_like(acc2)

    def pass3(i, state, lo):
        p = sbuf[i, :, lo:] * inv[:, lo:]
        ph = p.astype(BF16)
        p16[i, :, lo:] = ph
        ds = (p * (stbuf[i, :, lo:] - mean[:, lo:])).astype(BF16)
        vals = chunk(vv, i)
        acc1[:, lo:] += dot_tn(vals, ph)
        acc2[:, lo:] += dot_tn(vals[:, :HD], ds)
        return state

    over_keys(pass3, 0)
    attn_t = acc1[0:HD, :].astype(BF16)
    tan_t = (acc2[...] + acc1[HD:, :]).astype(BF16)
    at_own[...] = attn_t
    u_t = (0.5 * cosq) * (cosq * attn_t.astype(F32) + sinq * tan_t.astype(F32))
    ublk[...] = u_t.T.astype(BF16).reshape(2, 2, ROWS, HD)
    to_owners(ublk, uown.at[:, lanes(head, HD)], u_send, u_recv, "start")

    def at_copy(i, dx, dy):
        return remote(
            at_own, at.at[y, c, lanes(head, HD), :], at_send.at[i], at_recv, (chip_dev(dx, dy), t)
        )

    pltpu.make_async_copy(at_own, at.at[y, c, lanes(head, HD), :], at_recv).start()
    for i, (dx, dy) in enumerate(far_chips):
        at_copy(i, dx, dy).start()

    wload.wait()
    wait_for(uown, u_recv)
    u = uown[...]
    pick = (
        lax.broadcasted_iota(jnp.int32, (ROWS, 32), 0)
        == t * 20 + lax.broadcasted_iota(jnp.int32, (ROWS, 32), 1)
    ) & (lax.broadcasted_iota(jnp.int32, (ROWS, 32), 1) < 20)
    pick = pick.astype(F32).astype(BF16)

    def partial(tt):
        return dot_nn(u, w[:, lanes(tt, 512)]) + dot_nn(pick, negb[:, lanes(tt, 512)].astype(BF16))

    def rs_copy(dyh, dz):
        slot = dyh * 4 + dz
        return remote(
            part.at[slot], rs_rx.at[slot], rs_send.at[slot], rs_recv.at[slot], (s, tp_at(dyh, dz))
        )

    for dyh, dz in tps:
        part[dyh * 4 + dz] = partial(tp_at(dyh, dz)).astype(BF16)
        rs_copy(dyh, dz).start()
    total = partial(t)
    for dyh, dz in reversed(tps):
        rs_copy(dyh, dz).wait_recv()
        total = total + rs_rx[dyh * 4 + dz].astype(F32)
    cot[0] = total.astype(BF16)

    def t_copy(dyh, dz):
        slot = dyh * 4 + dz
        return remote(
            cot.at[0], cot.at[slot], t_send.at[slot], t_recv.at[slot], (s, tp_at(dyh, dz))
        )

    for dyh, dz in tps:
        t_copy(dyh, dz).start()

    def sqt_copy(dyh, dz):
        slot = dyh * 4 + dz
        return remote(
            sq_tp.at[0], sq_tp.at[slot], sqt_send.at[slot], sqt_recv.at[slot], (s, tp_at(dyh, dz))
        )

    sq = jnp.sum(jnp.sum(total * total, axis=0, keepdims=True), axis=1, keepdims=True)
    sq_tp[0] = jnp.zeros((8, 128), F32) + sq
    for dyh, dz in tps:
        sqt_copy(dyh, dz).start()

    grad = dot_nt(cot[0], w[:, lanes(t, 512)])
    for dyh, dz in reversed(tps):
        t_copy(dyh, dz).wait_recv()
        grad = grad + dot_nt(cot[dyh * 4 + dz], w[:, lanes(tp_from(dyh, dz), 512)])
    g_tx[...] = grad.astype(BF16)

    def g_moves(act):
        to_heads(
            lambda hx: g_tx.at[:, lanes(hx, HD)],
            lambda qu: g.at[qu, c],
            g_send,
            g_recv,
            0,
            act,
        )

    g_moves("start")

    sqv = sq_tp[0]
    for dyh, dz in tps:
        sqt_copy(dyh, dz).wait_recv()
        sqv = sqv + sq_tp[dyh * 4 + dz]
    sq_seq[0] = sqv

    def sqs_copy(d):
        return remote(
            sq_seq.at[0], sq_seq.at[d], sqs_send.at[d], sqs_recv.at[d], (lax.rem(s + d, 16), t)
        )

    for d in range(1, 16):
        sqs_copy(d).start()

    def tw_slot(src):
        sm = src // 2
        return jnp.where(sm < 4, sm, 7 - sm), sm // 4, src % 2

    def tw_view():
        a, b, e = tw_slot(s)
        return tw.at[a, b, e]

    def tw_src(dest):
        tt = dest // 2
        slot = lax.rem(yh + 2 - tt // 4, 2) * 4 + lax.rem(z + 4 - tt % 4, 4)
        return cot.at[slot, :, lanes(dest % 2, 256)]

    def tw_copy(d):
        dest = lax.rem(s + d, 16)
        return remote(tw_src(dest), tw_view(), tw_send.at[d], tw_recv, (dest, t))

    for d in range(1, 16):
        tw_copy(d).start()
    pltpu.make_async_copy(tw_src(s), tw_view(), tw_recv).start()

    wait_for(g, g_recv)
    gt = g[...].reshape(NQ, HD).astype(F32).T
    dterm = jnp.sum(gt * at_own[...].astype(F32), axis=0, keepdims=True)
    dqt[...] = jnp.zeros_like(dqt)

    def zero(i, state):
        dkv[:, i] = jnp.zeros((2, 2, ROWS, HD), BF16)
        return state

    lax.fori_loop(n1, 8, zero, 0)

    def back(i, state, lo):
        gq = g[...].reshape(NQ, HD)[lo:]
        queries = qq[...].reshape(NQ, 2 * HD)[lo:, HD:]
        keys = chunk(kk, i)[:, :HD]
        vals = chunk(vv, i)[:, :HD]
        ph = p16[i, :, lo:]
        dp = dot_nt(vals, gq)
        ds = (ph.astype(F32) * (dp - dterm[:, lo:])).astype(BF16)
        dkv[1, i] = dot_nn(ph, gq).astype(BF16).reshape(2, ROWS, HD)
        dkv[0, i] = (dot_nn(ds, queries) * SCALE).astype(BF16).reshape(2, ROWS, HD)
        dqt[:, lo:] += dot_tn(keys, ds)
        return state

    over_keys(back, 0)

    sib = remote(dkv.at[:, :, 1 - c], sib_rx, sib_send, sib_recv, (sibling, t))
    sib.start()
    dq_tx[...] = (dqt[...] * SCALE).T.astype(BF16).reshape(2, 2, ROWS, HD)
    to_owners(dq_tx, dq_rx.at[:, lanes(head, HD)], dq_send, dq_recv, "start")
    sib.wait_recv()
    dkv_tx[...] = (dkv[:, :, c].astype(F32) + sib_rx[...].astype(F32)).astype(BF16)

    def dkv_copy(dx, dy):
        cx, cy = chip_at(dx, dy)
        slot = dx * 2 + dy
        return remote(
            dkv_tx.at[:, cx * 2 + cy],
            dkv_rx.at[slot],
            dkv_send.at[slot],
            dkv_recv.at[slot],
            (chip_dev(dx, dy), t),
        )

    for dx, dy in far_chips:
        dkv_copy(dx, dy).start()

    wait_for(at.at[:, c], at_recv)
    atf = remote(at.at[:, c], at.at[:, c], atf_send, atf_recv, (sibling, t))
    atf.start()
    wait_for(tw, tw_recv)
    atf.wait_recv()

    gw = dot_nn(at[0, 0], tw[0].reshape(NQ, 256))
    for a in range(1, 4):
        gw = gw + dot_nn(at[a // 2, a % 2], tw[a].reshape(NQ, 256))
    gw_out[...] = gw

    sqv = sq_seq[0]
    for d in range(1, 16):
        sqs_copy(d).wait_recv()
        sqv = sqv + sq_seq[d]
    ms_out[...] = sqv

    wait_for(dq_rx, dq_recv)
    dq_out[...] = dq_rx[...]

    for dx in range(4):
        hx = lax.rem(x + 4 - dx, 4)
        tot = [None, None]
        for dy in (0, 1):
            if dx or dy:
                dkv_copy(dx, dy).wait_recv()
            for a in range(2):
                piece = dkv_rx[dx * 2 + dy, a] if dx or dy else dkv_tx[a, m]
                piece = piece.astype(F32)
                tot[a] = piece if tot[a] is None else tot[a] + piece
        dk_out[:, lanes(hx, HD)] = tot[0]
        dv_out[:, lanes(hx, HD)] = tot[1]

    for a in range(4):
        for i, (dx, dy) in enumerate(far_chips):
            kv_copy(a, i, dx, dy).wait_send()
        fw_copy(a).wait_send()
    q_moves("wait")
    to_owners(ublk, uown.at[:, lanes(head, HD)], u_send, u_recv, "wait")
    for i, (dx, dy) in enumerate(far_chips):
        at_copy(i, dx, dy).wait_send()
        dkv_copy(dx, dy).wait_send()
    for dyh, dz in tps:
        rs_copy(dyh, dz).wait_send()
        t_copy(dyh, dz).wait_send()
        sqt_copy(dyh, dz).wait_send()
    g_moves("wait")
    for d in range(1, 16):
        sqs_copy(d).wait_send()
        tw_copy(d).wait_send()
    sib.wait_send()
    to_owners(dq_tx, dq_rx.at[:, lanes(head, HD)], dq_send, dq_recv, "wait")
    atf.wait_send()


def on_device(q, k, v, qd, kd, vd, w, noisy, vel, time_index, frame_lengths):
    smem = pl.BlockSpec(memory_space=pltpu.SMEM)
    vmem = pl.BlockSpec(memory_space=pltpu.VMEM)
    hbm = pl.BlockSpec(memory_space=pl.ANY)
    dma = pltpu.SemaphoreType.DMA
    scratch = [
        pltpu.VMEM((512, 4096), BF16),
        pltpu.VMEM((NCHIP, 2, ROWS, 256), BF16),
        pltpu.VMEM((NCHIP, 2, ROWS, 256), BF16),
        pltpu.VMEM((2, 2, ROWS, 256), BF16),
        pltpu.VMEM((NCHIP, UNIT, NQ), F32),
        pltpu.VMEM((NCHIP, UNIT, NQ), F32),
        pltpu.VMEM((NCHIP, UNIT, NQ), BF16),
        pltpu.VMEM((256, NQ), F32),
        pltpu.VMEM((128, NQ), F32),
        pltpu.VMEM((2, 2, ROWS, HD), BF16),
        pltpu.VMEM((ROWS, 512), BF16),
        pltpu.VMEM((HD, NQ), BF16),
        pltpu.VMEM((2, 2, 512, NQ), BF16),
        pltpu.VMEM((32, 4096), F32),
        pltpu.VMEM((8, ROWS, 512), BF16),
        pltpu.VMEM((8, ROWS, 512), BF16),
        pltpu.VMEM((8, ROWS, 512), BF16),
        pltpu.VMEM((ROWS, 512), BF16),
        pltpu.VMEM((2, 2, ROWS, HD), BF16),
        pltpu.VMEM((HD, NQ), F32),
        pltpu.VMEM((2, 2, ROWS, HD), BF16),
        pltpu.VMEM((ROWS, 512), BF16),
        pltpu.VMEM((2, NCHIP, 2, ROWS, HD), BF16),
        pltpu.VMEM((2, NCHIP, ROWS, HD), BF16),
        pltpu.VMEM((2, NCHIP, ROWS, HD), BF16),
        pltpu.VMEM((NCHIP, 2, ROWS, HD), BF16),
        pltpu.VMEM((4, 2, 2, ROWS, 256), BF16),
        pltpu.VMEM((8, 8, 128), F32),
        pltpu.VMEM((16, 8, 128), F32),
        dma,
        dma((4, 7)),
        dma((4,)),
        dma((4,)),
        dma((4,)),
        dma((2, 4)),
        dma,
        dma((2, 2)),
        dma,
        dma((7,)),
        dma,
        dma,
        dma,
        dma((8,)),
        dma((8,)),
        dma((8,)),
        dma((8,)),
        dma((1, 4)),
        dma,
        dma((16,)),
        dma,
        dma((2, 2)),
        dma,
        dma,
        dma,
        dma((8,)),
        dma((8,)),
        dma((8,)),
        dma((8,)),
        dma((16,)),
        dma((16,)),
    ]
    dq, dk, dv, gw, ms = pl.pallas_call(
        kernel,
        out_shape=(
            jax.ShapeDtypeStruct((ROWS, 512), BF16),
            jax.ShapeDtypeStruct((ROWS, 512), F32),
            jax.ShapeDtypeStruct((ROWS, 512), F32),
            jax.ShapeDtypeStruct((512, 256), F32),
            jax.ShapeDtypeStruct((8, 128), F32),
        ),
        in_specs=[smem, smem] + [hbm] * 7 + [vmem] * 2,
        out_specs=(vmem,) * 5,
        scratch_shapes=scratch,
        compiler_params=pltpu.CompilerParams(
            collective_id=0, has_side_effects=True, vmem_limit_bytes=56 * 1024 * 1024
        ),
        cost_estimate=pl.CostEstimate(flops=7 * 10**9, bytes_accessed=8 * 10**6, transcendentals=1638400),
    )(frame_lengths, time_index, q, k, v, qd, kd, vd, w, noisy, vel)
    scale = lax.rsqrt(ms[0, 0] / (2560 * 4096) + 1e-05)
    return tuple((part.astype(F32) * scale).astype(BF16) for part in (dq, dk, dv, gw))


def solution(mesh):
    in_specs = (P("seq", "tp"),) * 6 + (P("tp", None), P(("seq", "tp"), None), P(("seq", "tp"), None), P(), P())
    out_specs = (P("seq", "tp"), P("seq", "tp"), P("seq", "tp"), P("tp", "seq"))
    return jax.shard_map(
        on_device, mesh=mesh, in_specs=in_specs, out_specs=out_specs, check_vma=False
    )
```

```python
import math

import jax
import jax.numpy as jnp
from jax import lax
from jax.experimental import pallas as pl
from jax.experimental.pallas import tpu as pltpu
from jax.sharding import PartitionSpec as P

HD = 128
TSTEPS = 64
FRAMES = 16
ROWS = 160
UNIT = 320
NCHIP = 8
NQ = 640
SCALE = 1.0 / math.sqrt(HD)
MESH = pl.DeviceIdType.MESH
F32 = jnp.float32
BF16 = jnp.bfloat16


def dot_nt(a, b):
    return lax.dot_general(a, b, (((1,), (1,)), ((), ())), preferred_element_type=F32)


def dot_nn(a, b):
    return lax.dot_general(a, b, (((1,), (0,)), ((), ())), preferred_element_type=F32)


def dot_tn(a, b):
    return lax.dot_general(a, b, (((0,), (0,)), ((), ())), preferred_element_type=F32)


def kernel(
    frame_ref,
    time_ref,
    q_ref,
    k_ref,
    v_ref,
    qd_ref,
    kd_ref,
    vd_ref,
    w_hbm,
    noisy_ref,
    vel_ref,
    dq_out,
    dk_out,
    dv_out,
    gw_out,
    ms_out,
    w,
    kk,
    vv,
    qq,
    sbuf,
    stbuf,
    p16,
    acc1,
    acc2,
    ublk,
    uown,
    at_own,
    at,
    negb,
    part_a,
    part_b,
    rx_a,
    rx_b,
    sum_a,
    sum_b,
    part_a2,
    part_b2,
    rx_a2,
    rx_b2,
    cot,
    g_tx,
    g,
    dqt,
    dq_tx,
    dq_rx,
    dkv,
    sib_rx,
    dkv_tx,
    dkv_rx,
    tw_part,
    tw,
    sq_tp,
    sq_seq,
    wsem,
    kvx_send,
    kvx_recv,
    kvy_send,
    kvy_recv,
    fwx_send,
    fwx_recv,
    fwy_send,
    fwy_recv,
    q_send,
    q_recv,
    u_send,
    u_recv,
    atx_send,
    atx_recv,
    aty_send,
    aty_recv,
    at2_recv,
    atf_send,
    atf_recv,
    rsa_send,
    rsa_recv,
    rsb_send,
    rsb_recv,
    rsa2_send,
    rsa2_recv,
    rsb2_send,
    rsb2_recv,
    t_send,
    t_recv,
    g_send,
    g_recv,
    tw_send,
    tw_recv,
    twg_send,
    twg_recv,
    dq_send,
    dq_recv,
    sib_send,
    sib_recv,
    dkv_send,
    dkv_recv,
    sqt_send,
    sqt_recv,
    sqs_send,
    sqs_recv,
):
    s = lax.axis_index("seq")
    t = lax.axis_index("tp")
    x = s // 4
    y = (s // 2) % 2
    c = s % 2
    m = s // 2
    yh = t // 4
    z = t % 4
    head = x
    far = (2, 1, 3)

    def ring(pos, step):
        return lax.rem(pos + step, 4)

    def seq_dev(px, py, pc):
        return (px * 4 + py * 2 + pc, t)

    def tp_dev(pyh, pz):
        return (s, pyh * 4 + pz)

    def remote(src, dst, ssem, rsem, dev):
        return pltpu.make_async_remote_copy(
            src_ref=src, dst_ref=dst, send_sem=ssem, recv_sem=rsem, device_id=dev, device_id_type=MESH
        )

    def lanes(index, width):
        return pl.ds(pl.multiple_of(index * width, width), width)

    def wait_for(ref, sem):
        pltpu.make_async_copy(ref, ref, sem).wait()

    pending = []

    def launch(copy):
        copy.start()
        pending.append(copy.wait_send)

    owed = {}

    def due(name):
        owed.pop(name)()

    def finish():
        for name in list(owed):
            due(name)
        for wait in pending:
            wait()

    wload = pltpu.make_async_copy(w_hbm, w, wsem)
    wload.start()
    owed["w"] = wload.wait

    barrier = pltpu.get_barrier_semaphore()
    sibling = s + 1 - 2 * c
    for d in range(1, 16):
        pl.semaphore_signal(barrier, inc=1, device_id=(lax.rem(s + d, 16), t), device_id_type=MESH)
    for d in range(1, 8):
        pl.semaphore_signal(barrier, inc=1, device_id=(s, lax.rem(t + d, 8)), device_id_type=MESH)
    pl.semaphore_wait(barrier, 22)

    kv_src = (k_ref, kd_ref, v_ref, vd_ref)
    kv_dst = ((kk, 0), (kk, 1), (vv, 0), (vv, 1))

    def kv_view(a, px, py, pc):
        buf, half = kv_dst[a]
        return buf.at[px, py, pc, :, half * HD : (half + 1) * HD]

    def kv_piece(a, px):
        return kv_src[a].at[:, lanes(px, HD)]

    def kv_all(a, py, pc):
        return kv_view(a, slice(None), py, pc)

    def kv_own(a):
        pltpu.make_async_copy(kv_piece(a, x), kv_view(a, x, y, c), kvx_recv.at[a]).start()
        launch(
            remote(
                kv_piece(a, x), kv_view(a, x, y, c), kvy_send.at[a, 0], kvy_recv.at[a], seq_dev(x, 1 - y, c)
            )
        )

    def kv_along_x(a):
        for dx in far:
            hx = ring(x, dx)
            launch(
                remote(
                    kv_piece(a, hx), kv_view(a, x, y, c), kvx_send.at[a, dx], kvx_recv.at[a], seq_dev(hx, y, c)
                )
            )
        owed["kvx", a] = lambda: wait_for(kv_all(a, y, c), kvx_recv.at[a])
        owed["kvy", a] = lambda: wait_for(kv_all(a, 1 - y, c), kvy_recv.at[a])

    def kv_across(a):
        due(("kvx", a))
        for dx in far:
            view = kv_view(a, ring(x, dx), y, c)
            launch(remote(view, view, kvy_send.at[a, dx], kvy_recv.at[a], seq_dev(x, 1 - y, c)))
        to_sibling(a, y, fwx_send, fwx_recv, "fwx")

    def to_sibling(a, py, send, recv, name):
        view = kv_all(a, py, c)
        launch(remote(view, view, send.at[a], recv.at[a], (sibling, t)))
        owed[name, a] = lambda: wait_for(kv_all(a, py, 1 - c), recv.at[a])

    def kv_received(a):
        due(("kvy", a))
        to_sibling(a, 1 - y, fwy_send, fwy_recv, "fwy")

    def kv_complete(a):
        due(("fwx", a))
        due(("fwy", a))

    home = jnp.where((x == 1) | (x == 2), 1, 0)
    unit = x // 2

    def to_heads(src_of, dst, send, recv, slot, act):
        for dx in (2, 1, 3, 0):
            hx = ring(x, dx)
            if dx:
                copy = remote(src_of(hx), dst, send.at[slot, dx], recv, seq_dev(hx, y, home))
                copy.start() if act == "start" else copy.wait_send()
            else:

                @pl.when(home != c)
                def _():
                    copy = remote(src_of(hx), dst, send.at[slot, dx], recv, seq_dev(hx, y, home))
                    copy.start() if act == "start" else copy.wait_send()

                if act == "start":

                    @pl.when(home == c)
                    def _():
                        pltpu.make_async_copy(src_of(hx), dst, recv).start()

    def to_owners(src, dst, send, recv, act):
        for u in range(2):
            ux = c if u == 0 else 3 - c
            for core in range(2):
                dev = ux * 4 + y * 2 + core

                @pl.when(dev != s)
                def _():
                    copy = remote(src.at[u, core], dst, send.at[u, core], recv, (dev, t))
                    copy.start() if act == "start" else copy.wait_send()

                if act == "start":

                    @pl.when(dev == s)
                    def _():
                        pltpu.make_async_copy(src.at[u, core], dst, recv).start()

    def q_moves(act):
        for a, ref in ((1, q_ref), (0, qd_ref)):
            to_heads(
                lambda hx, ref=ref: ref.at[:, lanes(hx, HD)],
                qq.at[unit, c, :, a * HD : (a + 1) * HD],
                q_send,
                q_recv,
                a,
                act,
            )

    kv_along_x(0)
    for a in range(4):
        kv_own(a)
    q_moves("start")
    pending.append(lambda: q_moves("wait"))
    owed["q"] = lambda: wait_for(qq, q_recv)
    for a in (1, 2, 3):
        kv_along_x(a)

    ends = []
    total = 0
    for f in range(FRAMES):
        total = total + frame_ref[f]
        ends.append(total)
    times = [time_ref[f] for f in range(FRAMES)]

    def frame_facts(pos):
        kend = jnp.zeros(pos.shape, jnp.int32) + ends[FRAMES - 1]
        level = jnp.zeros(pos.shape, jnp.int32) + times[FRAMES - 1]
        for f in range(FRAMES - 2, -1, -1):
            inside = pos < ends[f]
            kend = jnp.where(inside, ends[f], kend)
            level = jnp.where(inside, times[f], level)
        angle = (level.astype(F32) + 0.5) * (math.pi / (2 * TSTEPS))
        return kend, jnp.cos(angle), jnp.sin(angle)

    lane = lax.broadcasted_iota(jnp.int32, (1, NQ), 1)
    chip0 = 2 * c + y
    chip1 = 2 * (3 - c) + y
    qpos = jnp.where(lane < UNIT, UNIT * chip0 + lane, UNIT * chip1 + lane - UNIT)
    kend, cosq, sinq = frame_facts(qpos)

    rpos = s * ROWS + t * 20 + lax.broadcasted_iota(jnp.int32, (20, 1), 0)
    _, cosr, sinr = frame_facts(rpos)
    negb[...] = jnp.zeros_like(negb)
    negb[0:20, :] = sinr * cosr * noisy_ref[...].astype(F32) - cosr * cosr * vel_ref[...].astype(F32)

    n0 = chip0 + 2
    n1 = jnp.minimum(chip1 + 2, 8)

    def over_keys(body, carry):
        carry = lax.fori_loop(0, n0, lambda i, st: body(i, st, 0), carry)
        return lax.fori_loop(n0, n1, lambda i, st: body(i, st, 256), carry)

    def put(row, lo, part_row):
        if lo == 0:
            return part_row
        return jnp.concatenate([row[:, :lo], part_row], axis=1)

    kv_across(0)
    kv_across(1)
    kv_received(0)
    kv_across(2)
    due("q")
    kv_complete(0)

    def chunk(buf, i):
        return buf[i // 2, i % 2].reshape(UNIT, buf.shape[-1])

    def pass1(i, top, lo):
        keys = kk[i // 2, i % 2, :, :, :HD].reshape(UNIT, HD)
        queries = qq[...].reshape(NQ, 2 * HD)[lo:, HD:]
        sc = dot_nt(keys, queries) * SCALE
        kpos = i * UNIT + lax.broadcasted_iota(jnp.int32, (UNIT, 1), 0)
        sc = jnp.where(kpos < kend[:, lo:], sc, -1e30)
        sbuf[i, :, lo:] = sc
        return put(top, lo, jnp.maximum(top[:, lo:], jnp.max(sc, axis=0, keepdims=True)))

    top = over_keys(pass1, jnp.full((1, NQ), -1e30, F32))

    kv_across(3)
    kv_received(1)
    kv_complete(1)
    kv_received(2)

    def pass2(i, state, lo):
        den, tan = state
        st = dot_nt(chunk(kk, i), qq[...].reshape(NQ, 2 * HD)[lo:]) * SCALE
        p = jnp.exp(sbuf[i, :, lo:] - top[:, lo:])
        sbuf[i, :, lo:] = p
        stbuf[i, :, lo:] = st
        den = put(den, lo, den[:, lo:] + jnp.sum(p, axis=0, keepdims=True))
        tan = put(tan, lo, tan[:, lo:] + jnp.sum(p * st, axis=0, keepdims=True))
        return den, tan

    row0 = jnp.zeros((1, NQ), F32)
    den, tan = over_keys(pass2, (row0, row0))
    inv = 1.0 / den
    mean = tan * inv
    kv_received(3)
    kv_complete(2)
    kv_complete(3)

    acc1[...] = jnp.zeros_like(acc1)
    acc2[...] = jnp.zeros_like(acc2)

    def pass3(i, state, lo):
        p = sbuf[i, :, lo:] * inv[:, lo:]
        ph = p.astype(BF16)
        p16[i, :, lo:] = ph
        ds = (p * (stbuf[i, :, lo:] - mean[:, lo:])).astype(BF16)
        vals = chunk(vv, i)
        acc1[:, lo:] += dot_tn(vals, ph)
        acc2[:, lo:] += dot_tn(vals[:, :HD], ds)
        return state

    over_keys(pass3, 0)
    attn_t = acc1[0:HD, :].astype(BF16)
    tan_t = (acc2[...] + acc1[HD:, :]).astype(BF16)
    at_own[...] = attn_t
    u_t = (0.5 * cosq) * (cosq * attn_t.astype(F32) + sinq * tan_t.astype(F32))
    ublk[...] = u_t.T.astype(BF16).reshape(2, 2, ROWS, HD)
    to_owners(ublk, uown.at[:, lanes(head, HD)], u_send, u_recv, "start")
    owed["u"] = lambda: wait_for(uown, u_recv)
    pending.append(lambda: to_owners(ublk, uown.at[:, lanes(head, HD)], u_send, u_recv, "wait"))

    def at_view(py, hx):
        return at.at[py, c, lanes(hx, HD), :]

    pltpu.make_async_copy(at_own, at_view(y, x), atx_recv).start()
    launch(remote(at_own, at_view(y, x), aty_send, aty_recv, seq_dev(x, 1 - y, c)))
    owed["aty"] = lambda: wait_for(at_view(1 - y, x), aty_recv)
    for dx in far:
        launch(remote(at_own, at_view(y, x), atx_send.at[0, dx], atx_recv, seq_dev(ring(x, dx), y, c)))
    owed["atx"] = lambda: wait_for(at.at[y, c], atx_recv)

    def at_pass_on():
        due("aty")
        for dx in far:
            view = at_view(1 - y, x)
            launch(remote(view, view, atx_send.at[1, dx], at2_recv, seq_dev(ring(x, dx), y, c)))
        owed["at2"] = lambda: wait_for(at.at[1 - y, c, 0 : 3 * HD], at2_recv)

    due("w")
    due("u")
    u = uown[...]
    pick = (
        lax.broadcasted_iota(jnp.int32, (ROWS, 32), 0)
        == t * 20 + lax.broadcasted_iota(jnp.int32, (ROWS, 32), 1)
    ) & (lax.broadcasted_iota(jnp.int32, (ROWS, 32), 1) < 20)
    pick = pick.astype(F32).astype(BF16)

    def partial(pyh, pz, half):
        cols = pl.ds(pl.multiple_of((pyh * 4 + pz) * 512 + half * 256, 256), 256)
        return dot_nn(u, w[:, cols]) + dot_nn(pick, negb[:, cols].astype(BF16))

    for dz in range(4):
        part_b[dz] = partial(1 - yh, ring(z, dz), 1).astype(BF16)
    launch(remote(part_b, rx_b, rsb_send, rsb_recv, tp_dev(1 - yh, z)))
    owed["rsb"] = lambda: wait_for(rx_b, rsb_recv)

    for dz in far:
        for e in range(2):
            part_a[dz, e] = partial(yh if e == 0 else 1 - yh, ring(z, dz), 0).astype(BF16)
        copy = remote(part_a.at[dz], rx_a.at[dz], rsa_send.at[dz], rsa_recv.at[dz], tp_dev(yh, ring(z, dz)))
        launch(copy)
        owed["rsa", dz] = copy.wait_recv

    for dz in range(4):
        sum_b[dz] = partial(yh, ring(z, dz), 1)
    for e in range(2):
        sum_a[e] = partial(yh if e == 0 else 1 - yh, z, 0)

    at_pass_on()

    due("rsb")
    for dz in far:
        part_b2[dz] = (sum_b[dz] + rx_b[dz].astype(F32)).astype(BF16)
        copy = remote(part_b2.at[dz], rx_b2.at[dz], rsb2_send.at[dz], rsb2_recv.at[dz], tp_dev(yh, ring(z, dz)))
        launch(copy)
        owed["rsb2", dz] = copy.wait_recv
    for dz in far:
        due(("rsa", dz))
    other = sum_a[1]
    for dz in far:
        other = other + rx_a[dz, 1].astype(F32)
    part_a2[...] = other.astype(BF16)
    copy = remote(part_a2, rx_a2, rsa2_send, rsa2_recv, tp_dev(1 - yh, z))
    launch(copy)
    owed["rsa2"] = copy.wait_recv

    def cot_copy(a, src, dst, dev):
        sem = (a,) + dst
        copy = remote(cot.at[(a,) + src], cot.at[(a,) + dst], t_send.at[sem], t_recv.at[sem], dev)
        launch(copy)
        owed[("t",) + sem] = copy.wait_recv

    cot_b = sum_b[0] + rx_b[0].astype(F32)
    for dz in far:
        due(("rsb2", dz))
        cot_b = cot_b + rx_b2[dz].astype(F32)
    cot[1, 0, 0] = cot_b.astype(BF16)
    cot_copy(1, (0, 0), (1, 0), tp_dev(1 - yh, z))
    for dz in far:
        cot_copy(1, (0, 0), (0, dz), tp_dev(yh, ring(z, dz)))

    cot_a = sum_a[0]
    for dz in far:
        cot_a = cot_a + rx_a[dz, 0].astype(F32)
    due("rsa2")
    cot_a = cot_a + rx_a2[...].astype(F32)
    cot[0, 0, 0] = cot_a.astype(BF16)
    cot_copy(0, (0, 0), (1, 0), tp_dev(1 - yh, z))
    for dz in far:
        cot_copy(0, (0, 0), (0, dz), tp_dev(yh, ring(z, dz)))

    def sq_copy(buf, d, send, recv, dev, name):
        copy = remote(buf.at[0], buf.at[d], send.at[d], recv.at[d], dev)
        launch(copy)
        owed[name, d] = copy.wait_recv

    sq = jnp.sum(cot_a * cot_a + cot_b * cot_b, axis=0, keepdims=True)
    sq_tp[0] = jnp.zeros((8, 128), F32) + jnp.sum(sq, axis=1, keepdims=True)
    for d in range(1, 8):
        sq_copy(sq_tp, d, sqt_send, sqt_recv, (s, lax.rem(t + d, 8)), "sqt")

    def grad_part(a, dyh, dz):
        pyh = lax.rem(yh + dyh, 2)
        pz = lax.rem(z + 4 - dz, 4)
        cols = pl.ds(pl.multiple_of((pyh * 4 + pz) * 512 + a * 256, 256), 256)
        return dot_nt(cot[a, dyh, dz], w[:, cols])

    grad = grad_part(0, 0, 0) + grad_part(1, 0, 0)
    due(("t", 1, 1, 0))
    for dz in far:
        cot_copy(1, (1, 0), (1, dz), tp_dev(yh, ring(z, dz)))
    grad = grad + grad_part(1, 1, 0)
    for dz in (1, 3, 2):
        due(("t", 0, 0, dz))
        cot_copy(0, (0, dz), (1, dz), tp_dev(1 - yh, z))
    for dz in (1, 3, 2):
        grad = grad + grad_part(0, 0, dz)
        due(("t", 1, 0, dz))
        grad = grad + grad_part(1, 0, dz)
    for a, dz in ((0, 0), (0, 1), (0, 3), (0, 2), (1, 1), (1, 3), (1, 2)):
        due(("t", a, 1, dz))
        grad = grad + grad_part(a, 1, dz)
    g_tx[...] = grad.astype(BF16)

    def g_moves(act):
        to_heads(lambda hx: g_tx.at[:, lanes(hx, HD)], g.at[unit, c], g_send, g_recv, 0, act)

    g_moves("start")
    owed["g"] = lambda: wait_for(g, g_recv)
    pending.append(lambda: g_moves("wait"))

    row_half = pl.ds(pl.multiple_of(80 * (z % 2), 16), 80)
    chip_slot = y * 4 + home * 2 + unit

    def tw_send_all(act):
        for d in (8, 9, 7, 6, 10, 4, 12, 5, 11, 3, 13, 2, 14, 1, 15, 0):
            dest = lax.rem(s + d, 16)
            tt = dest // 2
            dyh = lax.rem(yh + tt // 4, 2)
            dz = lax.rem(z + 4 - tt % 4, 4)
            src = cot.at[dest % 2, dyh, dz, row_half, lanes(yh, HD)]
            dst = tw_part.at[chip_slot]
            if d:
                copy = remote(src, dst, tw_send.at[d], tw_recv, (dest, t))
                copy.start() if act == "start" else copy.wait_send()
            elif act == "start":
                pltpu.make_async_copy(src, dst, tw_recv).start()

    def tw_turn(act):
        @pl.when(c == z // 2)
        def _():
            tw_send_all(act)

    tw_turn("start")
    owed["tw"] = lambda: wait_for(tw_part, tw_recv)
    pending.append(lambda: tw_turn("wait"))

    sqv = sq_tp[0]
    for d in range(1, 8):
        due(("sqt", d))
        sqv = sqv + sq_tp[d]
    sq_seq[0] = sqv
    for d in range(1, 16):
        sq_copy(sq_seq, d, sqs_send, sqs_recv, (lax.rem(s + d, 16), t), "sqs")

    due("tw")
    tw_view = tw.at[:, z // 2, row_half, lanes(yh, HD)]
    pltpu.make_async_copy(tw_part, tw_view, twg_recv).start()
    for d in range(1, 8):
        launch(remote(tw_part, tw_view, twg_send.at[d], twg_recv, (s, lax.rem(t + d, 8))))
    owed["twg"] = lambda: wait_for(tw, twg_recv)

    due("g")
    gt = g[...].reshape(NQ, HD).astype(F32).T
    dterm = jnp.sum(gt * at_own[...].astype(F32), axis=0, keepdims=True)
    dqt[...] = jnp.zeros_like(dqt)

    def zero(i, state):
        dkv[:, i] = jnp.zeros((2, 2, ROWS, HD), BF16)
        return state

    lax.fori_loop(n1, 8, zero, 0)

    def back(i, state, lo):
        gq = g[...].reshape(NQ, HD)[lo:]
        queries = qq[...].reshape(NQ, 2 * HD)[lo:, HD:]
        keys = chunk(kk, i)[:, :HD]
        vals = chunk(vv, i)[:, :HD]
        ph = p16[i, :, lo:]
        dp = dot_nt(vals, gq)
        ds = (ph.astype(F32) * (dp - dterm[:, lo:])).astype(BF16)
        dkv[1, i] = dot_nn(ph, gq).astype(BF16).reshape(2, ROWS, HD)
        dkv[0, i] = (dot_nn(ds, queries) * SCALE).astype(BF16).reshape(2, ROWS, HD)
        dqt[:, lo:] += dot_tn(keys, ds)
        return state

    over_keys(back, 0)

    sib = remote(dkv.at[:, :, 1 - c], sib_rx, sib_send, sib_recv, (sibling, t))
    launch(sib)
    owed["sib"] = sib.wait_recv
    dq_tx[...] = (dqt[...] * SCALE).T.astype(BF16).reshape(2, 2, ROWS, HD)
    to_owners(dq_tx, dq_rx.at[:, lanes(head, HD)], dq_send, dq_recv, "start")
    owed["dq"] = lambda: wait_for(dq_rx, dq_recv)
    pending.append(lambda: to_owners(dq_tx, dq_rx.at[:, lanes(head, HD)], dq_send, dq_recv, "wait"))
    due("sib")
    dkv_tx[...] = (dkv[:, :, c].astype(F32) + sib_rx[...].astype(F32)).astype(BF16)

    def dkv_copy(dx, dy):
        cx = ring(x, dx)
        cy = lax.rem(y + dy, 2)
        slot = dx * 2 + dy
        return remote(
            dkv_tx.at[:, cx * 2 + cy],
            dkv_rx.at[slot],
            dkv_send.at[slot],
            dkv_recv.at[slot],
            seq_dev(cx, cy, c),
        )

    far_chips = [(dx, dy) for dx in (2, 1, 3, 0) for dy in (1, 0) if dx or dy]
    for dx, dy in far_chips:
        launch(dkv_copy(dx, dy))
        owed["dkv", dx, dy] = dkv_copy(dx, dy).wait_recv

    due("atx")
    due("at2")
    atf = remote(at.at[:, c], at.at[:, c], atf_send, atf_recv, (sibling, t))
    launch(atf)
    owed["atf"] = atf.wait_recv
    due("twg")
    due("atf")

    gw = jnp.zeros((512, 256), F32)
    for a in range(4):
        rows = tw[2 * a : 2 * a + 2].reshape(NQ, 256)
        gw = gw + dot_nn(at[a // 2, a % 2], rows)
    gw_out[...] = gw

    sqv = sq_seq[0]
    for d in range(1, 16):
        due(("sqs", d))
        sqv = sqv + sq_seq[d]
    ms_out[...] = sqv

    due("dq")
    dq_out[...] = dq_rx[...]

    for dx in range(4):
        hx = lax.rem(x + 4 - dx, 4)
        tot = [None, None]
        for dy in (0, 1):
            if dx or dy:
                due(("dkv", dx, dy))
            for a in range(2):
                piece = dkv_rx[dx * 2 + dy, a] if dx or dy else dkv_tx[a, m]
                piece = piece.astype(F32)
                tot[a] = piece if tot[a] is None else tot[a] + piece
        dk_out[:, lanes(hx, HD)] = tot[0]
        dv_out[:, lanes(hx, HD)] = tot[1]

    finish()


def scaled(ms_ref, *refs):
    scale = lax.rsqrt(ms_ref[0:1, 0:1] / (2560 * 4096) + 1e-05)
    for src, dst in zip(refs[:4], refs[4:]):
        dst[...] = (src[...].astype(F32) * scale).astype(BF16)


def on_device(q, k, v, qd, kd, vd, w, noisy, vel, time_index, frame_lengths):
    smem = pl.BlockSpec(memory_space=pltpu.SMEM)
    vmem = pl.BlockSpec(memory_space=pltpu.VMEM)
    hbm = pl.BlockSpec(memory_space=pl.ANY)
    dma = pltpu.SemaphoreType.DMA
    scratch = [
        pltpu.VMEM((512, 4096), BF16),
        pltpu.VMEM((4, 2, 2, ROWS, 256), BF16),
        pltpu.VMEM((4, 2, 2, ROWS, 256), BF16),
        pltpu.VMEM((2, 2, ROWS, 256), BF16),
        pltpu.VMEM((8, UNIT, NQ), F32),
        pltpu.VMEM((8, UNIT, NQ), F32),
        pltpu.VMEM((8, UNIT, NQ), BF16),
        pltpu.VMEM((256, NQ), F32),
        pltpu.VMEM((HD, NQ), F32),
        pltpu.VMEM((2, 2, ROWS, HD), BF16),
        pltpu.VMEM((ROWS, 512), BF16),
        pltpu.VMEM((HD, NQ), BF16),
        pltpu.VMEM((2, 2, 512, NQ), BF16),
        pltpu.VMEM((32, 4096), F32),
        pltpu.VMEM((4, 2, ROWS, 256), BF16),
        pltpu.VMEM((4, ROWS, 256), BF16),
        pltpu.VMEM((4, 2, ROWS, 256), BF16),
        pltpu.VMEM((4, ROWS, 256), BF16),
        pltpu.VMEM((2, ROWS, 256), F32),
        pltpu.VMEM((4, ROWS, 256), F32),
        pltpu.VMEM((ROWS, 256), BF16),
        pltpu.VMEM((4, ROWS, 256), BF16),
        pltpu.VMEM((ROWS, 256), BF16),
        pltpu.VMEM((4, ROWS, 256), BF16),
        pltpu.VMEM((2, 2, 4, ROWS, 256), BF16),
        pltpu.VMEM((ROWS, 512), BF16),
        pltpu.VMEM((2, 2, ROWS, HD), BF16),
        pltpu.VMEM((HD, NQ), F32),
        pltpu.VMEM((2, 2, ROWS, HD), BF16),
        pltpu.VMEM((ROWS, 512), BF16),
        pltpu.VMEM((2, 8, 2, ROWS, HD), BF16),
        pltpu.VMEM((2, 8, ROWS, HD), BF16),
        pltpu.VMEM((2, 8, ROWS, HD), BF16),
        pltpu.VMEM((8, 2, ROWS, HD), BF16),
        pltpu.VMEM((8, 80, HD), BF16),
        pltpu.VMEM((8, 2, ROWS, 256), BF16),
        pltpu.VMEM((8, 8, 128), F32),
        pltpu.VMEM((16, 8, 128), F32),
        dma,
        dma((4, 4)),
        dma((4,)),
        dma((4, 4)),
        dma((4,)),
        dma((4,)),
        dma((4,)),
        dma((4,)),
        dma((4,)),
        dma((2, 4)),
        dma,
        dma((2, 2)),
        dma,
        dma((2, 4)),
        dma,
        dma,
        dma,
        dma,
        dma,
        dma,
        dma((4,)),
        dma((4,)),
        dma,
        dma,
        dma,
        dma,
        dma((4,)),
        dma((4,)),
        dma((2, 2, 4)),
        dma((2, 2, 4)),
        dma((1, 4)),
        dma,
        dma((16,)),
        dma,
        dma((8,)),
        dma,
        dma((2, 2)),
        dma,
        dma,
        dma,
        dma((8,)),
        dma((8,)),
        dma((8,)),
        dma((8,)),
        dma((16,)),
        dma((16,)),
    ]
    dq, dk, dv, gw, ms = pl.pallas_call(
        kernel,
        out_shape=(
            jax.ShapeDtypeStruct((ROWS, 512), BF16),
            jax.ShapeDtypeStruct((ROWS, 512), F32),
            jax.ShapeDtypeStruct((ROWS, 512), F32),
            jax.ShapeDtypeStruct((512, 256), F32),
            jax.ShapeDtypeStruct((8, 128), F32),
        ),
        in_specs=[smem, smem] + [hbm] * 7 + [vmem] * 2,
        out_specs=(vmem,) * 5,
        scratch_shapes=scratch,
        compiler_params=pltpu.CompilerParams(
            collective_id=0, has_side_effects=True, vmem_limit_bytes=56 * 1024 * 1024
        ),
        cost_estimate=pl.CostEstimate(flops=7 * 10**9, bytes_accessed=8 * 10**6, transcendentals=1638400),
    )(frame_lengths, time_index, q, k, v, qd, kd, vd, w, noisy, vel)
    return pl.pallas_call(
        scaled,
        out_shape=tuple(jax.ShapeDtypeStruct(part.shape, BF16) for part in (dq, dk, dv, gw)),
        in_specs=[vmem] * 5,
        out_specs=(vmem,) * 4,
    )(ms, dq, dk, dv, gw)


def solution(mesh):
    in_specs = (P("seq", "tp"),) * 6 + (P("tp", None), P(("seq", "tp"), None), P(("seq", "tp"), None), P(), P())
    out_specs = (P("seq", "tp"), P("seq", "tp"), P("seq", "tp"), P("tp", "seq"))
    return jax.shard_map(
        on_device, mesh=mesh, in_specs=in_specs, out_specs=out_specs, check_vma=False
    )
```

```python
import math

import jax
import jax.numpy as jnp
from jax import lax
from jax.experimental import pallas as pl
from jax.experimental.pallas import tpu as pltpu
from jax.sharding import PartitionSpec as P

HD = 128
TSTEPS = 64
FRAMES = 16
ROWS = 160
UNIT = 320
NCHIP = 8
NQ = 640
SCALE = 1.0 / math.sqrt(HD)
MESH = pl.DeviceIdType.MESH
F32 = jnp.float32
BF16 = jnp.bfloat16


def dot_nt(a, b):
    return lax.dot_general(a, b, (((1,), (1,)), ((), ())), preferred_element_type=F32)


def dot_nn(a, b):
    return lax.dot_general(a, b, (((1,), (0,)), ((), ())), preferred_element_type=F32)


def dot_tn(a, b):
    return lax.dot_general(a, b, (((0,), (0,)), ((), ())), preferred_element_type=F32)


def kernel(
    frame_ref,
    time_ref,
    q_ref,
    k_ref,
    v_ref,
    qd_ref,
    kd_ref,
    vd_ref,
    w_hbm,
    noisy_ref,
    vel_ref,
    dq_out,
    dk_out,
    dv_out,
    gw_out,
    ms_out,
    w,
    kk,
    vv,
    qq,
    sbuf,
    stbuf,
    p16,
    acc1,
    acc2,
    ublk,
    uown,
    at_own,
    at,
    negb,
    part_a,
    part_b,
    rx_a,
    rx_b,
    sum_a,
    sum_b,
    part_a2,
    part_b2,
    rx_a2,
    rx_b2,
    cot,
    g_tx,
    g,
    dqt,
    dq_tx,
    dq_rx,
    dkv,
    sib_rx,
    dkv_tx,
    dkv_rx,
    tw_part,
    tw,
    sq_tp,
    sq_seq,
    wsem,
    kvx_send,
    kvx_recv,
    kvy_send,
    kvy_recv,
    fwx_send,
    fwx_recv,
    fwy_send,
    fwy_recv,
    q_send,
    q_recv,
    u_send,
    u_recv,
    atx_send,
    atx_recv,
    aty_send,
    aty_recv,
    at2_recv,
    atf_send,
    atf_recv,
    rsa_send,
    rsa_recv,
    rsb_send,
    rsb_recv,
    rsa2_send,
    rsa2_recv,
    rsb2_send,
    rsb2_recv,
    t_send,
    t_recv,
    g_send,
    g_recv,
    tw_send,
    tw_recv,
    twg_send,
    twg_recv,
    dq_send,
    dq_recv,
    sib_send,
    sib_recv,
    dkv_send,
    dkv_recv,
    sqt_send,
    sqt_recv,
    sqs_send,
    sqs_recv,
):
    s = lax.axis_index("seq")
    t = lax.axis_index("tp")
    x = s // 4
    y = (s // 2) % 2
    c = s % 2
    m = s // 2
    yh = t // 4
    z = t % 4
    head = x
    far = (2, 1, 3)

    def ring(pos, step):
        return lax.rem(pos + step, 4)

    def seq_dev(px, py, pc):
        return (px * 4 + py * 2 + pc, t)

    def tp_dev(pyh, pz):
        return (s, pyh * 4 + pz)

    def local_copy(src, dst, sem):
        return pltpu.make_async_copy(src, dst, sem)

    def remote(src, dst, ssem, rsem, dev):
        return pltpu.make_async_remote_copy(
            src_ref=src, dst_ref=dst, send_sem=ssem, recv_sem=rsem, device_id=dev, device_id_type=MESH
        )

    def lanes(index, width):
        return pl.ds(pl.multiple_of(index * width, width), width)

    def wait_for(ref, sem):
        pltpu.make_async_copy(ref, ref, sem).wait()

    pending = []

    def launch(copy):
        copy.start()
        pending.append(copy.wait_send)

    owed = {}

    def due(name):
        owed.pop(name)()

    def finish():
        for name in list(owed):
            due(name)
        for wait in pending:
            wait()

    wload = pltpu.make_async_copy(w_hbm, w, wsem)
    wload.start()
    owed["w"] = wload.wait

    barrier = pltpu.get_barrier_semaphore()
    sibling = s + 1 - 2 * c
    partners = [seq_dev(x, 1 - y, c), (sibling, t), tp_dev(1 - yh, z)]
    for dx in far:
        partners += [seq_dev(ring(x, dx), y, c), seq_dev(ring(x, dx), y, 1 - c), tp_dev(yh, ring(z, dx))]
    for dev in partners:
        pl.semaphore_signal(barrier, inc=1, device_id=dev, device_id_type=MESH)
    pl.semaphore_wait(barrier, len(partners))

    kv_src = (k_ref, kd_ref, v_ref, vd_ref)
    kv_dst = ((kk, 0), (kk, 1), (vv, 0), (vv, 1))

    def kv_view(a, px, py, pc):
        buf, half = kv_dst[a]
        return buf.at[px, py, pc, :, half * HD : (half + 1) * HD]

    def kv_piece(a, px):
        return kv_src[a].at[:, lanes(px, HD)]

    def kv_all(a, py, pc):
        return kv_view(a, slice(None), py, pc)

    def kv_own(a):
        local_copy(kv_piece(a, x), kv_view(a, x, y, c), kvx_recv.at[a]).start()
        launch(
            remote(
                kv_piece(a, x), kv_view(a, x, y, c), kvy_send.at[a, 0], kvy_recv.at[a], seq_dev(x, 1 - y, c)
            )
        )

    def kv_along_x(a):
        for dx in far:
            hx = ring(x, dx)
            launch(
                remote(
                    kv_piece(a, hx), kv_view(a, x, y, c), kvx_send.at[a, dx], kvx_recv.at[a], seq_dev(hx, y, c)
                )
            )
        owed["kvx", a] = lambda: wait_for(kv_all(a, y, c), kvx_recv.at[a])
        owed["kvy", a] = lambda: wait_for(kv_all(a, 1 - y, c), kvy_recv.at[a])

    def kv_across(a):
        due(("kvx", a))
        for dx in far:
            view = kv_view(a, ring(x, dx), y, c)
            launch(remote(view, view, kvy_send.at[a, dx], kvy_recv.at[a], seq_dev(x, 1 - y, c)))
        to_sibling(a, y, fwx_send, fwx_recv, "fwx")

    def to_sibling(a, py, send, recv, name):
        view = kv_all(a, py, c)
        launch(remote(view, view, send.at[a], recv.at[a], (sibling, t)))
        owed[name, a] = lambda: wait_for(kv_all(a, py, 1 - c), recv.at[a])

    def kv_received(a):
        due(("kvy", a))
        to_sibling(a, 1 - y, fwy_send, fwy_recv, "fwy")

    def kv_complete(a):
        due(("fwx", a))
        due(("fwy", a))

    home = jnp.where((x == 1) | (x == 2), 1, 0)
    unit = x // 2

    def to_heads(src_of, dst, send, recv, slot, act):
        for dx in (2, 1, 3, 0):
            hx = ring(x, dx)
            if dx:
                copy = remote(src_of(hx), dst, send.at[slot, dx], recv, seq_dev(hx, y, home))
                copy.start() if act == "start" else copy.wait_send()
            else:

                @pl.when(home != c)
                def _():
                    copy = remote(src_of(hx), dst, send.at[slot, dx], recv, seq_dev(hx, y, home))
                    copy.start() if act == "start" else copy.wait_send()

                if act == "start":

                    @pl.when(home == c)
                    def _():
                        local_copy(src_of(hx), dst, recv).start()

    def to_owners(src, dst, send, recv, act):
        for u in range(2):
            ux = c if u == 0 else 3 - c
            for core in range(2):
                dev = ux * 4 + y * 2 + core

                @pl.when(dev != s)
                def _():
                    copy = remote(src.at[u, core], dst, send.at[u, core], recv, (dev, t))
                    copy.start() if act == "start" else copy.wait_send()

                if act == "start":

                    @pl.when(dev == s)
                    def _():
                        local_copy(src.at[u, core], dst, recv).start()

    def q_moves(act):
        for a, ref in ((1, q_ref), (0, qd_ref)):
            to_heads(
                lambda hx, ref=ref: ref.at[:, lanes(hx, HD)],
                qq.at[unit, c, :, a * HD : (a + 1) * HD],
                q_send,
                q_recv,
                a,
                act,
            )

    kv_along_x(0)
    for a in range(4):
        kv_own(a)
    q_moves("start")
    pending.append(lambda: q_moves("wait"))
    owed["q"] = lambda: wait_for(qq, q_recv)
    for a in (1, 2, 3):
        kv_along_x(a)

    ends = []
    total = 0
    for f in range(FRAMES):
        total = total + frame_ref[f]
        ends.append(total)
    times = [time_ref[f] for f in range(FRAMES)]

    def frame_facts(pos):
        kend = jnp.zeros(pos.shape, jnp.int32) + ends[FRAMES - 1]
        level = jnp.zeros(pos.shape, jnp.int32) + times[FRAMES - 1]
        for f in range(FRAMES - 2, -1, -1):
            inside = pos < ends[f]
            kend = jnp.where(inside, ends[f], kend)
            level = jnp.where(inside, times[f], level)
        angle = (level.astype(F32) + 0.5) * (math.pi / (2 * TSTEPS))
        return kend, jnp.cos(angle), jnp.sin(angle)

    lane = lax.broadcasted_iota(jnp.int32, (1, NQ), 1)
    chip0 = 2 * c + y
    chip1 = 2 * (3 - c) + y
    qpos = jnp.where(lane < UNIT, UNIT * chip0 + lane, UNIT * chip1 + lane - UNIT)
    kend, cosq, sinq = frame_facts(qpos)

    rpos = s * ROWS + t * 20 + lax.broadcasted_iota(jnp.int32, (20, 1), 0)
    _, cosr, sinr = frame_facts(rpos)
    negb[...] = jnp.zeros_like(negb)
    negb[0:20, :] = sinr * cosr * noisy_ref[...].astype(F32) - cosr * cosr * vel_ref[...].astype(F32)

    n0 = chip0 + 2
    n1 = jnp.minimum(chip1 + 2, 8)

    def over_keys(body, carry):
        carry = lax.fori_loop(0, n0, lambda i, st: body(i, st, 0), carry)
        return lax.fori_loop(n0, n1, lambda i, st: body(i, st, 256), carry)

    def put(row, lo, part_row):
        if lo == 0:
            return part_row
        return jnp.concatenate([row[:, :lo], part_row], axis=1)

    kv_across(0)
    kv_across(1)
    kv_received(0)
    kv_across(2)
    due("q")
    kv_complete(0)

    def chunk(buf, i):
        return buf[i // 2, i % 2].reshape(UNIT, buf.shape[-1])

    def pass1(i, top, lo):
        keys = kk[i // 2, i % 2, :, :, :HD].reshape(UNIT, HD)
        queries = qq[...].reshape(NQ, 2 * HD)[lo:, HD:]
        sc = dot_nt(keys, queries) * SCALE
        kpos = i * UNIT + lax.broadcasted_iota(jnp.int32, (UNIT, 1), 0)
        sc = jnp.where(kpos < kend[:, lo:], sc, -1e30)
        sbuf[i, :, lo:] = sc
        return put(top, lo, jnp.maximum(top[:, lo:], jnp.max(sc, axis=0, keepdims=True)))

    top = over_keys(pass1, jnp.full((1, NQ), -1e30, F32))

    kv_across(3)
    kv_received(1)
    kv_complete(1)

    def pass2(i, state, lo):
        den, tan = state
        st = dot_nt(chunk(kk, i), qq[...].reshape(NQ, 2 * HD)[lo:]) * SCALE
        p = jnp.exp(sbuf[i, :, lo:] - top[:, lo:])
        sbuf[i, :, lo:] = p
        stbuf[i, :, lo:] = st
        den = put(den, lo, den[:, lo:] + jnp.sum(p, axis=0, keepdims=True))
        tan = put(tan, lo, tan[:, lo:] + jnp.sum(p * st, axis=0, keepdims=True))
        return den, tan

    row0 = jnp.zeros((1, NQ), F32)
    den, tan = over_keys(pass2, (row0, row0))
    inv = 1.0 / den
    mean = tan * inv
    kv_received(2)
    kv_received(3)
    kv_complete(2)

    acc1[...] = jnp.zeros_like(acc1)
    acc2[...] = jnp.zeros_like(acc2)

    def pass3(i, state, lo):
        p = sbuf[i, :, lo:] * inv[:, lo:]
        ph = p.astype(BF16)
        p16[i, :, lo:] = ph
        ds = (p * (stbuf[i, :, lo:] - mean[:, lo:])).astype(BF16)
        vals = vv[i // 2, i % 2, :, :, :HD].reshape(UNIT, HD)
        acc1[:, lo:] += dot_tn(vals, ph)
        acc2[:, lo:] += dot_tn(vals, ds)
        return state

    over_keys(pass3, 0)
    kv_complete(3)

    def pass4(i, state, lo):
        vals_dot = vv[i // 2, i % 2, :, :, HD:].reshape(UNIT, HD)
        acc2[:, lo:] += dot_tn(vals_dot, p16[i, :, lo:])
        return state

    over_keys(pass4, 0)
    attn_t = acc1[...].astype(BF16)
    tan_t = acc2[...].astype(BF16)
    at_own[...] = attn_t
    u_t = (0.5 * cosq) * (cosq * attn_t.astype(F32) + sinq * tan_t.astype(F32))
    ublk[...] = u_t.T.astype(BF16).reshape(2, 2, ROWS, HD)
    to_owners(ublk, uown.at[:, lanes(head, HD)], u_send, u_recv, "start")
    owed["u"] = lambda: wait_for(uown, u_recv)
    pending.append(lambda: to_owners(ublk, uown.at[:, lanes(head, HD)], u_send, u_recv, "wait"))

    def at_view(py, hx):
        return at.at[py, c, lanes(hx, HD), :]

    local_copy(at_own, at_view(y, x), atx_recv).start()
    launch(remote(at_own, at_view(y, x), aty_send, aty_recv, seq_dev(x, 1 - y, c)))
    owed["aty"] = lambda: wait_for(at_view(1 - y, x), aty_recv)
    for dx in far:
        launch(remote(at_own, at_view(y, x), atx_send.at[0, dx], atx_recv, seq_dev(ring(x, dx), y, c)))
    owed["atx"] = lambda: wait_for(at.at[y, c], atx_recv)

    def at_pass_on():
        due("aty")
        for dx in far:
            view = at_view(1 - y, x)
            launch(remote(view, view, atx_send.at[1, dx], at2_recv, seq_dev(ring(x, dx), y, c)))
        owed["at2"] = lambda: wait_for(at.at[1 - y, c, 0 : 3 * HD], at2_recv)

    due("w")
    due("u")
    u = uown[...]
    pick = (
        lax.broadcasted_iota(jnp.int32, (ROWS, 32), 0)
        == t * 20 + lax.broadcasted_iota(jnp.int32, (ROWS, 32), 1)
    ) & (lax.broadcasted_iota(jnp.int32, (ROWS, 32), 1) < 20)
    pick = pick.astype(F32).astype(BF16)

    def partial(pyh, pz, half):
        cols = pl.ds(pl.multiple_of((pyh * 4 + pz) * 512 + half * 256, 256), 256)
        return dot_nn(u, w[:, cols]) + dot_nn(pick, negb[:, cols].astype(BF16))

    for dz in range(4):
        part_b[dz] = partial(1 - yh, ring(z, dz), 1).astype(BF16)
    launch(remote(part_b, rx_b, rsb_send, rsb_recv, tp_dev(1 - yh, z)))
    owed["rsb"] = lambda: wait_for(rx_b, rsb_recv)

    for dz in far:
        for e in range(2):
            part_a[dz, e] = partial(yh if e == 0 else 1 - yh, ring(z, dz), 0).astype(BF16)
        copy = remote(part_a.at[dz], rx_a.at[dz], rsa_send.at[dz], rsa_recv.at[dz], tp_dev(yh, ring(z, dz)))
        launch(copy)
        owed["rsa", dz] = copy.wait_recv

    for dz in range(4):
        sum_b[dz] = partial(yh, ring(z, dz), 1)
    for e in range(2):
        sum_a[e] = partial(yh if e == 0 else 1 - yh, z, 0)

    at_pass_on()

    due("rsb")
    for dz in far:
        part_b2[dz] = (sum_b[dz] + rx_b[dz].astype(F32)).astype(BF16)
        copy = remote(part_b2.at[dz], rx_b2.at[dz], rsb2_send.at[dz], rsb2_recv.at[dz], tp_dev(yh, ring(z, dz)))
        launch(copy)
        owed["rsb2", dz] = copy.wait_recv
    for dz in far:
        due(("rsa", dz))
    other = sum_a[1]
    for dz in far:
        other = other + rx_a[dz, 1].astype(F32)
    part_a2[...] = other.astype(BF16)
    copy = remote(part_a2, rx_a2, rsa2_send, rsa2_recv, tp_dev(1 - yh, z))
    launch(copy)
    owed["rsa2"] = copy.wait_recv

    def cot_copy(a, src, dst, dev):
        sem = (a,) + dst
        copy = remote(cot.at[(a,) + src], cot.at[(a,) + dst], t_send.at[sem], t_recv.at[sem], dev)
        launch(copy)
        owed[("t",) + sem] = copy.wait_recv

    cot_b = sum_b[0] + rx_b[0].astype(F32)
    for dz in far:
        due(("rsb2", dz))
        cot_b = cot_b + rx_b2[dz].astype(F32)
    cot[1, 0, 0] = cot_b.astype(BF16)
    cot_copy(1, (0, 0), (1, 0), tp_dev(1 - yh, z))
    for dz in far:
        cot_copy(1, (0, 0), (0, dz), tp_dev(yh, ring(z, dz)))

    cot_a = sum_a[0]
    for dz in far:
        cot_a = cot_a + rx_a[dz, 0].astype(F32)
    due("rsa2")
    cot_a = cot_a + rx_a2[...].astype(F32)
    cot[0, 0, 0] = cot_a.astype(BF16)
    cot_copy(0, (0, 0), (1, 0), tp_dev(1 - yh, z))
    for dz in far:
        cot_copy(0, (0, 0), (0, dz), tp_dev(yh, ring(z, dz)))

    def sq_copy(buf, d, send, recv, dev, name):
        copy = remote(buf.at[0], buf.at[d], send.at[d], recv.at[d], dev)
        launch(copy)
        owed[name, d] = copy.wait_recv

    sq = jnp.sum(cot_a * cot_a + cot_b * cot_b, axis=0, keepdims=True)
    sq_tp[0] = jnp.zeros((8, 128), F32) + jnp.sum(sq, axis=1, keepdims=True)
    for d in range(1, 8):
        sq_copy(sq_tp, d, sqt_send, sqt_recv, (s, lax.rem(t + d, 8)), "sqt")

    def grad_part(a, dyh, dz):
        pyh = lax.rem(yh + dyh, 2)
        pz = lax.rem(z + 4 - dz, 4)
        cols = pl.ds(pl.multiple_of((pyh * 4 + pz) * 512 + a * 256, 256), 256)
        return dot_nt(cot[a, dyh, dz], w[:, cols])

    grad = grad_part(0, 0, 0) + grad_part(1, 0, 0)
    due(("t", 1, 1, 0))
    for dz in far:
        cot_copy(1, (1, 0), (1, dz), tp_dev(yh, ring(z, dz)))
    grad = grad + grad_part(1, 1, 0)
    for dz in (1, 3, 2):
        due(("t", 0, 0, dz))
        cot_copy(0, (0, dz), (1, dz), tp_dev(1 - yh, z))
    for dz in (1, 3, 2):
        grad = grad + grad_part(0, 0, dz)
        due(("t", 1, 0, dz))
        grad = grad + grad_part(1, 0, dz)
    for a, dz in ((0, 0), (0, 1), (0, 3), (0, 2), (1, 1), (1, 3), (1, 2)):
        due(("t", a, 1, dz))
        grad = grad + grad_part(a, 1, dz)
    g_tx[...] = grad.astype(BF16)

    def g_moves(act):
        to_heads(lambda hx: g_tx.at[:, lanes(hx, HD)], g.at[unit, c], g_send, g_recv, 0, act)

    g_moves("start")
    owed["g"] = lambda: wait_for(g, g_recv)
    pending.append(lambda: g_moves("wait"))

    row_half = pl.ds(pl.multiple_of(80 * (z % 2), 16), 80)
    chip_slot = y * 4 + home * 2 + unit

    def tw_send_all(act):
        for d in (8, 9, 7, 6, 10, 4, 12, 5, 11, 3, 13, 2, 14, 1, 15, 0):
            dest = lax.rem(s + d, 16)
            tt = dest // 2
            dyh = lax.rem(yh + tt // 4, 2)
            dz = lax.rem(z + 4 - tt % 4, 4)
            src = cot.at[dest % 2, dyh, dz, row_half, lanes(yh, HD)]
            dst = tw_part.at[chip_slot]
            if d:
                copy = remote(src, dst, tw_send.at[d], tw_recv, (dest, t))
                copy.start() if act == "start" else copy.wait_send()
            elif act == "start":
                local_copy(src, dst, tw_recv).start()

    def tw_turn(act):
        @pl.when(c == z // 2)
        def _():
            tw_send_all(act)

    tw_turn("start")
    owed["tw"] = lambda: wait_for(tw_part, tw_recv)
    pending.append(lambda: tw_turn("wait"))

    sqv = sq_tp[0]
    for d in range(1, 8):
        due(("sqt", d))
        sqv = sqv + sq_tp[d]
    sq_seq[0] = sqv
    for d in range(1, 16):
        sq_copy(sq_seq, d, sqs_send, sqs_recv, (lax.rem(s + d, 16), t), "sqs")

    due("tw")

    def tw_view(a, dyh, dz):
        pyh = lax.rem(yh + dyh, 2)
        pz = lax.rem(z + 4 - dz, 4)
        rows = pl.ds(pl.multiple_of(80 * (pz % 2), 16), 80)
        return tw.at[4 * a : 4 * a + 4, pz // 2, rows, lanes(pyh, HD)]

    def twg_copy(a, origin, slot, dev):
        view = tw_view(a, *origin)
        src = tw_part.at[4 * a : 4 * a + 4] if origin == (0, 0) else view
        sem = (a,) + slot
        copy = remote(src, view, twg_send.at[sem], twg_recv.at[sem], dev)
        launch(copy)
        owed[("twg",) + sem] = copy.wait_recv

    for a in range(2):
        local_copy(tw_part.at[4 * a : 4 * a + 4], tw_view(a, 0, 0), twg_recv.at[a, 0, 0]).start()
        owed["twg", a, 0, 0] = lambda a=a: wait_for(tw_view(a, 0, 0), twg_recv.at[a, 0, 0])
        for dz in far:
            twg_copy(a, (0, 0), (0, dz), tp_dev(yh, ring(z, dz)))
    for a in (1, 0):
        twg_copy(a, (0, 0), (1, 0), tp_dev(1 - yh, z))

    def tw_pass_on():
        due(("twg", 1, 1, 0))
        for dz in far:
            twg_copy(1, (1, 0), (1, dz), tp_dev(yh, ring(z, dz)))
        for dz in (1, 3, 2):
            due(("twg", 0, 0, dz))
            twg_copy(0, (0, dz), (1, dz), tp_dev(1 - yh, z))

    due("g")
    gt = g[...].reshape(NQ, HD).astype(F32).T
    dterm = jnp.sum(gt * at_own[...].astype(F32), axis=0, keepdims=True)
    dqt[...] = jnp.zeros_like(dqt)

    def back(i, lo):
        gq = g[...].reshape(NQ, HD)[lo:]
        queries = qq[...].reshape(NQ, 2 * HD)[lo:, HD:]
        keys = chunk(kk, i)[:, :HD]
        vals = chunk(vv, i)[:, :HD]
        ph = p16[i, :, lo:]
        dp = dot_nt(vals, gq)
        ds = (ph.astype(F32) * (dp - dterm[:, lo:])).astype(BF16)
        dkv[1, i] = dot_nn(ph, gq).astype(BF16).reshape(2, ROWS, HD)
        dkv[0, i] = (dot_nn(ds, queries) * SCALE).astype(BF16).reshape(2, ROWS, HD)
        dqt[:, lo:] += dot_tn(keys, ds)

    def sib_copy(i):
        return remote(
            dkv.at[:, i, 1 - c], sib_rx.at[:, i], sib_send.at[i], sib_recv.at[i], (sibling, t)
        )

    def dkv_copy(i):
        return remote(
            dkv_tx.at[:, i], dkv_rx.at[m], dkv_send.at[i], dkv_recv.at[m], seq_dev(i // 2, i % 2, c)
        )

    def both_cores(i):
        sib_copy(i).wait_recv()
        return dkv[:, i, c].astype(F32) + sib_rx[:, i].astype(F32)

    def back_step(k, state):
        i = lax.rem(m + 1 + k, 8)

        @pl.when(i < n0)
        def _():
            back(i, 0)

        @pl.when((i >= n0) & (i < n1))
        def _():
            back(i, 256)

        @pl.when(i >= n1)
        def _():
            dkv[:, i] = jnp.zeros((2, 2, ROWS, HD), BF16)

        sib_copy(i).start()

        @pl.when(k > 0)
        def _():
            done = lax.rem(m + k, 8)
            dkv_tx[:, done] = both_cores(done).astype(BF16)
            dkv_copy(done).start()

        return state

    lax.fori_loop(0, 8, back_step, 0)
    dq_tx[...] = (dqt[...] * SCALE).T.astype(BF16).reshape(2, 2, ROWS, HD)
    to_owners(dq_tx, dq_rx.at[:, lanes(head, HD)], dq_send, dq_recv, "start")
    owed["dq"] = lambda: wait_for(dq_rx, dq_recv)
    pending.append(lambda: to_owners(dq_tx, dq_rx.at[:, lanes(head, HD)], dq_send, dq_recv, "wait"))
    tw_pass_on()
    dkv_rx[m] = both_cores(m).astype(BF16)

    due("atx")
    due("at2")
    atf = remote(at.at[:, c], at.at[:, c], atf_send, atf_recv, (sibling, t))
    launch(atf)
    owed["atf"] = atf.wait_recv
    for a in range(2):
        for dyh in range(2):
            for dz in range(4):
                if ("twg", a, dyh, dz) in owed:
                    due(("twg", a, dyh, dz))
    due("atf")

    gw = jnp.zeros((512, 256), F32)
    for a in range(4):
        rows = tw[2 * a : 2 * a + 2].reshape(NQ, 256)
        gw = gw + dot_nn(at[a // 2, a % 2], rows)
    gw_out[...] = gw

    sqv = sq_seq[0]
    for d in range(1, 16):
        due(("sqs", d))
        sqv = sqv + sq_seq[d]
    ms_out[...] = sqv

    due("dq")
    dq_out[...] = dq_rx[...]

    def all_dkv(k, state):
        i = lax.rem(m + 1 + k, 8)
        sib_copy(i).wait_send()

        @pl.when(k < 7)
        def _():
            dkv_copy(i).wait_send()
            remote(dkv_tx.at[:, i], dkv_rx.at[i], dkv_send.at[i], dkv_recv.at[i], (sibling, t)).wait_recv()

        return state

    lax.fori_loop(0, 8, all_dkv, 0)
    for h in range(4):
        for a, out in enumerate((dk_out, dv_out)):
            out[:, h * HD : (h + 1) * HD] = dkv_rx[2 * h, a].astype(F32) + dkv_rx[2 * h + 1, a].astype(F32)
    finish()


def scaled(ms_ref, *refs):
    scale = lax.rsqrt(ms_ref[0:1, 0:1] / (2560 * 4096) + 1e-05)
    for src, dst in zip(refs[:4], refs[4:]):
        dst[...] = (src[...].astype(F32) * scale).astype(BF16)


def on_device(q, k, v, qd, kd, vd, w, noisy, vel, time_index, frame_lengths):
    smem = pl.BlockSpec(memory_space=pltpu.SMEM)
    vmem = pl.BlockSpec(memory_space=pltpu.VMEM)
    hbm = pl.BlockSpec(memory_space=pl.ANY)
    dma = pltpu.SemaphoreType.DMA
    scratch = [
        pltpu.VMEM((512, 4096), BF16),
        pltpu.VMEM((4, 2, 2, ROWS, 256), BF16),
        pltpu.VMEM((4, 2, 2, ROWS, 256), BF16),
        pltpu.VMEM((2, 2, ROWS, 256), BF16),
        pltpu.VMEM((8, UNIT, NQ), F32),
        pltpu.VMEM((8, UNIT, NQ), F32),
        pltpu.VMEM((8, UNIT, NQ), BF16),
        pltpu.VMEM((HD, NQ), F32),
        pltpu.VMEM((HD, NQ), F32),
        pltpu.VMEM((2, 2, ROWS, HD), BF16),
        pltpu.VMEM((ROWS, 512), BF16),
        pltpu.VMEM((HD, NQ), BF16),
        pltpu.VMEM((2, 2, 512, NQ), BF16),
        pltpu.VMEM((32, 4096), F32),
        pltpu.VMEM((4, 2, ROWS, 256), BF16),
        pltpu.VMEM((4, ROWS, 256), BF16),
        pltpu.VMEM((4, 2, ROWS, 256), BF16),
        pltpu.VMEM((4, ROWS, 256), BF16),
        pltpu.VMEM((2, ROWS, 256), F32),
        pltpu.VMEM((4, ROWS, 256), F32),
        pltpu.VMEM((ROWS, 256), BF16),
        pltpu.VMEM((4, ROWS, 256), BF16),
        pltpu.VMEM((ROWS, 256), BF16),
        pltpu.VMEM((4, ROWS, 256), BF16),
        pltpu.VMEM((2, 2, 4, ROWS, 256), BF16),
        pltpu.VMEM((ROWS, 512), BF16),
        pltpu.VMEM((2, 2, ROWS, HD), BF16),
        pltpu.VMEM((HD, NQ), F32),
        pltpu.VMEM((2, 2, ROWS, HD), BF16),
        pltpu.VMEM((ROWS, 512), BF16),
        pltpu.VMEM((2, 8, 2, ROWS, HD), BF16),
        pltpu.VMEM((2, 8, ROWS, HD), BF16),
        pltpu.VMEM((2, 8, ROWS, HD), BF16),
        pltpu.VMEM((8, 2, ROWS, HD), BF16),
        pltpu.VMEM((8, 80, HD), BF16),
        pltpu.VMEM((8, 2, ROWS, 256), BF16),
        pltpu.VMEM((8, 8, 128), F32),
        pltpu.VMEM((16, 8, 128), F32),
        dma,
        dma((4, 4)),
        dma((4,)),
        dma((4, 4)),
        dma((4,)),
        dma((4,)),
        dma((4,)),
        dma((4,)),
        dma((4,)),
        dma((2, 4)),
        dma,
        dma((2, 2)),
        dma,
        dma((2, 4)),
        dma,
        dma,
        dma,
        dma,
        dma,
        dma,
        dma((4,)),
        dma((4,)),
        dma,
        dma,
        dma,
        dma,
        dma((4,)),
        dma((4,)),
        dma((2, 2, 4)),
        dma((2, 2, 4)),
        dma((1, 4)),
        dma,
        dma((16,)),
        dma,
        dma((2, 2, 4)),
        dma((2, 2, 4)),
        dma((2, 2)),
        dma,
        dma((8,)),
        dma((8,)),
        dma((8,)),
        dma((8,)),
        dma((8,)),
        dma((8,)),
        dma((16,)),
        dma((16,)),
    ]
    dq, dk, dv, gw, ms = pl.pallas_call(
        kernel,
        out_shape=(
            jax.ShapeDtypeStruct((ROWS, 512), BF16),
            jax.ShapeDtypeStruct((ROWS, 512), F32),
            jax.ShapeDtypeStruct((ROWS, 512), F32),
            jax.ShapeDtypeStruct((512, 256), F32),
            jax.ShapeDtypeStruct((8, 128), F32),
        ),
        in_specs=[smem, smem] + [hbm] * 7 + [vmem] * 2,
        out_specs=(vmem,) * 5,
        scratch_shapes=scratch,
        compiler_params=pltpu.CompilerParams(
            collective_id=0, has_side_effects=True, vmem_limit_bytes=56 * 1024 * 1024
        ),
        cost_estimate=pl.CostEstimate(flops=7 * 10**9, bytes_accessed=8 * 10**6, transcendentals=1638400),
    )(frame_lengths, time_index, q, k, v, qd, kd, vd, w, noisy, vel)
    return pl.pallas_call(
        scaled,
        out_shape=tuple(jax.ShapeDtypeStruct(part.shape, BF16) for part in (dq, dk, dv, gw)),
        in_specs=[vmem] * 5,
        out_specs=(vmem,) * 4,
    )(ms, dq, dk, dv, gw)


def solution(mesh):
    in_specs = (P("seq", "tp"),) * 6 + (P("tp", None), P(("seq", "tp"), None), P(("seq", "tp"), None), P(), P())
    out_specs = (P("seq", "tp"), P("seq", "tp"), P("seq", "tp"), P("tp", "seq"))
    return jax.shard_map(
        on_device, mesh=mesh, in_specs=in_specs, out_specs=out_specs, check_vma=False
    )
```

```python
import math

import jax
import jax.numpy as jnp
from jax import lax
from jax.experimental import pallas as pl
from jax.experimental.pallas import tpu as pltpu
from jax.sharding import PartitionSpec as P

HD = 128
TSTEPS = 64
FRAMES = 16
ROWS = 160
UNIT = 320
NCHIP = 8
NQ = 640
SCALE = 1.0 / math.sqrt(HD)
MESH = pl.DeviceIdType.MESH
F32 = jnp.float32
BF16 = jnp.bfloat16


def dot_nt(a, b):
    return lax.dot_general(a, b, (((1,), (1,)), ((), ())), preferred_element_type=F32)


def dot_nn(a, b):
    return lax.dot_general(a, b, (((1,), (0,)), ((), ())), preferred_element_type=F32)


def dot_tn(a, b):
    return lax.dot_general(a, b, (((0,), (0,)), ((), ())), preferred_element_type=F32)


def kernel(
    frame_ref,
    time_ref,
    q_ref,
    k_ref,
    v_ref,
    qd_ref,
    kd_ref,
    vd_ref,
    w_hbm,
    noisy_ref,
    vel_ref,
    dq_out,
    dk_out,
    dv_out,
    gw_out,
    ms_out,
    w,
    kk,
    vv,
    qq,
    sbuf,
    stbuf,
    p16,
    acc1,
    acc2,
    ublk,
    uown,
    at_own,
    at,
    negb,
    part_a,
    part_b,
    rx_a,
    rx_b,
    sum_a,
    sum_b,
    part_a2,
    part_b2,
    rx_a2,
    rx_b2,
    cot,
    g_tx,
    g,
    dqt,
    dq_tx,
    dq_rx,
    dkv,
    sib_rx,
    dkv_tx,
    dkv_rx,
    tw_part,
    tw,
    sq_tp,
    sq_seq,
    wsem,
    kvx_send,
    kvx_recv,
    kvy_send,
    kvy_recv,
    fwx_send,
    fwx_recv,
    fwy_send,
    fwy_recv,
    q_send,
    q_recv,
    u_send,
    u_recv,
    atx_send,
    atx_recv,
    aty_send,
    aty_recv,
    at2_recv,
    atf_send,
    atf_recv,
    rsa_send,
    rsa_recv,
    rsb_send,
    rsb_recv,
    rsa2_send,
    rsa2_recv,
    rsb2_send,
    rsb2_recv,
    t_send,
    t_recv,
    g_send,
    g_recv,
    tw_send,
    tw_recv,
    twg_send,
    twg_recv,
    dq_send,
    dq_recv,
    sib_send,
    sib_recv,
    dkv_send,
    dkv_recv,
    sqt_send,
    sqt_recv,
    sqs_send,
    sqs_recv,
):
    s = lax.axis_index("seq")
    t = lax.axis_index("tp")
    x = s // 4
    y = (s // 2) % 2
    c = s % 2
    m = s // 2
    yh = t // 4
    z = t % 4
    head = x
    far = (2, 1, 3)

    def ring(pos, step):
        return lax.rem(pos + step, 4)

    def seq_dev(px, py, pc):
        return (px * 4 + py * 2 + pc, t)

    def tp_dev(pyh, pz):
        return (s, pyh * 4 + pz)

    def local_copy(src, dst, sem):
        return pltpu.make_async_copy(src, dst, sem)

    def remote(src, dst, ssem, rsem, dev):
        return pltpu.make_async_remote_copy(
            src_ref=src, dst_ref=dst, send_sem=ssem, recv_sem=rsem, device_id=dev, device_id_type=MESH
        )

    def lanes(index, width):
        return pl.ds(pl.multiple_of(index * width, width), width)

    def wait_for(ref, sem):
        pltpu.make_async_copy(ref, ref, sem).wait()

    pending = []

    def launch(copy):
        copy.start()
        pending.append(copy.wait_send)

    owed = {}

    def due(name):
        owed.pop(name)()

    def finish():
        for name in list(owed):
            due(name)
        for wait in pending:
            wait()

    wload = pltpu.make_async_copy(w_hbm, w, wsem)
    wload.start()
    owed["w"] = wload.wait

    barrier = pltpu.get_barrier_semaphore()
    sibling = s + 1 - 2 * c
    partners = [seq_dev(x, 1 - y, c), (sibling, t), tp_dev(1 - yh, z)]
    for dx in far:
        partners += [seq_dev(ring(x, dx), y, c), seq_dev(ring(x, dx), y, 1 - c), tp_dev(yh, ring(z, dx))]
    for dev in partners:
        pl.semaphore_signal(barrier, inc=1, device_id=dev, device_id_type=MESH)
    pl.semaphore_wait(barrier, len(partners))

    kv_src = (k_ref, kd_ref, v_ref, vd_ref)
    kv_dst = ((kk, 0), (kk, 1), (vv, 0), (vv, 1))

    def kv_view(a, px, py, pc):
        buf, half = kv_dst[a]
        return buf.at[px, py, pc, :, half * HD : (half + 1) * HD]

    def kv_piece(a, px):
        return kv_src[a].at[:, lanes(px, HD)]

    def kv_all(a, py, pc):
        return kv_view(a, slice(None), py, pc)

    def kv_own(a):
        local_copy(kv_piece(a, x), kv_view(a, x, y, c), kvx_recv.at[a]).start()
        launch(
            remote(
                kv_piece(a, x), kv_view(a, x, y, c), kvy_send.at[a, 0], kvy_recv.at[a], seq_dev(x, 1 - y, c)
            )
        )

    def kv_along_x(a):
        for dx in far:
            hx = ring(x, dx)
            launch(
                remote(
                    kv_piece(a, hx), kv_view(a, x, y, c), kvx_send.at[a, dx], kvx_recv.at[a], seq_dev(hx, y, c)
                )
            )
        owed["kvx", a] = lambda: wait_for(kv_all(a, y, c), kvx_recv.at[a])
        owed["kvy", a] = lambda: wait_for(kv_all(a, 1 - y, c), kvy_recv.at[a])

    def kv_across(a):
        due(("kvx", a))
        for dx in far:
            view = kv_view(a, ring(x, dx), y, c)
            launch(remote(view, view, kvy_send.at[a, dx], kvy_recv.at[a], seq_dev(x, 1 - y, c)))
        to_sibling(a, y, fwx_send, fwx_recv, "fwx")

    def to_sibling(a, py, send, recv, name):
        view = kv_all(a, py, c)
        launch(remote(view, view, send.at[a], recv.at[a], (sibling, t)))
        owed[name, a] = lambda: wait_for(kv_all(a, py, 1 - c), recv.at[a])

    def kv_received(a):
        due(("kvy", a))
        to_sibling(a, 1 - y, fwy_send, fwy_recv, "fwy")

    def kv_complete(a):
        due(("fwx", a))
        due(("fwy", a))

    home = jnp.where((x == 1) | (x == 2), 1, 0)
    unit = x // 2

    def to_heads(src_of, dst, send, recv, slot, act):
        for dx in (2, 1, 3, 0):
            hx = ring(x, dx)
            if dx:
                copy = remote(src_of(hx), dst, send.at[slot, dx], recv, seq_dev(hx, y, home))
                copy.start() if act == "start" else copy.wait_send()
            else:

                @pl.when(home != c)
                def _():
                    copy = remote(src_of(hx), dst, send.at[slot, dx], recv, seq_dev(hx, y, home))
                    copy.start() if act == "start" else copy.wait_send()

                if act == "start":

                    @pl.when(home == c)
                    def _():
                        local_copy(src_of(hx), dst, recv).start()

    def to_owners(src, dst, send, recv, act):
        for u in range(2):
            ux = c if u == 0 else 3 - c
            for core in range(2):
                dev = ux * 4 + y * 2 + core

                @pl.when(dev != s)
                def _():
                    copy = remote(src.at[u, core], dst, send.at[u, core], recv, (dev, t))
                    copy.start() if act == "start" else copy.wait_send()

                if act == "start":

                    @pl.when(dev == s)
                    def _():
                        local_copy(src.at[u, core], dst, recv).start()

    def q_moves(act):
        for a, ref in ((1, q_ref), (0, qd_ref)):
            to_heads(
                lambda hx, ref=ref: ref.at[:, lanes(hx, HD)],
                qq.at[unit, c, :, a * HD : (a + 1) * HD],
                q_send,
                q_recv,
                a,
                act,
            )

    kv_along_x(0)
    for a in range(4):
        kv_own(a)
    kv_along_x(1)
    kv_along_x(2)
    q_moves("start")
    pending.append(lambda: q_moves("wait"))
    owed["q"] = lambda: wait_for(qq, q_recv)
    kv_along_x(3)

    ends = []
    total = 0
    for f in range(FRAMES):
        total = total + frame_ref[f]
        ends.append(total)
    times = [time_ref[f] for f in range(FRAMES)]

    def frame_facts(pos):
        kend = jnp.zeros(pos.shape, jnp.int32) + ends[FRAMES - 1]
        level = jnp.zeros(pos.shape, jnp.int32) + times[FRAMES - 1]
        for f in range(FRAMES - 2, -1, -1):
            inside = pos < ends[f]
            kend = jnp.where(inside, ends[f], kend)
            level = jnp.where(inside, times[f], level)
        angle = (level.astype(F32) + 0.5) * (math.pi / (2 * TSTEPS))
        return kend, jnp.cos(angle), jnp.sin(angle)

    lane = lax.broadcasted_iota(jnp.int32, (1, NQ), 1)
    chip0 = 2 * c + y
    chip1 = 2 * (3 - c) + y
    qpos = jnp.where(lane < UNIT, UNIT * chip0 + lane, UNIT * chip1 + lane - UNIT)
    kend, cosq, sinq = frame_facts(qpos)

    rpos = s * ROWS + t * 20 + lax.broadcasted_iota(jnp.int32, (20, 1), 0)
    _, cosr, sinr = frame_facts(rpos)
    negb[...] = jnp.zeros_like(negb)
    negb[0:20, :] = sinr * cosr * noisy_ref[...].astype(F32) - cosr * cosr * vel_ref[...].astype(F32)

    n0 = chip0 + 2
    n1 = jnp.minimum(chip1 + 2, 8)

    def over_keys(body, carry, between=None):
        carry = lax.fori_loop(0, n0, lambda i, st: body(i, st, 0), carry)
        if between is not None:
            between()
        return lax.fori_loop(n0, n1, lambda i, st: body(i, st, 256), carry)

    def put(row, lo, part_row):
        if lo == 0:
            return part_row
        return jnp.concatenate([row[:, :lo], part_row], axis=1)

    kv_across(0)
    kv_across(1)
    kv_across(2)
    kv_received(0)
    kv_received(1)
    due("q")
    kv_complete(0)

    def chunk(buf, i):
        return buf[i // 2, i % 2].reshape(UNIT, buf.shape[-1])

    def pass1(i, top, lo):
        keys = kk[i // 2, i % 2, :, :, :HD].reshape(UNIT, HD)
        queries = qq[...].reshape(NQ, 2 * HD)[lo:, HD:]
        sc = dot_nt(keys, queries) * SCALE
        kpos = i * UNIT + lax.broadcasted_iota(jnp.int32, (UNIT, 1), 0)
        sc = jnp.where(kpos < kend[:, lo:], sc, -1e30)
        sbuf[i, :, lo:] = sc
        return put(top, lo, jnp.maximum(top[:, lo:], jnp.max(sc, axis=0, keepdims=True)))

    top = over_keys(pass1, jnp.full((1, NQ), -1e30, F32))

    kv_across(3)
    kv_complete(1)

    def pass2(i, state, lo):
        den, tan = state
        st = dot_nt(chunk(kk, i), qq[...].reshape(NQ, 2 * HD)[lo:]) * SCALE
        p = jnp.exp(sbuf[i, :, lo:] - top[:, lo:])
        sbuf[i, :, lo:] = p
        stbuf[i, :, lo:] = st
        den = put(den, lo, den[:, lo:] + jnp.sum(p, axis=0, keepdims=True))
        tan = put(tan, lo, tan[:, lo:] + jnp.sum(p * st, axis=0, keepdims=True))
        return den, tan

    row0 = jnp.zeros((1, NQ), F32)
    den, tan = over_keys(pass2, (row0, row0), lambda: kv_received(2))
    inv = 1.0 / den
    mean = tan * inv
    kv_complete(2)

    acc1[...] = jnp.zeros_like(acc1)
    acc2[...] = jnp.zeros_like(acc2)

    def pass3(i, state, lo):
        p = sbuf[i, :, lo:] * inv[:, lo:]
        ph = p.astype(BF16)
        p16[i, :, lo:] = ph
        ds = (p * (stbuf[i, :, lo:] - mean[:, lo:])).astype(BF16)
        vals = vv[i // 2, i % 2, :, :, :HD].reshape(UNIT, HD)
        acc1[:, lo:] += dot_tn(vals, ph)
        acc2[:, lo:] += dot_tn(vals, ds)
        return state

    over_keys(pass3, 0, lambda: kv_received(3))
    kv_complete(3)

    def pass4(i, state, lo):
        vals_dot = vv[i // 2, i % 2, :, :, HD:].reshape(UNIT, HD)
        acc2[:, lo:] += dot_tn(vals_dot, p16[i, :, lo:])
        return state

    over_keys(pass4, 0)
    attn_t = acc1[...].astype(BF16)
    tan_t = acc2[...].astype(BF16)
    at_own[...] = attn_t
    u_t = (0.5 * cosq) * (cosq * attn_t.astype(F32) + sinq * tan_t.astype(F32))
    ublk[...] = u_t.T.astype(BF16).reshape(2, 2, ROWS, HD)
    to_owners(ublk, uown.at[:, lanes(head, HD)], u_send, u_recv, "start")
    owed["u"] = lambda: wait_for(uown, u_recv)
    pending.append(lambda: to_owners(ublk, uown.at[:, lanes(head, HD)], u_send, u_recv, "wait"))

    def at_view(py, hx):
        return at.at[py, c, lanes(hx, HD), :]

    def at_pass_on():
        due("aty")
        for dx in far:
            view = at_view(1 - y, x)
            launch(remote(view, view, atx_send.at[1, dx], at2_recv, seq_dev(ring(x, dx), y, c)))
        owed["at2"] = lambda: wait_for(at.at[1 - y, c, 0 : 3 * HD], at2_recv)

    due("w")
    due("u")
    u = uown[...]
    pick = (
        lax.broadcasted_iota(jnp.int32, (ROWS, 32), 0)
        == t * 20 + lax.broadcasted_iota(jnp.int32, (ROWS, 32), 1)
    ) & (lax.broadcasted_iota(jnp.int32, (ROWS, 32), 1) < 20)
    pick = pick.astype(F32).astype(BF16)

    def partial(pyh, pz, half):
        cols = pl.ds(pl.multiple_of((pyh * 4 + pz) * 512 + half * 256, 256), 256)
        return dot_nn(u, w[:, cols]) + dot_nn(pick, negb[:, cols].astype(BF16))

    for dz in range(4):
        part_b[dz] = partial(1 - yh, ring(z, dz), 1).astype(BF16)
    halves = [slice(0, 80), slice(80, 160)]

    def stage(name, key, src, dst, send, recv, dev):
        copy = remote(src, dst, send.at[key], recv.at[key], dev)
        launch(copy)
        owed[(name,) + key] = copy.wait_recv

    def send_b(hf):
        rows = halves[hf]
        stage("rsb", (hf,), part_b.at[:, rows], rx_b.at[:, rows], rsb_send, rsb_recv, tp_dev(1 - yh, z))

    send_b(0)

    for dz in far:
        for e in range(2):
            part_a[dz, e] = partial(yh if e == 0 else 1 - yh, ring(z, dz), 0).astype(BF16)

    def send_a(hf):
        rows = halves[hf]
        for dz in far:
            dev = tp_dev(yh, ring(z, dz))
            stage("rsa", (hf, dz), part_a.at[dz, :, rows], rx_a.at[dz, :, rows], rsa_send, rsa_recv, dev)

    send_a(0)
    send_b(1)
    send_a(1)

    local_copy(at_own, at_view(y, x), atx_recv).start()
    launch(remote(at_own, at_view(y, x), aty_send, aty_recv, seq_dev(x, 1 - y, c)))
    owed["aty"] = lambda: wait_for(at_view(1 - y, x), aty_recv)
    for dx in far:
        launch(remote(at_own, at_view(y, x), atx_send.at[0, dx], atx_recv, seq_dev(ring(x, dx), y, c)))
    owed["atx"] = lambda: wait_for(at.at[y, c], atx_recv)

    for dz in range(4):
        sum_b[dz] = partial(yh, ring(z, dz), 1)
    for e in range(2):
        sum_a[e] = partial(yh if e == 0 else 1 - yh, z, 0)


    def cot_copy(a, src, dst, dev, hf):
        rows = halves[hf]
        sem = (a,) + dst + (hf,)
        stage("t", sem, cot.at[(a,) + src + (rows,)], cot.at[(a,) + dst + (rows,)], t_send, t_recv, dev)

    for hf in range(2):
        rows = halves[hf]
        due(("rsb", hf))
        for dz in far:
            part_b2[dz, rows] = (sum_b[dz, rows] + rx_b[dz, rows].astype(F32)).astype(BF16)
            dev = tp_dev(yh, ring(z, dz))
            stage("rsb2", (hf, dz), part_b2.at[dz, rows], rx_b2.at[dz, rows], rsb2_send, rsb2_recv, dev)
        other = sum_a[1, rows]
        for dz in far:
            due(("rsa", hf, dz))
            other = other + rx_a[dz, 1, rows].astype(F32)
        part_a2[rows] = other.astype(BF16)
        stage("rsa2", (hf,), part_a2.at[rows], rx_a2.at[rows], rsa2_send, rsa2_recv, tp_dev(1 - yh, z))

    sq = jnp.zeros((1, 256), F32)
    for hf in range(2):
        rows = halves[hf]
        cot_a = sum_a[0, rows]
        for dz in far:
            cot_a = cot_a + rx_a[dz, 0, rows].astype(F32)
        due(("rsa2", hf))
        cot_a = cot_a + rx_a2[rows].astype(F32)
        cot[0, 0, 0, rows] = cot_a.astype(BF16)
        for dz in far:
            cot_copy(0, (0, 0), (0, dz), tp_dev(yh, ring(z, dz)), hf)
        cot_b = sum_b[0, rows] + rx_b[0, rows].astype(F32)
        for dz in far:
            due(("rsb2", hf, dz))
            cot_b = cot_b + rx_b2[dz, rows].astype(F32)
        cot[1, 0, 0, rows] = cot_b.astype(BF16)
        cot_copy(1, (0, 0), (1, 0), tp_dev(1 - yh, z), hf)
        for dz in far:
            cot_copy(1, (0, 0), (0, dz), tp_dev(yh, ring(z, dz)), hf)
        cot_copy(0, (0, 0), (1, 0), tp_dev(1 - yh, z), hf)
        sq = sq + jnp.sum(cot_a * cot_a + cot_b * cot_b, axis=0, keepdims=True)

    def sq_copy(buf, d, send, recv, dev, name):
        copy = remote(buf.at[0], buf.at[d], send.at[d], recv.at[d], dev)
        launch(copy)
        owed[name, d] = copy.wait_recv

    sq_tp[0] = jnp.zeros((8, 128), F32) + jnp.sum(sq, axis=1, keepdims=True)
    for d in range(1, 8):
        sq_copy(sq_tp, d, sqt_send, sqt_recv, (s, lax.rem(t + d, 8)), "sqt")

    at_pass_on()

    def grad_part(a, dyh, dz):
        pyh = lax.rem(yh + dyh, 2)
        pz = lax.rem(z + 4 - dz, 4)
        cols = pl.ds(pl.multiple_of((pyh * 4 + pz) * 512 + a * 256, 256), 256)
        return dot_nt(cot[a, dyh, dz], w[:, cols])

    grad = grad_part(0, 0, 0) + grad_part(1, 0, 0)
    for hf in range(2):
        due(("t", 1, 1, 0, hf))
        for dz in far:
            cot_copy(1, (1, 0), (1, dz), tp_dev(yh, ring(z, dz)), hf)
        for dz in (1, 3, 2):
            due(("t", 0, 0, dz, hf))
            cot_copy(0, (0, dz), (1, dz), tp_dev(1 - yh, z), hf)
    grad = grad + grad_part(1, 1, 0)
    for dz in (1, 3, 2):
        grad = grad + grad_part(0, 0, dz)
        due(("t", 1, 0, dz, 0))
        due(("t", 1, 0, dz, 1))
        grad = grad + grad_part(1, 0, dz)
    for a, dz in ((0, 0), (0, 1), (0, 3), (0, 2), (1, 1), (1, 3), (1, 2)):
        due(("t", a, 1, dz, 0))
        due(("t", a, 1, dz, 1))
        grad = grad + grad_part(a, 1, dz)
    g_tx[...] = grad.astype(BF16)

    def g_moves(act):
        to_heads(lambda hx: g_tx.at[:, lanes(hx, HD)], g.at[unit, c], g_send, g_recv, 0, act)

    g_moves("start")
    owed["g"] = lambda: wait_for(g, g_recv)
    pending.append(lambda: g_moves("wait"))

    row_half = pl.ds(pl.multiple_of(80 * (z % 2), 16), 80)
    chip_slot = y * 4 + home * 2 + unit

    def tw_send_all(act):
        for d in (8, 9, 7, 6, 10, 4, 12, 5, 11, 3, 13, 2, 14, 1, 15, 0):
            dest = lax.rem(s + d, 16)
            tt = dest // 2
            dyh = lax.rem(yh + tt // 4, 2)
            dz = lax.rem(z + 4 - tt % 4, 4)
            src = cot.at[dest % 2, dyh, dz, row_half, lanes(yh, HD)]
            dst = tw_part.at[chip_slot]
            if d:
                copy = remote(src, dst, tw_send.at[d], tw_recv, (dest, t))
                copy.start() if act == "start" else copy.wait_send()
            elif act == "start":
                local_copy(src, dst, tw_recv).start()

    def tw_turn(act):
        @pl.when(c == z // 2)
        def _():
            tw_send_all(act)

    tw_turn("start")
    owed["tw"] = lambda: wait_for(tw_part, tw_recv)
    pending.append(lambda: tw_turn("wait"))

    sqv = sq_tp[0]
    for d in range(1, 8):
        due(("sqt", d))
        sqv = sqv + sq_tp[d]
    sq_seq[0] = sqv
    for d in range(1, 16):
        sq_copy(sq_seq, d, sqs_send, sqs_recv, (lax.rem(s + d, 16), t), "sqs")

    due("tw")

    def tw_view(dyh, dz):
        pyh = lax.rem(yh + dyh, 2)
        pz = lax.rem(z + 4 - dz, 4)
        rows = pl.ds(pl.multiple_of(80 * (pz % 2), 16), 80)
        return tw.at[:, pz // 2, rows, lanes(pyh, HD)]

    def twg_copy(origin, slot, dev):
        view = tw_view(*origin)
        src = tw_part if origin == (0, 0) else view
        stage("twg", slot, src, view, twg_send, twg_recv, dev)

    twg_copy((0, 0), (1, 0), tp_dev(1 - yh, z))
    local_copy(tw_part, tw_view(0, 0), twg_recv.at[0, 0]).start()
    owed["twg", 0, 0] = lambda: wait_for(tw_view(0, 0), twg_recv.at[0, 0])
    for dz in far:
        twg_copy((0, 0), (0, dz), tp_dev(yh, ring(z, dz)))

    def tw_pass_on():
        due(("twg", 1, 0))
        for dz in far:
            twg_copy((1, 0), (1, dz), tp_dev(yh, ring(z, dz)))

    due("g")
    gt = g[...].reshape(NQ, HD).astype(F32).T
    dterm = jnp.sum(gt * at_own[...].astype(F32), axis=0, keepdims=True)
    dqt[...] = jnp.zeros_like(dqt)

    def back(i, lo):
        gq = g[...].reshape(NQ, HD)[lo:]
        queries = qq[...].reshape(NQ, 2 * HD)[lo:, HD:]
        keys = chunk(kk, i)[:, :HD]
        vals = chunk(vv, i)[:, :HD]
        ph = p16[i, :, lo:]
        dp = dot_nt(vals, gq)
        ds = (ph.astype(F32) * (dp - dterm[:, lo:])).astype(BF16)
        dkv[1, i] = dot_nn(ph, gq).astype(BF16).reshape(2, ROWS, HD)
        dkv[0, i] = (dot_nn(ds, queries) * SCALE).astype(BF16).reshape(2, ROWS, HD)
        dqt[:, lo:] += dot_tn(keys, ds)

    def sib_copy(i):
        return remote(
            dkv.at[:, i, 1 - c], sib_rx.at[:, i], sib_send.at[i], sib_recv.at[i], (sibling, t)
        )

    def dkv_copy(i):
        return remote(
            dkv_tx.at[:, i], dkv_rx.at[m], dkv_send.at[i], dkv_recv.at[m], seq_dev(i // 2, i % 2, c)
        )

    def both_cores(i):
        sib_copy(i).wait_recv()
        return dkv[:, i, c].astype(F32) + sib_rx[:, i].astype(F32)

    def back_step(k, state):
        i = lax.rem(m + 1 + k, 8)

        @pl.when(i < n0)
        def _():
            back(i, 0)

        @pl.when((i >= n0) & (i < n1))
        def _():
            back(i, 256)

        @pl.when(i >= n1)
        def _():
            dkv[:, i] = jnp.zeros((2, 2, ROWS, HD), BF16)

        sib_copy(i).start()

        @pl.when(k > 0)
        def _():
            done = lax.rem(m + k, 8)
            dkv_tx[:, done] = both_cores(done).astype(BF16)
            dkv_copy(done).start()

        return state

    lax.fori_loop(0, 5, back_step, 0)
    tw_pass_on()
    lax.fori_loop(5, 8, back_step, 0)
    dq_tx[...] = (dqt[...] * SCALE).T.astype(BF16).reshape(2, 2, ROWS, HD)
    to_owners(dq_tx, dq_rx.at[:, lanes(head, HD)], dq_send, dq_recv, "start")
    owed["dq"] = lambda: wait_for(dq_rx, dq_recv)
    pending.append(lambda: to_owners(dq_tx, dq_rx.at[:, lanes(head, HD)], dq_send, dq_recv, "wait"))
    dkv_rx[m] = both_cores(m).astype(BF16)

    due("atx")
    due("at2")
    atf = remote(at.at[:, c], at.at[:, c], atf_send, atf_recv, (sibling, t))
    launch(atf)
    owed["atf"] = atf.wait_recv
    for dyh in range(2):
        for dz in range(4):
            if (dyh, dz) != (1, 0):
                due(("twg", dyh, dz))
    due("atf")

    gw = jnp.zeros((512, 256), F32)
    for a in range(4):
        rows = tw[2 * a : 2 * a + 2].reshape(NQ, 256)
        gw = gw + dot_nn(at[a // 2, a % 2], rows)
    gw_out[...] = gw

    sqv = sq_seq[0]
    for d in range(1, 16):
        due(("sqs", d))
        sqv = sqv + sq_seq[d]
    ms_out[...] = sqv

    due("dq")
    dq_out[...] = dq_rx[...]

    def all_dkv(k, state):
        i = lax.rem(m + 1 + k, 8)
        sib_copy(i).wait_send()

        @pl.when(k < 7)
        def _():
            dkv_copy(i).wait_send()
            remote(dkv_tx.at[:, i], dkv_rx.at[i], dkv_send.at[i], dkv_recv.at[i], (sibling, t)).wait_recv()

        return state

    lax.fori_loop(0, 8, all_dkv, 0)
    for h in range(4):
        for a, out in enumerate((dk_out, dv_out)):
            out[:, h * HD : (h + 1) * HD] = dkv_rx[2 * h, a].astype(F32) + dkv_rx[2 * h + 1, a].astype(F32)
    finish()


def scaled(ms_ref, *refs):
    scale = lax.rsqrt(ms_ref[0:1, 0:1] / (2560 * 4096) + 1e-05)
    for src, dst in zip(refs[:4], refs[4:]):
        dst[...] = (src[...].astype(F32) * scale).astype(BF16)


def on_device(q, k, v, qd, kd, vd, w, noisy, vel, time_index, frame_lengths):
    smem = pl.BlockSpec(memory_space=pltpu.SMEM)
    vmem = pl.BlockSpec(memory_space=pltpu.VMEM)
    hbm = pl.BlockSpec(memory_space=pl.ANY)
    dma = pltpu.SemaphoreType.DMA
    scratch = [
        pltpu.VMEM((512, 4096), BF16),
        pltpu.VMEM((4, 2, 2, ROWS, 256), BF16),
        pltpu.VMEM((4, 2, 2, ROWS, 256), BF16),
        pltpu.VMEM((2, 2, ROWS, 256), BF16),
        pltpu.VMEM((8, UNIT, NQ), F32),
        pltpu.VMEM((8, UNIT, NQ), F32),
        pltpu.VMEM((8, UNIT, NQ), BF16),
        pltpu.VMEM((HD, NQ), F32),
        pltpu.VMEM((HD, NQ), F32),
        pltpu.VMEM((2, 2, ROWS, HD), BF16),
        pltpu.VMEM((ROWS, 512), BF16),
        pltpu.VMEM((HD, NQ), BF16),
        pltpu.VMEM((2, 2, 512, NQ), BF16),
        pltpu.VMEM((32, 4096), F32),
        pltpu.VMEM((4, 2, ROWS, 256), BF16),
        pltpu.VMEM((4, ROWS, 256), BF16),
        pltpu.VMEM((4, 2, ROWS, 256), BF16),
        pltpu.VMEM((4, ROWS, 256), BF16),
        pltpu.VMEM((2, ROWS, 256), F32),
        pltpu.VMEM((4, ROWS, 256), F32),
        pltpu.VMEM((ROWS, 256), BF16),
        pltpu.VMEM((4, ROWS, 256), BF16),
        pltpu.VMEM((ROWS, 256), BF16),
        pltpu.VMEM((4, ROWS, 256), BF16),
        pltpu.VMEM((2, 2, 4, ROWS, 256), BF16),
        pltpu.VMEM((ROWS, 512), BF16),
        pltpu.VMEM((2, 2, ROWS, HD), BF16),
        pltpu.VMEM((HD, NQ), F32),
        pltpu.VMEM((2, 2, ROWS, HD), BF16),
        pltpu.VMEM((ROWS, 512), BF16),
        pltpu.VMEM((2, 8, 2, ROWS, HD), BF16),
        pltpu.VMEM((2, 8, ROWS, HD), BF16),
        pltpu.VMEM((2, 8, ROWS, HD), BF16),
        pltpu.VMEM((8, 2, ROWS, HD), BF16),
        pltpu.VMEM((8, 80, HD), BF16),
        pltpu.VMEM((8, 2, ROWS, 256), BF16),
        pltpu.VMEM((8, 8, 128), F32),
        pltpu.VMEM((16, 8, 128), F32),
        dma,
        dma((4, 4)),
        dma((4,)),
        dma((4, 4)),
        dma((4,)),
        dma((4,)),
        dma((4,)),
        dma((4,)),
        dma((4,)),
        dma((2, 4)),
        dma,
        dma((2, 2)),
        dma,
        dma((2, 4)),
        dma,
        dma,
        dma,
        dma,
        dma,
        dma,
        dma((2, 4)),
        dma((2, 4)),
        dma((2,)),
        dma((2,)),
        dma((2,)),
        dma((2,)),
        dma((2, 4)),
        dma((2, 4)),
        dma((2, 2, 4, 2)),
        dma((2, 2, 4, 2)),
        dma((1, 4)),
        dma,
        dma((16,)),
        dma,
        dma((2, 4)),
        dma((2, 4)),
        dma((2, 2)),
        dma,
        dma((8,)),
        dma((8,)),
        dma((8,)),
        dma((8,)),
        dma((8,)),
        dma((8,)),
        dma((16,)),
        dma((16,)),
    ]
    dq, dk, dv, gw, ms = pl.pallas_call(
        kernel,
        out_shape=(
            jax.ShapeDtypeStruct((ROWS, 512), BF16),
            jax.ShapeDtypeStruct((ROWS, 512), F32),
            jax.ShapeDtypeStruct((ROWS, 512), F32),
            jax.ShapeDtypeStruct((512, 256), F32),
            jax.ShapeDtypeStruct((8, 128), F32),
        ),
        in_specs=[smem, smem] + [hbm] * 7 + [vmem] * 2,
        out_specs=(vmem,) * 5,
        scratch_shapes=scratch,
        compiler_params=pltpu.CompilerParams(
            collective_id=0, has_side_effects=True, vmem_limit_bytes=56 * 1024 * 1024
        ),
        cost_estimate=pl.CostEstimate(flops=7 * 10**9, bytes_accessed=8 * 10**6, transcendentals=1638400),
    )(frame_lengths, time_index, q, k, v, qd, kd, vd, w, noisy, vel)
    return pl.pallas_call(
        scaled,
        out_shape=tuple(jax.ShapeDtypeStruct(part.shape, BF16) for part in (dq, dk, dv, gw)),
        in_specs=[vmem] * 5,
        out_specs=(vmem,) * 4,
    )(ms, dq, dk, dv, gw)


def solution(mesh):
    in_specs = (P("seq", "tp"),) * 6 + (P("tp", None), P(("seq", "tp"), None), P(("seq", "tp"), None), P(), P())
    out_specs = (P("seq", "tp"), P("seq", "tp"), P("seq", "tp"), P("tp", "seq"))
    return jax.shard_map(
        on_device, mesh=mesh, in_specs=in_specs, out_specs=out_specs, check_vma=False
    )
```

```python
import math

import jax
import jax.numpy as jnp
from jax import lax
from jax.experimental import pallas as pl
from jax.experimental.pallas import tpu as pltpu
from jax.sharding import PartitionSpec as P

HD = 128
TSTEPS = 64
FRAMES = 16
ROWS = 160
UNIT = 320
NCHIP = 8
NQ = 640
SCALE = 1.0 / math.sqrt(HD)
MESH = pl.DeviceIdType.MESH
F32 = jnp.float32
BF16 = jnp.bfloat16


def dot_nt(a, b):
    return lax.dot_general(a, b, (((1,), (1,)), ((), ())), preferred_element_type=F32)


def dot_nn(a, b):
    return lax.dot_general(a, b, (((1,), (0,)), ((), ())), preferred_element_type=F32)


def dot_tn(a, b):
    return lax.dot_general(a, b, (((0,), (0,)), ((), ())), preferred_element_type=F32)


def kernel(
    frame_ref,
    time_ref,
    q_ref,
    k_ref,
    v_ref,
    qd_ref,
    kd_ref,
    vd_ref,
    w_hbm,
    noisy_ref,
    vel_ref,
    dq_out,
    dk_out,
    dv_out,
    gw_out,
    ms_out,
    w,
    kk,
    vv,
    qq,
    sbuf,
    stbuf,
    p16,
    acc1,
    acc2,
    ublk,
    uown,
    at_own,
    at,
    negb,
    lat,
    lat_sem,
    part_a,
    part_b,
    rx_a,
    rx_b,
    sum_a,
    sum_b,
    part_a2,
    part_b2,
    rx_a2,
    rx_b2,
    cot,
    g_tx,
    g,
    dqt,
    dq_tx,
    dq_rx,
    dkv,
    sib_rx,
    dkv_tx,
    dkv_rx,
    tw_part,
    tw,
    sq_tp,
    sq_seq,
    wsem,
    kvx_send,
    kvx_recv,
    kvy_send,
    kvy_recv,
    fwx_send,
    fwx_recv,
    fwy_send,
    fwy_recv,
    q_send,
    q_recv,
    u_send,
    u_recv,
    atx_send,
    atx_recv,
    aty_send,
    aty_recv,
    at2_recv,
    atf_send,
    atf_recv,
    rsa_send,
    rsa_recv,
    rsb_send,
    rsb_recv,
    rsa2_send,
    rsa2_recv,
    rsb2_send,
    rsb2_recv,
    t_send,
    t_recv,
    g_send,
    g_recv,
    tw_send,
    twd_send,
    twd_recv,
    tw_recv,
    twg_send,
    twg_recv,
    dq_send,
    dq_recv,
    sib_send,
    sib_recv,
    dkv_send,
    dkv_recv,
    sqt_send,
    sqt_recv,
    sqs_send,
    sqs_recv,
):
    s = lax.axis_index("seq")
    t = lax.axis_index("tp")
    x = s // 4
    y = (s // 2) % 2
    c = s % 2
    m = s // 2
    yh = t // 4
    z = t % 4
    head = x
    far = (2, 1, 3)

    def ring(pos, step):
        return lax.rem(pos + step, 4)

    def seq_dev(px, py, pc):
        return (px * 4 + py * 2 + pc, t)

    def tp_dev(pyh, pz):
        return (s, pyh * 4 + pz)

    def local_copy(src, dst, sem):
        return pltpu.make_async_copy(src, dst, sem)

    def remote(src, dst, ssem, rsem, dev):
        return pltpu.make_async_remote_copy(
            src_ref=src, dst_ref=dst, send_sem=ssem, recv_sem=rsem, device_id=dev, device_id_type=MESH
        )

    def lanes(index, width):
        return pl.ds(pl.multiple_of(index * width, width), width)

    def wait_for(ref, sem):
        pltpu.make_async_copy(ref, ref, sem).wait()

    pending = []

    def launch(copy):
        copy.start()
        pending.append(copy.wait_send)

    owed = {}

    def due(name):
        owed.pop(name)()

    def finish():
        for name in list(owed):
            due(name)
        for wait in pending:
            wait()

    wload = pltpu.make_async_copy(w_hbm, w, wsem)
    wload.start()
    lat_loads = [pltpu.make_async_copy(ref, lat.at[i], lat_sem.at[i]) for i, ref in enumerate((noisy_ref, vel_ref))]
    for i, load in enumerate(lat_loads):
        load.start()
        owed["lat", i] = load.wait
    owed["w"] = wload.wait

    barrier = pltpu.get_barrier_semaphore()
    sibling = s + 1 - 2 * c
    partners = [seq_dev(x, 1 - y, c), (sibling, t), tp_dev(1 - yh, z)]
    for dx in far:
        partners += [seq_dev(ring(x, dx), y, c), seq_dev(ring(x, dx), y, 1 - c), tp_dev(yh, ring(z, dx))]
    for dev in partners:
        pl.semaphore_signal(barrier, inc=1, device_id=dev, device_id_type=MESH)
    pl.semaphore_wait(barrier, len(partners))

    kv_src = (k_ref, kd_ref, v_ref, vd_ref)
    kv_dst = ((kk, 0), (kk, 1), (vv, 0), (vv, 1))

    def kv_view(a, px, py, pc):
        buf, half = kv_dst[a]
        return buf.at[px, py, pc, :, half * HD : (half + 1) * HD]

    def kv_piece(a, px):
        return kv_src[a].at[:, lanes(px, HD)]

    def kv_all(a, py, pc):
        return kv_view(a, slice(None), py, pc)

    def kv_own(a):
        local_copy(kv_piece(a, x), kv_view(a, x, y, c), kvx_recv.at[a]).start()
        launch(
            remote(
                kv_piece(a, x), kv_view(a, x, y, c), kvy_send.at[a, 0], kvy_recv.at[a], seq_dev(x, 1 - y, c)
            )
        )

    def kv_along_x(a):
        for dx in far:
            hx = ring(x, dx)
            launch(
                remote(
                    kv_piece(a, hx), kv_view(a, x, y, c), kvx_send.at[a, dx], kvx_recv.at[a], seq_dev(hx, y, c)
                )
            )
        owed["kvx", a] = lambda: wait_for(kv_all(a, y, c), kvx_recv.at[a])
        owed["kvy", a] = lambda: wait_for(kv_all(a, 1 - y, c), kvy_recv.at[a])

    def kv_across(a):
        due(("kvx", a))
        for dx in far:
            view = kv_view(a, ring(x, dx), y, c)
            launch(remote(view, view, kvy_send.at[a, dx], kvy_recv.at[a], seq_dev(x, 1 - y, c)))
        to_sibling(a, y, fwx_send, fwx_recv, "fwx")

    def to_sibling(a, py, send, recv, name):
        view = kv_all(a, py, c)
        launch(remote(view, view, send.at[a], recv.at[a], (sibling, t)))
        owed[name, a] = lambda: wait_for(kv_all(a, py, 1 - c), recv.at[a])

    def kv_received(a):
        due(("kvy", a))
        to_sibling(a, 1 - y, fwy_send, fwy_recv, "fwy")

    def kv_complete(a):
        due(("fwx", a))
        due(("fwy", a))

    home = jnp.where((x == 1) | (x == 2), 1, 0)
    unit = x // 2

    def to_heads(src_of, dst, send, recv, slot, act):
        for dx in (2, 1, 3, 0):
            hx = ring(x, dx)
            if dx:
                copy = remote(src_of(hx), dst, send.at[slot, dx], recv, seq_dev(hx, y, home))
                copy.start() if act == "start" else copy.wait_send()
            else:

                @pl.when(home != c)
                def _():
                    copy = remote(src_of(hx), dst, send.at[slot, dx], recv, seq_dev(hx, y, home))
                    copy.start() if act == "start" else copy.wait_send()

                if act == "start":

                    @pl.when(home == c)
                    def _():
                        local_copy(src_of(hx), dst, recv).start()

    def to_owners(src, dst, send, recv, act):
        for u in range(2):
            ux = c if u == 0 else 3 - c
            for core in range(2):
                dev = ux * 4 + y * 2 + core

                @pl.when(dev != s)
                def _():
                    copy = remote(src.at[u, core], dst, send.at[u, core], recv, (dev, t))
                    copy.start() if act == "start" else copy.wait_send()

                if act == "start":

                    @pl.when(dev == s)
                    def _():
                        local_copy(src.at[u, core], dst, recv).start()

    def q_moves(act, which=(1, 0)):
        for a in which:
            ref = (qd_ref, q_ref)[a]
            to_heads(
                lambda hx, ref=ref: ref.at[:, lanes(hx, HD)],
                qq.at[unit, c, :, a * HD : (a + 1) * HD],
                q_send,
                q_recv.at[a],
                a,
                act,
            )

    kv_along_x(0)
    for a in range(4):
        kv_own(a)
    kv_along_x(1)
    q_moves("start", (1,))
    kv_along_x(2)
    q_moves("start", (0,))
    pending.append(lambda: q_moves("wait"))
    for a in range(2):
        owed["q", a] = lambda a=a: wait_for(qq.at[:, :, :, a * HD : (a + 1) * HD], q_recv.at[a])
    kv_along_x(3)

    ends = []
    total = 0
    for f in range(FRAMES):
        total = total + frame_ref[f]
        ends.append(total)
    times = [time_ref[f] for f in range(FRAMES)]

    def frame_facts(pos):
        kend = jnp.zeros(pos.shape, jnp.int32) + ends[FRAMES - 1]
        level = jnp.zeros(pos.shape, jnp.int32) + times[FRAMES - 1]
        for f in range(FRAMES - 2, -1, -1):
            inside = pos < ends[f]
            kend = jnp.where(inside, ends[f], kend)
            level = jnp.where(inside, times[f], level)
        angle = (level.astype(F32) + 0.5) * (math.pi / (2 * TSTEPS))
        return kend, jnp.cos(angle), jnp.sin(angle)

    lane = lax.broadcasted_iota(jnp.int32, (1, NQ), 1)
    chip0 = 2 * c + y
    chip1 = 2 * (3 - c) + y
    qpos = jnp.where(lane < UNIT, UNIT * chip0 + lane, UNIT * chip1 + lane - UNIT)
    kend, cosq, sinq = frame_facts(qpos)

    rpos = s * ROWS + t * 20 + lax.broadcasted_iota(jnp.int32, (20, 1), 0)
    _, cosr, sinr = frame_facts(rpos)
    for i in range(2):
        due(("lat", i))
    negb[...] = jnp.zeros_like(negb)
    negb[0:20, :] = sinr * cosr * lat[0].astype(F32) - cosr * cosr * lat[1].astype(F32)

    n0 = chip0 + 2
    n1 = jnp.minimum(chip1 + 2, 8)

    def over_keys(body, carry, between=None):
        carry = lax.fori_loop(0, n0, lambda i, st: body(i, st, 0), carry)
        if between is not None:
            between()
        return lax.fori_loop(n0, n1, lambda i, st: body(i, st, 256), carry)

    def put(row, lo, part_row):
        if lo == 0:
            return part_row
        return jnp.concatenate([row[:, :lo], part_row], axis=1)

    kv_across(0)
    kv_across(1)
    kv_across(2)
    kv_received(0)
    due(("q", 1))
    kv_complete(0)

    def chunk(buf, i):
        return buf[i // 2, i % 2].reshape(UNIT, buf.shape[-1])

    def pass1(i, top, lo):
        keys = kk[i // 2, i % 2, :, :, :HD].reshape(UNIT, HD)
        queries = qq[:, :, :, HD:].reshape(NQ, HD)[lo:]
        sc = dot_nt(keys, queries) * SCALE
        kpos = i * UNIT + lax.broadcasted_iota(jnp.int32, (UNIT, 1), 0)
        sc = jnp.where(kpos < kend[:, lo:], sc, -1e30)
        sbuf[i, :, lo:] = sc
        return put(top, lo, jnp.maximum(top[:, lo:], jnp.max(sc, axis=0, keepdims=True)))

    top = over_keys(pass1, jnp.full((1, NQ), -1e30, F32))

    kv_received(1)
    due(("q", 0))
    kv_across(3)
    kv_complete(1)

    def pass2(i, state, lo):
        den, tan = state
        st = dot_nt(chunk(kk, i), qq[...].reshape(NQ, 2 * HD)[lo:]) * SCALE
        p = jnp.exp(sbuf[i, :, lo:] - top[:, lo:])
        sbuf[i, :, lo:] = p
        stbuf[i, :, lo:] = st
        den = put(den, lo, den[:, lo:] + jnp.sum(p, axis=0, keepdims=True))
        tan = put(tan, lo, tan[:, lo:] + jnp.sum(p * st, axis=0, keepdims=True))
        return den, tan

    row0 = jnp.zeros((1, NQ), F32)
    den, tan = over_keys(pass2, (row0, row0), lambda: kv_received(2))
    inv = 1.0 / den
    mean = tan * inv
    kv_complete(2)

    acc2[...] = jnp.zeros_like(acc2)

    def pass3(i, state, lo):
        p = sbuf[i, :, lo:] * inv[:, lo:]
        p16[i, :, lo:] = p.astype(BF16)
        ds = (p * (stbuf[i, :, lo:] - mean[:, lo:])).astype(BF16)
        vals = vv[i // 2, i % 2, :, :, :HD].reshape(UNIT, HD)
        acc2[:, lo:] += dot_tn(vals, ds)
        return state

    over_keys(pass3, 0, lambda: kv_received(3))
    kv_complete(3)
    acc1[...] = jnp.zeros_like(acc1)

    def pass4(i, state, lo):
        acc1[:, lo:] += dot_tn(chunk(vv, i), p16[i, :, lo:])
        return state

    over_keys(pass4, 0)
    attn_t = acc1[0:HD].astype(BF16)
    tan_t = (acc2[...] + acc1[HD:]).astype(BF16)
    at_own[...] = attn_t
    u_t = (0.5 * cosq) * (cosq * attn_t.astype(F32) + sinq * tan_t.astype(F32))
    ublk[...] = u_t.T.astype(BF16).reshape(2, 2, ROWS, HD)
    to_owners(ublk, uown.at[:, lanes(head, HD)], u_send, u_recv, "start")
    owed["u"] = lambda: wait_for(uown, u_recv)
    pending.append(lambda: to_owners(ublk, uown.at[:, lanes(head, HD)], u_send, u_recv, "wait"))

    def at_view(py, hx):
        return at.at[py, c, lanes(hx, HD), :]

    launch(remote(at_own, at_view(y, x), aty_send, aty_recv, seq_dev(x, 1 - y, c)))
    owed["aty"] = lambda: wait_for(at_view(1 - y, x), aty_recv)

    def at_pass_on():
        due("aty")
        for dx in far:
            view = at_view(1 - y, x)
            launch(remote(view, view, atx_send.at[1, dx], at2_recv, seq_dev(ring(x, dx), y, c)))
        owed["at2"] = lambda: wait_for(at.at[1 - y, c, 0 : 3 * HD], at2_recv)

    due("w")
    due("u")
    u = uown[...]
    pick = (
        lax.broadcasted_iota(jnp.int32, (ROWS, 32), 0)
        == t * 20 + lax.broadcasted_iota(jnp.int32, (ROWS, 32), 1)
    ) & (lax.broadcasted_iota(jnp.int32, (ROWS, 32), 1) < 20)
    pick = pick.astype(F32).astype(BF16)

    def partial(pyh, pz, half):
        cols = pl.ds(pl.multiple_of((pyh * 4 + pz) * 512 + half * 256, 256), 256)
        return dot_nn(u, w[:, cols]) + dot_nn(pick, negb[:, cols].astype(BF16))

    for dz in range(4):
        part_b[dz] = partial(1 - yh, ring(z, dz), 1).astype(BF16)
    halves = [slice(0, 80), slice(80, 160)]

    def stage(name, key, src, dst, send, recv, dev):
        copy = remote(src, dst, send.at[key], recv.at[key], dev)
        launch(copy)
        owed[(name,) + key] = copy.wait_recv

    def send_b(hf):
        rows = halves[hf]
        stage("rsb", (hf,), part_b.at[:, rows], rx_b.at[:, rows], rsb_send, rsb_recv, tp_dev(1 - yh, z))

    send_b(0)

    for dz in far:
        for e in range(2):
            part_a[dz, e] = partial(yh if e == 0 else 1 - yh, ring(z, dz), 0).astype(BF16)

    def send_a(hf):
        rows = halves[hf]
        for dz in far:
            dev = tp_dev(yh, ring(z, dz))
            stage("rsa", (hf, dz), part_a.at[dz, :, rows], rx_a.at[dz, :, rows], rsa_send, rsa_recv, dev)

    send_a(0)
    send_b(1)
    send_a(1)

    local_copy(at_own, at_view(y, x), atx_recv).start()
    for dx in far:
        launch(remote(at_own, at_view(y, x), atx_send.at[0, dx], atx_recv, seq_dev(ring(x, dx), y, c)))
    owed["atx"] = lambda: wait_for(at.at[y, c], atx_recv)

    for dz in range(4):
        sum_b[dz] = partial(yh, ring(z, dz), 1)
    for e in range(2):
        sum_a[e] = partial(yh if e == 0 else 1 - yh, z, 0)


    def cot_copy(a, src, dst, dev, hf):
        rows = halves[hf]
        sem = (a,) + dst + (hf,)
        stage("t", sem, cot.at[(a,) + src + (rows,)], cot.at[(a,) + dst + (rows,)], t_send, t_recv, dev)

    for hf in range(2):
        rows = halves[hf]
        due(("rsb", hf))
        for dz in far:
            part_b2[dz, rows] = (sum_b[dz, rows] + rx_b[dz, rows].astype(F32)).astype(BF16)
            dev = tp_dev(yh, ring(z, dz))
            stage("rsb2", (hf, dz), part_b2.at[dz, rows], rx_b2.at[dz, rows], rsb2_send, rsb2_recv, dev)
        other = sum_a[1, rows]
        for dz in far:
            due(("rsa", hf, dz))
            other = other + rx_a[dz, 1, rows].astype(F32)
        part_a2[rows] = other.astype(BF16)
        stage("rsa2", (hf,), part_a2.at[rows], rx_a2.at[rows], rsa2_send, rsa2_recv, tp_dev(1 - yh, z))

    sq = jnp.zeros((1, 256), F32)
    for hf in range(2):
        rows = halves[hf]
        cot_a = sum_a[0, rows]
        for dz in far:
            cot_a = cot_a + rx_a[dz, 0, rows].astype(F32)
        due(("rsa2", hf))
        cot_a = cot_a + rx_a2[rows].astype(F32)
        cot[0, 0, 0, rows] = cot_a.astype(BF16)
        for dz in far:
            cot_copy(0, (0, 0), (0, dz), tp_dev(yh, ring(z, dz)), hf)
        cot_b = sum_b[0, rows] + rx_b[0, rows].astype(F32)
        for dz in far:
            due(("rsb2", hf, dz))
            cot_b = cot_b + rx_b2[dz, rows].astype(F32)
        cot[1, 0, 0, rows] = cot_b.astype(BF16)
        cot_copy(1, (0, 0), (1, 0), tp_dev(1 - yh, z), hf)
        for dz in far:
            cot_copy(1, (0, 0), (0, dz), tp_dev(yh, ring(z, dz)), hf)
        cot_copy(0, (0, 0), (1, 0), tp_dev(1 - yh, z), hf)
        sq = sq + jnp.sum(cot_a * cot_a + cot_b * cot_b, axis=0, keepdims=True)

    def sq_copy(buf, d, send, recv, dev, name):
        copy = remote(buf.at[0], buf.at[d], send.at[d], recv.at[d], dev)
        launch(copy)
        owed[name, d] = copy.wait_recv

    sq_tp[0] = jnp.zeros((8, 128), F32) + jnp.sum(sq, axis=1, keepdims=True)
    for d in range(1, 8):
        sq_copy(sq_tp, d, sqt_send, sqt_recv, (s, lax.rem(t + d, 8)), "sqt")

    at_pass_on()

    def grad_part(a, dyh, dz):
        pyh = lax.rem(yh + dyh, 2)
        pz = lax.rem(z + 4 - dz, 4)
        cols = pl.ds(pl.multiple_of((pyh * 4 + pz) * 512 + a * 256, 256), 256)
        return dot_nt(cot[a, dyh, dz], w[:, cols])

    grad = grad_part(0, 0, 0) + grad_part(1, 0, 0)
    for hf in range(2):
        due(("t", 1, 1, 0, hf))
        for dz in far:
            cot_copy(1, (1, 0), (1, dz), tp_dev(yh, ring(z, dz)), hf)
        for dz in (1, 3, 2):
            due(("t", 0, 0, dz, hf))
            cot_copy(0, (0, dz), (1, dz), tp_dev(1 - yh, z), hf)
    grad = grad + grad_part(1, 1, 0)
    for dz in (1, 3, 2):
        grad = grad + grad_part(0, 0, dz)
        due(("t", 1, 0, dz, 0))
        due(("t", 1, 0, dz, 1))
        grad = grad + grad_part(1, 0, dz)
    for a, dz in ((0, 0), (0, 1), (0, 3), (0, 2), (1, 1), (1, 3), (1, 2)):
        due(("t", a, 1, dz, 0))
        due(("t", a, 1, dz, 1))
        grad = grad + grad_part(a, 1, dz)
    g_tx[...] = grad.astype(BF16)

    def g_moves(act):
        to_heads(lambda hx: g_tx.at[:, lanes(hx, HD)], g.at[unit, c], g_send, g_recv, 0, act)

    g_moves("start")
    owed["g"] = lambda: wait_for(g, g_recv)
    pending.append(lambda: g_moves("wait"))

    row_half = pl.ds(pl.multiple_of(80 * (z % 2), 16), 80)
    chip_slot = y * 4 + home * 2 + unit

    def tw_source(dest):
        tt = dest // 2
        dyh = lax.rem(yh + tt // 4, 2)
        dz = lax.rem(z + 4 - tt % 4, 4)
        return cot.at[dest % 2, dyh, dz]

    def tw_send_all(act):
        for dx in (2, 1, 3, 0):
            for pc in range(2):
                dest, _ = seq_dev(ring(x, dx), 1 - y, pc)
                copy = remote(
                    tw_source(dest).at[row_half, lanes(yh, HD)],
                    tw_part.at[home * 2 + unit],
                    tw_send.at[dx, pc],
                    tw_recv,
                    (dest, t),
                )
                copy.start() if act == "start" else copy.wait_send()

    def tw_turn(act):
        @pl.when(c == z // 2)
        def _():
            tw_send_all(act)

    tw_turn("start")
    for dx in (2, 1, 3, 0):
        for e in range(2):
            dest, _ = seq_dev(ring(x, dx), y, c if e == 0 else 1 - c)
            if dx or e:
                launch(remote(tw_source(dest), tw.at[chip_slot, c], twd_send.at[dx, e], twd_recv, (dest, t)))
            else:
                local_copy(tw_source(s), tw.at[chip_slot, c], twd_recv).start()
    owed["twd"] = lambda: wait_for(tw.at[pl.ds(y * 4, 4)], twd_recv)
    owed["tw"] = lambda: wait_for(tw_part, tw_recv)
    pending.append(lambda: tw_turn("wait"))

    due("tw")

    def tw_view(dyh, dz):
        pyh = lax.rem(yh + dyh, 2)
        pz = lax.rem(z + 4 - dz, 4)
        rows = pl.ds(pl.multiple_of(80 * (pz % 2), 16), 80)
        return tw.at[pl.ds((1 - y) * 4, 4), pz // 2, rows, lanes(pyh, HD)]

    def twg_copy(origin, slot, dev):
        view = tw_view(*origin)
        src = tw_part if origin == (0, 0) else view
        stage("twg", slot, src, view, twg_send, twg_recv, dev)

    twg_copy((0, 0), (1, 0), tp_dev(1 - yh, z))
    local_copy(tw_part, tw_view(0, 0), twg_recv.at[0, 0]).start()
    owed["twg", 0, 0] = lambda: wait_for(tw_view(0, 0), twg_recv.at[0, 0])
    for dz in far:
        twg_copy((0, 0), (0, dz), tp_dev(yh, ring(z, dz)))

    def tw_pass_on():
        due(("twg", 1, 0))
        for dz in far:
            twg_copy((1, 0), (1, dz), tp_dev(yh, ring(z, dz)))

    due("g")
    gt = g[...].reshape(NQ, HD).astype(F32).T
    dterm = jnp.sum(gt * at_own[...].astype(F32), axis=0, keepdims=True)
    dqt[...] = jnp.zeros_like(dqt)

    def back(i, lo):
        gq = g[...].reshape(NQ, HD)[lo:]
        queries = qq[...].reshape(NQ, 2 * HD)[lo:, HD:]
        keys = chunk(kk, i)[:, :HD]
        vals = chunk(vv, i)[:, :HD]
        ph = p16[i, :, lo:]
        dp = dot_nt(vals, gq)
        ds = (ph.astype(F32) * (dp - dterm[:, lo:])).astype(BF16)
        dkv[1, i] = dot_nn(ph, gq).astype(BF16).reshape(2, ROWS, HD)
        dkv[0, i] = (dot_nn(ds, queries) * SCALE).astype(BF16).reshape(2, ROWS, HD)
        dqt[:, lo:] += dot_tn(keys, ds)

    def sib_copy(i):
        return remote(
            dkv.at[:, i, 1 - c], sib_rx.at[:, i], sib_send.at[i], sib_recv.at[i], (sibling, t)
        )

    def dkv_copy(i):
        return remote(
            dkv_tx.at[:, i], dkv_rx.at[m], dkv_send.at[i], dkv_recv.at[m], seq_dev(i // 2, i % 2, c)
        )

    def both_cores(i):
        sib_copy(i).wait_recv()
        return dkv[:, i, c].astype(F32) + sib_rx[:, i].astype(F32)

    def back_step(k, state):
        i = lax.rem(m + 1 + k, 8)

        @pl.when(i < n0)
        def _():
            back(i, 0)

        @pl.when((i >= n0) & (i < n1))
        def _():
            back(i, 256)

        @pl.when(i >= n1)
        def _():
            dkv[:, i] = jnp.zeros((2, 2, ROWS, HD), BF16)

        sib_copy(i).start()

        @pl.when(k > 0)
        def _():
            done = lax.rem(m + k, 8)
            dkv_tx[:, done] = both_cores(done).astype(BF16)
            dkv_copy(done).start()

        return state

    lax.fori_loop(0, 5, back_step, 0)
    tw_pass_on()
    sqv = sq_tp[0]
    for d in range(1, 8):
        due(("sqt", d))
        sqv = sqv + sq_tp[d]
    sq_seq[0] = sqv
    for d in range(1, 16):
        sq_copy(sq_seq, d, sqs_send, sqs_recv, (lax.rem(s + d, 16), t), "sqs")

    lax.fori_loop(5, 8, back_step, 0)
    dq_tx[...] = (dqt[...] * SCALE).T.astype(BF16).reshape(2, 2, ROWS, HD)
    to_owners(dq_tx, dq_rx.at[:, lanes(head, HD)], dq_send, dq_recv, "start")
    owed["dq"] = lambda: wait_for(dq_rx, dq_recv)
    pending.append(lambda: to_owners(dq_tx, dq_rx.at[:, lanes(head, HD)], dq_send, dq_recv, "wait"))
    dkv_rx[m] = both_cores(m).astype(BF16)

    due("atx")
    due("at2")
    atf = remote(at.at[:, c], at.at[:, c], atf_send, atf_recv, (sibling, t))
    launch(atf)
    owed["atf"] = atf.wait_recv
    for dyh in range(2):
        for dz in range(4):
            if (dyh, dz) != (1, 0):
                due(("twg", dyh, dz))
    due("twd")
    due("atf")

    gw = jnp.zeros((512, 256), F32)
    for a in range(4):
        rows = tw[2 * a : 2 * a + 2].reshape(NQ, 256)
        gw = gw + dot_nn(at[a // 2, a % 2], rows)
    gw_out[...] = gw

    sqv = sq_seq[0]
    for d in range(1, 16):
        due(("sqs", d))
        sqv = sqv + sq_seq[d]
    ms_out[...] = sqv

    due("dq")
    dq_out[...] = dq_rx[...]

    def all_dkv(k, state):
        i = lax.rem(m + 1 + k, 8)
        sib_copy(i).wait_send()

        @pl.when(k < 7)
        def _():
            dkv_copy(i).wait_send()
            remote(dkv_tx.at[:, i], dkv_rx.at[i], dkv_send.at[i], dkv_recv.at[i], (sibling, t)).wait_recv()

        return state

    lax.fori_loop(0, 8, all_dkv, 0)
    for h in range(4):
        for a, out in enumerate((dk_out, dv_out)):
            out[:, h * HD : (h + 1) * HD] = dkv_rx[2 * h, a].astype(F32) + dkv_rx[2 * h + 1, a].astype(F32)
    finish()


def scaled(ms_ref, *refs):
    scale = lax.rsqrt(ms_ref[0:1, 0:1] / (2560 * 4096) + 1e-05)
    for src, dst in zip(refs[:4], refs[4:]):
        dst[...] = (src[...].astype(F32) * scale).astype(BF16)


def on_device(q, k, v, qd, kd, vd, w, noisy, vel, time_index, frame_lengths):
    smem = pl.BlockSpec(memory_space=pltpu.SMEM)
    vmem = pl.BlockSpec(memory_space=pltpu.VMEM)
    hbm = pl.BlockSpec(memory_space=pl.ANY)
    dma = pltpu.SemaphoreType.DMA
    scratch = [
        pltpu.VMEM((512, 4096), BF16),
        pltpu.VMEM((4, 2, 2, ROWS, 256), BF16),
        pltpu.VMEM((4, 2, 2, ROWS, 256), BF16),
        pltpu.VMEM((2, 2, ROWS, 256), BF16),
        pltpu.VMEM((8, UNIT, NQ), F32),
        pltpu.VMEM((8, UNIT, NQ), F32),
        pltpu.VMEM((8, UNIT, NQ), BF16),
        pltpu.VMEM((2 * HD, NQ), F32),
        pltpu.VMEM((HD, NQ), F32),
        pltpu.VMEM((2, 2, ROWS, HD), BF16),
        pltpu.VMEM((ROWS, 512), BF16),
        pltpu.VMEM((HD, NQ), BF16),
        pltpu.VMEM((2, 2, 512, NQ), BF16),
        pltpu.VMEM((32, 4096), F32),
        pltpu.VMEM((2, 20, 4096), BF16),
        dma((2,)),
        pltpu.VMEM((4, 2, ROWS, 256), BF16),
        pltpu.VMEM((4, ROWS, 256), BF16),
        pltpu.VMEM((4, 2, ROWS, 256), BF16),
        pltpu.VMEM((4, ROWS, 256), BF16),
        pltpu.VMEM((2, ROWS, 256), F32),
        pltpu.VMEM((4, ROWS, 256), F32),
        pltpu.VMEM((ROWS, 256), BF16),
        pltpu.VMEM((4, ROWS, 256), BF16),
        pltpu.VMEM((ROWS, 256), BF16),
        pltpu.VMEM((4, ROWS, 256), BF16),
        pltpu.VMEM((2, 2, 4, ROWS, 256), BF16),
        pltpu.VMEM((ROWS, 512), BF16),
        pltpu.VMEM((2, 2, ROWS, HD), BF16),
        pltpu.VMEM((HD, NQ), F32),
        pltpu.VMEM((2, 2, ROWS, HD), BF16),
        pltpu.VMEM((ROWS, 512), BF16),
        pltpu.VMEM((2, 8, 2, ROWS, HD), BF16),
        pltpu.VMEM((2, 8, ROWS, HD), BF16),
        pltpu.VMEM((2, 8, ROWS, HD), BF16),
        pltpu.VMEM((8, 2, ROWS, HD), BF16),
        pltpu.VMEM((4, 80, HD), BF16),
        pltpu.VMEM((8, 2, ROWS, 256), BF16),
        pltpu.VMEM((8, 8, 128), F32),
        pltpu.VMEM((16, 8, 128), F32),
        dma,
        dma((4, 4)),
        dma((4,)),
        dma((4, 4)),
        dma((4,)),
        dma((4,)),
        dma((4,)),
        dma((4,)),
        dma((4,)),
        dma((2, 4)),
        dma((2,)),
        dma((2, 2)),
        dma,
        dma((2, 4)),
        dma,
        dma,
        dma,
        dma,
        dma,
        dma,
        dma((2, 4)),
        dma((2, 4)),
        dma((2,)),
        dma((2,)),
        dma((2,)),
        dma((2,)),
        dma((2, 4)),
        dma((2, 4)),
        dma((2, 2, 4, 2)),
        dma((2, 2, 4, 2)),
        dma((1, 4)),
        dma,
        dma((4, 2)),
        dma((4, 2)),
        dma,
        dma,
        dma((2, 4)),
        dma((2, 4)),
        dma((2, 2)),
        dma,
        dma((8,)),
        dma((8,)),
        dma((8,)),
        dma((8,)),
        dma((8,)),
        dma((8,)),
        dma((16,)),
        dma((16,)),
    ]
    dq, dk, dv, gw, ms = pl.pallas_call(
        kernel,
        out_shape=(
            jax.ShapeDtypeStruct((ROWS, 512), BF16),
            jax.ShapeDtypeStruct((ROWS, 512), F32),
            jax.ShapeDtypeStruct((ROWS, 512), F32),
            jax.ShapeDtypeStruct((512, 256), F32),
            jax.ShapeDtypeStruct((8, 128), F32),
        ),
        in_specs=[smem, smem] + [hbm] * 9,
        out_specs=(vmem,) * 5,
        scratch_shapes=scratch,
        compiler_params=pltpu.CompilerParams(
            collective_id=0, has_side_effects=True, vmem_limit_bytes=56 * 1024 * 1024
        ),
        cost_estimate=pl.CostEstimate(flops=7 * 10**9, bytes_accessed=8 * 10**6, transcendentals=1638400),
    )(frame_lengths, time_index, q, k, v, qd, kd, vd, w, noisy, vel)
    return pl.pallas_call(
        scaled,
        out_shape=tuple(jax.ShapeDtypeStruct(part.shape, BF16) for part in (dq, dk, dv, gw)),
        in_specs=[vmem] * 5,
        out_specs=(vmem,) * 4,
    )(ms, dq, dk, dv, gw)


def solution(mesh):
    in_specs = (P("seq", "tp"),) * 6 + (P("tp", None), P(("seq", "tp"), None), P(("seq", "tp"), None), P(), P())
    out_specs = (P("seq", "tp"), P("seq", "tp"), P("seq", "tp"), P("tp", "seq"))
    return jax.shard_map(
        on_device, mesh=mesh, in_specs=in_specs, out_specs=out_specs, check_vma=False
    )
```

```python
import math

import jax
import jax.numpy as jnp
from jax import lax
from jax.experimental import pallas as pl
from jax.experimental.pallas import tpu as pltpu
from jax.sharding import PartitionSpec as P

HD = 128
TSTEPS = 64
FRAMES = 16
ROWS = 160
UNIT = 320
NCHIP = 8
NQ = 640
CUTS = (0, 80, 160)
SCALE = 1.0 / math.sqrt(HD)
MESH = pl.DeviceIdType.MESH
F32 = jnp.float32
BF16 = jnp.bfloat16


def dot_nt(a, b):
    return lax.dot_general(a, b, (((1,), (1,)), ((), ())), preferred_element_type=F32)


def dot_nn(a, b):
    return lax.dot_general(a, b, (((1,), (0,)), ((), ())), preferred_element_type=F32)


def dot_tn(a, b):
    return lax.dot_general(a, b, (((0,), (0,)), ((), ())), preferred_element_type=F32)


def kernel(
    frame_ref,
    time_ref,
    q_ref,
    k_ref,
    v_ref,
    qd_ref,
    kd_ref,
    vd_ref,
    w_hbm,
    noisy_ref,
    vel_ref,
    dq_out,
    dk_out,
    dv_out,
    gw_out,
    ms_out,
    w,
    kk,
    vv,
    qq,
    sbuf,
    stbuf,
    p16,
    acc1,
    acc2,
    ublk,
    uown,
    at_own,
    at,
    negb,
    lat,
    lat_sem,
    part_a,
    part_b,
    rx_a,
    rx_b,
    sum_a,
    sum_b,
    part_a2,
    part_b2,
    rx_a2,
    rx_b2,
    cot,
    g_tx,
    g,
    dqt,
    dq_tx,
    dq_rx,
    dkv,
    sib_rx,
    dkv_tx,
    dkv_rx,
    tw_part,
    tw,
    sq_tp,
    sq_seq,
    wsem,
    kvx_send,
    kvx_recv,
    kvy_send,
    kvy_recv,
    fwx_send,
    fwx_recv,
    fwy_send,
    fwy_recv,
    q_send,
    q_recv,
    u_send,
    u_recv,
    atx_send,
    atx_recv,
    aty_send,
    aty_recv,
    at2_recv,
    atf_send,
    atf_recv,
    rsa_send,
    rsa_recv,
    rsb_send,
    rsb_recv,
    rsa2_send,
    rsa2_recv,
    rsb2_send,
    rsb2_recv,
    t_send,
    t_recv,
    g_send,
    g_recv,
    tw_send,
    twd_send,
    twd_recv,
    tw_recv,
    twg_send,
    twg_recv,
    dq_send,
    dq_recv,
    sib_send,
    sib_recv,
    dkv_send,
    dkv_recv,
    sqt_send,
    sqt_recv,
    sqs_send,
    sqs_recv,
):
    s = lax.axis_index("seq")
    t = lax.axis_index("tp")
    x = s // 4
    y = (s // 2) % 2
    c = s % 2
    m = s // 2
    yh = t // 4
    z = t % 4
    head = x
    far = (2, 1, 3)

    def ring(pos, step):
        return lax.rem(pos + step, 4)

    def seq_dev(px, py, pc):
        return (px * 4 + py * 2 + pc, t)

    def tp_dev(pyh, pz):
        return (s, pyh * 4 + pz)

    def local_copy(src, dst, sem):
        return pltpu.make_async_copy(src, dst, sem)

    def remote(src, dst, ssem, rsem, dev):
        return pltpu.make_async_remote_copy(
            src_ref=src, dst_ref=dst, send_sem=ssem, recv_sem=rsem, device_id=dev, device_id_type=MESH
        )

    def lanes(index, width):
        return pl.ds(pl.multiple_of(index * width, width), width)

    def wait_for(ref, sem):
        pltpu.make_async_copy(ref, ref, sem).wait()

    pending = []

    def launch(copy):
        copy.start()
        pending.append(copy.wait_send)

    owed = {}

    def due(name):
        owed.pop(name)()

    def finish():
        for name in list(owed):
            due(name)
        for wait in pending:
            wait()

    wload = pltpu.make_async_copy(w_hbm, w, wsem)
    wload.start()
    lat_loads = [pltpu.make_async_copy(ref, lat.at[i], lat_sem.at[i]) for i, ref in enumerate((noisy_ref, vel_ref))]
    for i, load in enumerate(lat_loads):
        load.start()
        owed["lat", i] = load.wait
    owed["w"] = wload.wait

    barrier = pltpu.get_barrier_semaphore()
    sibling = s + 1 - 2 * c
    partners = [seq_dev(x, 1 - y, c), (sibling, t), tp_dev(1 - yh, z)]
    for dx in far:
        partners += [seq_dev(ring(x, dx), y, c), seq_dev(ring(x, dx), y, 1 - c), tp_dev(yh, ring(z, dx))]
    for dev in partners:
        pl.semaphore_signal(barrier, inc=1, device_id=dev, device_id_type=MESH)
    pl.semaphore_wait(barrier, len(partners))

    kv_src = (k_ref, kd_ref, v_ref, vd_ref)
    kv_dst = ((kk, 0), (kk, 1), (vv, 0), (vv, 1))

    def kv_view(a, px, py, pc):
        buf, half = kv_dst[a]
        return buf.at[px, py, pc, :, half * HD : (half + 1) * HD]

    def kv_piece(a, px):
        return kv_src[a].at[:, lanes(px, HD)]

    def kv_all(a, py, pc):
        return kv_view(a, slice(None), py, pc)

    def kv_own(a):
        local_copy(kv_piece(a, x), kv_view(a, x, y, c), kvx_recv.at[a]).start()
        launch(
            remote(
                kv_piece(a, x), kv_view(a, x, y, c), kvy_send.at[a, 0], kvy_recv.at[a], seq_dev(x, 1 - y, c)
            )
        )

    def kv_along_x(a):
        for dx in far:
            hx = ring(x, dx)
            launch(
                remote(
                    kv_piece(a, hx), kv_view(a, x, y, c), kvx_send.at[a, dx], kvx_recv.at[a], seq_dev(hx, y, c)
                )
            )
        owed["kvx", a] = lambda: wait_for(kv_all(a, y, c), kvx_recv.at[a])
        owed["kvy", a] = lambda: wait_for(kv_all(a, 1 - y, c), kvy_recv.at[a])

    def kv_across(a):
        due(("kvx", a))
        for dx in far:
            view = kv_view(a, ring(x, dx), y, c)
            launch(remote(view, view, kvy_send.at[a, dx], kvy_recv.at[a], seq_dev(x, 1 - y, c)))
        to_sibling(a, y, fwx_send, fwx_recv, "fwx")

    def to_sibling(a, py, send, recv, name):
        view = kv_all(a, py, c)
        launch(remote(view, view, send.at[a], recv.at[a], (sibling, t)))
        owed[name, a] = lambda: wait_for(kv_all(a, py, 1 - c), recv.at[a])

    def kv_received(a):
        due(("kvy", a))
        to_sibling(a, 1 - y, fwy_send, fwy_recv, "fwy")

    def kv_complete(a):
        due(("fwx", a))
        due(("fwy", a))

    home = jnp.where((x == 1) | (x == 2), 1, 0)
    unit = x // 2

    def to_heads(src_of, dst, send, recv, slot, act):
        for dx in (2, 1, 3, 0):
            hx = ring(x, dx)
            if dx:
                copy = remote(src_of(hx), dst, send.at[slot, dx], recv, seq_dev(hx, y, home))
                copy.start() if act == "start" else copy.wait_send()
            else:

                @pl.when(home != c)
                def _():
                    copy = remote(src_of(hx), dst, send.at[slot, dx], recv, seq_dev(hx, y, home))
                    copy.start() if act == "start" else copy.wait_send()

                if act == "start":

                    @pl.when(home == c)
                    def _():
                        local_copy(src_of(hx), dst, recv).start()

    def to_owners(src, dst, send, recv, act):
        for u in range(2):
            ux = c if u == 0 else 3 - c
            for core in range(2):
                dev = ux * 4 + y * 2 + core

                @pl.when(dev != s)
                def _():
                    copy = remote(src.at[u, core], dst, send.at[u, core], recv, (dev, t))
                    copy.start() if act == "start" else copy.wait_send()

                if act == "start":

                    @pl.when(dev == s)
                    def _():
                        local_copy(src.at[u, core], dst, recv).start()

    def q_moves(act, which=(1, 0)):
        for a in which:
            ref = (qd_ref, q_ref)[a]
            to_heads(
                lambda hx, ref=ref: ref.at[:, lanes(hx, HD)],
                qq.at[unit, c, :, a * HD : (a + 1) * HD],
                q_send,
                q_recv.at[a],
                a,
                act,
            )

    kv_along_x(0)
    for a in range(4):
        kv_own(a)
    kv_along_x(1)
    q_moves("start", (1,))
    kv_along_x(2)
    q_moves("start", (0,))
    pending.append(lambda: q_moves("wait"))
    for a in range(2):
        owed["q", a] = lambda a=a: wait_for(qq.at[:, :, :, a * HD : (a + 1) * HD], q_recv.at[a])
    kv_along_x(3)

    ends = []
    total = 0
    for f in range(FRAMES):
        total = total + frame_ref[f]
        ends.append(total)
    times = [time_ref[f] for f in range(FRAMES)]

    def frame_facts(pos):
        kend = jnp.zeros(pos.shape, jnp.int32) + ends[FRAMES - 1]
        level = jnp.zeros(pos.shape, jnp.int32) + times[FRAMES - 1]
        for f in range(FRAMES - 2, -1, -1):
            inside = pos < ends[f]
            kend = jnp.where(inside, ends[f], kend)
            level = jnp.where(inside, times[f], level)
        angle = (level.astype(F32) + 0.5) * (math.pi / (2 * TSTEPS))
        return kend, jnp.cos(angle), jnp.sin(angle)

    lane = lax.broadcasted_iota(jnp.int32, (1, NQ), 1)
    chip0 = 2 * c + y
    chip1 = 2 * (3 - c) + y
    qpos = jnp.where(lane < UNIT, UNIT * chip0 + lane, UNIT * chip1 + lane - UNIT)
    kend, cosq, sinq = frame_facts(qpos)

    rpos = s * ROWS + t * 20 + lax.broadcasted_iota(jnp.int32, (20, 1), 0)
    _, cosr, sinr = frame_facts(rpos)
    for i in range(2):
        due(("lat", i))
    negb[...] = jnp.zeros_like(negb)
    negb[0:20, :] = sinr * cosr * lat[0].astype(F32) - cosr * cosr * lat[1].astype(F32)

    n0 = chip0 + 2
    n1 = jnp.minimum(chip1 + 2, 8)

    def over_keys(body, carry, between=None):
        carry = lax.fori_loop(0, n0, lambda i, st: body(i, st, 0), carry)
        if between is not None:
            between()
        return lax.fori_loop(n0, n1, lambda i, st: body(i, st, 256), carry)

    def put(row, lo, part_row):
        if lo == 0:
            return part_row
        return jnp.concatenate([row[:, :lo], part_row], axis=1)

    kv_across(0)
    kv_across(1)
    kv_across(2)
    kv_received(0)
    due(("q", 1))
    kv_complete(0)

    def chunk(buf, i):
        return buf[i // 2, i % 2].reshape(UNIT, buf.shape[-1])

    def pass1(i, top, lo):
        keys = kk[i // 2, i % 2, :, :, :HD].reshape(UNIT, HD)
        queries = qq[:, :, :, HD:].reshape(NQ, HD)[lo:]
        sc = dot_nt(keys, queries) * SCALE
        kpos = i * UNIT + lax.broadcasted_iota(jnp.int32, (UNIT, 1), 0)
        sc = jnp.where(kpos < kend[:, lo:], sc, -1e30)
        sbuf[i, :, lo:] = sc
        return put(top, lo, jnp.maximum(top[:, lo:], jnp.max(sc, axis=0, keepdims=True)))

    top = over_keys(pass1, jnp.full((1, NQ), -1e30, F32))

    kv_received(1)
    due(("q", 0))
    kv_across(3)
    kv_complete(1)

    def pass2(i, state, lo):
        den, tan = state
        st = dot_nt(chunk(kk, i), qq[...].reshape(NQ, 2 * HD)[lo:]) * SCALE
        p = jnp.exp(sbuf[i, :, lo:] - top[:, lo:])
        sbuf[i, :, lo:] = p
        stbuf[i, :, lo:] = st
        den = put(den, lo, den[:, lo:] + jnp.sum(p, axis=0, keepdims=True))
        tan = put(tan, lo, tan[:, lo:] + jnp.sum(p * st, axis=0, keepdims=True))
        return den, tan

    row0 = jnp.zeros((1, NQ), F32)
    den, tan = over_keys(pass2, (row0, row0), lambda: kv_received(2))
    inv = 1.0 / den
    mean = tan * inv
    kv_complete(2)

    acc2[...] = jnp.zeros_like(acc2)

    def pass3(i, state, lo):
        p = sbuf[i, :, lo:] * inv[:, lo:]
        p16[i, :, lo:] = p.astype(BF16)
        ds = (p * (stbuf[i, :, lo:] - mean[:, lo:])).astype(BF16)
        vals = vv[i // 2, i % 2, :, :, :HD].reshape(UNIT, HD)
        acc2[:, lo:] += dot_tn(vals, ds)
        return state

    over_keys(pass3, 0, lambda: kv_received(3))
    kv_complete(3)
    acc1[...] = jnp.zeros_like(acc1)

    def pass4(i, state, lo):
        acc1[:, lo:] += dot_tn(chunk(vv, i), p16[i, :, lo:])
        return state

    over_keys(pass4, 0)
    attn_t = acc1[0:HD].astype(BF16)
    tan_t = (acc2[...] + acc1[HD:]).astype(BF16)
    at_own[...] = attn_t
    u_t = (0.5 * cosq) * (cosq * attn_t.astype(F32) + sinq * tan_t.astype(F32))
    ublk[...] = u_t.T.astype(BF16).reshape(2, 2, ROWS, HD)
    to_owners(ublk, uown.at[:, lanes(head, HD)], u_send, u_recv, "start")
    owed["u"] = lambda: wait_for(uown, u_recv)
    pending.append(lambda: to_owners(ublk, uown.at[:, lanes(head, HD)], u_send, u_recv, "wait"))

    def at_view(py, hx):
        return at.at[py, c, lanes(hx, HD), :]

    launch(remote(at_own, at_view(y, x), aty_send, aty_recv, seq_dev(x, 1 - y, c)))
    owed["aty"] = lambda: wait_for(at_view(1 - y, x), aty_recv)

    def at_pass_on():
        due("aty")
        for dx in far:
            view = at_view(1 - y, x)
            launch(remote(view, view, atx_send.at[1, dx], at2_recv, seq_dev(ring(x, dx), y, c)))
        owed["at2"] = lambda: wait_for(at.at[1 - y, c, 0 : 3 * HD], at2_recv)

    due("w")
    due("u")
    u = uown[...]
    pick = (
        lax.broadcasted_iota(jnp.int32, (ROWS, 32), 0)
        == t * 20 + lax.broadcasted_iota(jnp.int32, (ROWS, 32), 1)
    ) & (lax.broadcasted_iota(jnp.int32, (ROWS, 32), 1) < 20)
    pick = pick.astype(F32).astype(BF16)

    def partial(pyh, pz, half):
        cols = pl.ds(pl.multiple_of((pyh * 4 + pz) * 512 + half * 256, 256), 256)
        return dot_nn(u, w[:, cols]) + dot_nn(pick, negb[:, cols].astype(BF16))

    for dz in range(4):
        part_b[dz] = partial(1 - yh, ring(z, dz), 1).astype(BF16)
    halves = [slice(lo, hi) for lo, hi in zip(CUTS[:-1], CUTS[1:])]
    pieces = range(len(halves))

    def stage(name, key, src, dst, send, recv, dev):
        copy = remote(src, dst, send.at[key], recv.at[key], dev)
        launch(copy)
        owed[(name,) + key] = copy.wait_recv

    def send_b(hf):
        rows = halves[hf]
        stage("rsb", (hf,), part_b.at[:, rows], rx_b.at[:, rows], rsb_send, rsb_recv, tp_dev(1 - yh, z))

    send_b(0)

    for dz in far:
        for e in range(2):
            part_a[dz, e] = partial(yh if e == 0 else 1 - yh, ring(z, dz), 0).astype(BF16)

    def send_a(hf):
        rows = halves[hf]
        for dz in far:
            dev = tp_dev(yh, ring(z, dz))
            stage("rsa", (hf, dz), part_a.at[dz, :, rows], rx_a.at[dz, :, rows], rsa_send, rsa_recv, dev)

    send_a(0)
    for hf in pieces[1:]:
        send_b(hf)
        send_a(hf)

    local_copy(at_own, at_view(y, x), atx_recv).start()
    for dx in far:
        launch(remote(at_own, at_view(y, x), atx_send.at[0, dx], atx_recv, seq_dev(ring(x, dx), y, c)))
    owed["atx"] = lambda: wait_for(at.at[y, c], atx_recv)

    at_pass_on()

    for dz in range(4):
        sum_b[dz] = partial(yh, ring(z, dz), 1)
    for e in range(2):
        sum_a[e] = partial(yh if e == 0 else 1 - yh, z, 0)


    def cot_copy(a, src, dst, dev, hf):
        rows = halves[hf]
        sem = (a,) + dst + (hf,)
        stage("t", sem, cot.at[(a,) + src + (rows,)], cot.at[(a,) + dst + (rows,)], t_send, t_recv, dev)

    for hf in pieces:
        rows = halves[hf]
        due(("rsb", hf))
        for dz in far:
            part_b2[dz, rows] = (sum_b[dz, rows] + rx_b[dz, rows].astype(F32)).astype(BF16)
            dev = tp_dev(yh, ring(z, dz))
            stage("rsb2", (hf, dz), part_b2.at[dz, rows], rx_b2.at[dz, rows], rsb2_send, rsb2_recv, dev)
        other = sum_a[1, rows]
        for dz in far:
            due(("rsa", hf, dz))
            other = other + rx_a[dz, 1, rows].astype(F32)
        part_a2[rows] = other.astype(BF16)
        stage("rsa2", (hf,), part_a2.at[rows], rx_a2.at[rows], rsa2_send, rsa2_recv, tp_dev(1 - yh, z))

    sq = jnp.zeros((1, 256), F32)
    for hf in pieces:
        rows = halves[hf]
        cot_a = sum_a[0, rows]
        for dz in far:
            cot_a = cot_a + rx_a[dz, 0, rows].astype(F32)
        due(("rsa2", hf))
        cot_a = cot_a + rx_a2[rows].astype(F32)
        cot[0, 0, 0, rows] = cot_a.astype(BF16)
        for dz in far:
            cot_copy(0, (0, 0), (0, dz), tp_dev(yh, ring(z, dz)), hf)
        cot_b = sum_b[0, rows] + rx_b[0, rows].astype(F32)
        for dz in far:
            due(("rsb2", hf, dz))
            cot_b = cot_b + rx_b2[dz, rows].astype(F32)
        cot[1, 0, 0, rows] = cot_b.astype(BF16)
        cot_copy(1, (0, 0), (1, 0), tp_dev(1 - yh, z), hf)
        for dz in far:
            cot_copy(1, (0, 0), (0, dz), tp_dev(yh, ring(z, dz)), hf)
        cot_copy(0, (0, 0), (1, 0), tp_dev(1 - yh, z), hf)
        sq = sq + jnp.sum(cot_a * cot_a + cot_b * cot_b, axis=0, keepdims=True)

    def sq_copy(buf, d, send, recv, dev, name):
        copy = remote(buf.at[0], buf.at[d], send.at[d], recv.at[d], dev)
        launch(copy)
        owed[name, d] = copy.wait_recv

    sq_tp[0] = jnp.zeros((8, 128), F32) + jnp.sum(sq, axis=1, keepdims=True)
    for d in range(1, 8):
        sq_copy(sq_tp, d, sqt_send, sqt_recv, (s, lax.rem(t + d, 8)), "sqt")

    def grad_part(a, dyh, dz):
        pyh = lax.rem(yh + dyh, 2)
        pz = lax.rem(z + 4 - dz, 4)
        cols = pl.ds(pl.multiple_of((pyh * 4 + pz) * 512 + a * 256, 256), 256)
        return dot_nt(cot[a, dyh, dz], w[:, cols])

    grad = grad_part(0, 0, 0) + grad_part(1, 0, 0)
    for hf in pieces:
        due(("t", 1, 1, 0, hf))
        for dz in far:
            cot_copy(1, (1, 0), (1, dz), tp_dev(yh, ring(z, dz)), hf)
        for dz in (1, 3, 2):
            due(("t", 0, 0, dz, hf))
            cot_copy(0, (0, dz), (1, dz), tp_dev(1 - yh, z), hf)
    grad = grad + grad_part(1, 1, 0)
    for dz in (1, 3, 2):
        grad = grad + grad_part(0, 0, dz)
        for hf in pieces:
            due(("t", 1, 0, dz, hf))
        grad = grad + grad_part(1, 0, dz)
    for a, dz in ((0, 0), (0, 1), (0, 3), (0, 2), (1, 1), (1, 3), (1, 2)):
        for hf in pieces:
            due(("t", a, 1, dz, hf))
        grad = grad + grad_part(a, 1, dz)
    g_tx[...] = grad.astype(BF16)

    def g_moves(act):
        to_heads(lambda hx: g_tx.at[:, lanes(hx, HD)], g.at[unit, c], g_send, g_recv, 0, act)

    g_moves("start")
    owed["g"] = lambda: wait_for(g, g_recv)
    pending.append(lambda: g_moves("wait"))

    row_half = pl.ds(pl.multiple_of(80 * (z % 2), 16), 80)
    chip_slot = y * 4 + home * 2 + unit

    def tw_source(dest):
        tt = dest // 2
        dyh = lax.rem(yh + tt // 4, 2)
        dz = lax.rem(z + 4 - tt % 4, 4)
        return cot.at[dest % 2, dyh, dz]

    def tw_send_all(act):
        for dx in (2, 1, 3, 0):
            for pc in range(2):
                dest, _ = seq_dev(ring(x, dx), 1 - y, pc)
                copy = remote(
                    tw_source(dest).at[row_half, lanes(yh, HD)],
                    tw_part.at[home * 2 + unit],
                    tw_send.at[dx, pc],
                    tw_recv,
                    (dest, t),
                )
                copy.start() if act == "start" else copy.wait_send()

    def tw_turn(act):
        @pl.when(c == z // 2)
        def _():
            tw_send_all(act)

    tw_turn("start")
    for dx in (2, 1, 3, 0):
        for e in range(2):
            dest, _ = seq_dev(ring(x, dx), y, c if e == 0 else 1 - c)
            if dx or e:
                launch(remote(tw_source(dest), tw.at[chip_slot, c], twd_send.at[dx, e], twd_recv, (dest, t)))
            else:
                local_copy(tw_source(s), tw.at[chip_slot, c], twd_recv).start()
    owed["twd"] = lambda: wait_for(tw.at[pl.ds(y * 4, 4)], twd_recv)
    owed["tw"] = lambda: wait_for(tw_part, tw_recv)
    pending.append(lambda: tw_turn("wait"))

    def tw_view(dyh, dz):
        pyh = lax.rem(yh + dyh, 2)
        pz = lax.rem(z + 4 - dz, 4)
        rows = pl.ds(pl.multiple_of(80 * (pz % 2), 16), 80)
        return tw.at[pl.ds((1 - y) * 4, 4), pz // 2, rows, lanes(pyh, HD)]

    def twg_copy(origin, slot, dev):
        view = tw_view(*origin)
        src = tw_part if origin == (0, 0) else view
        stage("twg", slot, src, view, twg_send, twg_recv, dev)

    def tw_spread():
        due("tw")
        twg_copy((0, 0), (1, 0), tp_dev(1 - yh, z))
        local_copy(tw_part, tw_view(0, 0), twg_recv.at[0, 0]).start()
        owed["twg", 0, 0] = lambda: wait_for(tw_view(0, 0), twg_recv.at[0, 0])
        for dz in far:
            twg_copy((0, 0), (0, dz), tp_dev(yh, ring(z, dz)))

    def tw_pass_on():
        due(("twg", 1, 0))
        for dz in far:
            twg_copy((1, 0), (1, dz), tp_dev(yh, ring(z, dz)))

    due("g")
    gt = g[...].reshape(NQ, HD).astype(F32).T
    dterm = jnp.sum(gt * at_own[...].astype(F32), axis=0, keepdims=True)
    dqt[...] = jnp.zeros_like(dqt)

    def back(i, lo):
        gq = g[...].reshape(NQ, HD)[lo:]
        queries = qq[...].reshape(NQ, 2 * HD)[lo:, HD:]
        keys = chunk(kk, i)[:, :HD]
        vals = chunk(vv, i)[:, :HD]
        ph = p16[i, :, lo:]
        dp = dot_nt(vals, gq)
        ds = (ph.astype(F32) * (dp - dterm[:, lo:])).astype(BF16)
        dkv[1, i] = dot_nn(ph, gq).astype(BF16).reshape(2, ROWS, HD)
        dkv[0, i] = (dot_nn(ds, queries) * SCALE).astype(BF16).reshape(2, ROWS, HD)
        dqt[:, lo:] += dot_tn(keys, ds)

    def sib_copy(i):
        return remote(
            dkv.at[:, i, 1 - c], sib_rx.at[:, i], sib_send.at[i], sib_recv.at[i], (sibling, t)
        )

    def dkv_copy(i):
        return remote(
            dkv_tx.at[:, i], dkv_rx.at[m], dkv_send.at[i], dkv_recv.at[m], seq_dev(i // 2, i % 2, c)
        )

    def both_cores(i):
        sib_copy(i).wait_recv()
        return dkv[:, i, c].astype(F32) + sib_rx[:, i].astype(F32)

    def pass_to_owner(i):
        dkv_tx[:, i] = both_cores(i).astype(BF16)
        dkv_copy(i).start()

    def back_step(k, state):
        i = lax.rem(m + 1 + k, 8)

        @pl.when(i < n0)
        def _():
            back(i, 0)

        @pl.when((i >= n0) & (i < n1))
        def _():
            back(i, 256)

        @pl.when(i >= n1)
        def _():
            dkv[:, i] = jnp.zeros((2, 2, ROWS, HD), BF16)

        sib_copy(i).start()

        @pl.when(k > 0)
        def _():
            pass_to_owner(lax.rem(m + k, 8))

        return state

    lax.fori_loop(0, 1, back_step, 0)
    tw_spread()
    lax.fori_loop(1, 6, back_step, 0)
    tw_pass_on()
    due("atx")
    due("at2")
    atf = remote(at.at[:, c], at.at[:, c], atf_send, atf_recv, (sibling, t))
    launch(atf)
    owed["atf"] = atf.wait_recv
    sqv = sq_tp[0]
    for d in range(1, 8):
        due(("sqt", d))
        sqv = sqv + sq_tp[d]
    sq_seq[0] = sqv
    for d in range(1, 16):
        sq_copy(sq_seq, d, sqs_send, sqs_recv, (lax.rem(s + d, 16), t), "sqs")

    lax.fori_loop(6, 8, back_step, 0)
    dq_tx[...] = (dqt[...] * SCALE).T.astype(BF16).reshape(2, 2, ROWS, HD)
    to_owners(dq_tx, dq_rx.at[:, lanes(head, HD)], dq_send, dq_recv, "start")
    owed["dq"] = lambda: wait_for(dq_rx, dq_recv)
    pending.append(lambda: to_owners(dq_tx, dq_rx.at[:, lanes(head, HD)], dq_send, dq_recv, "wait"))
    dkv_rx[m] = both_cores(m).astype(BF16)

    for dyh in range(2):
        for dz in range(4):
            if (dyh, dz) != (1, 0):
                due(("twg", dyh, dz))
    due("twd")
    due("atf")

    gw = jnp.zeros((512, 256), F32)
    for a in range(4):
        rows = tw[2 * a : 2 * a + 2].reshape(NQ, 256)
        gw = gw + dot_nn(at[a // 2, a % 2], rows)
    gw_out[...] = gw

    sqv = sq_seq[0]
    for d in range(1, 16):
        due(("sqs", d))
        sqv = sqv + sq_seq[d]
    ms_out[...] = sqv

    due("dq")
    dq_out[...] = dq_rx[...]

    def all_dkv(k, state):
        i = lax.rem(m + 1 + k, 8)
        sib_copy(i).wait_send()

        @pl.when(k < 7)
        def _():
            dkv_copy(i).wait_send()
            remote(dkv_tx.at[:, i], dkv_rx.at[i], dkv_send.at[i], dkv_recv.at[i], (sibling, t)).wait_recv()

        return state

    lax.fori_loop(0, 8, all_dkv, 0)
    for h in range(4):
        for a, out in enumerate((dk_out, dv_out)):
            out[:, h * HD : (h + 1) * HD] = dkv_rx[2 * h, a].astype(F32) + dkv_rx[2 * h + 1, a].astype(F32)
    finish()


def scaled(ms_ref, *refs):
    scale = lax.rsqrt(ms_ref[0:1, 0:1] / (2560 * 4096) + 1e-05)
    for src, dst in zip(refs[:4], refs[4:]):
        dst[...] = (src[...].astype(F32) * scale).astype(BF16)


def on_device(q, k, v, qd, kd, vd, w, noisy, vel, time_index, frame_lengths):
    smem = pl.BlockSpec(memory_space=pltpu.SMEM)
    vmem = pl.BlockSpec(memory_space=pltpu.VMEM)
    hbm = pl.BlockSpec(memory_space=pl.ANY)
    dma = pltpu.SemaphoreType.DMA
    scratch = [
        pltpu.VMEM((512, 4096), BF16),
        pltpu.VMEM((4, 2, 2, ROWS, 256), BF16),
        pltpu.VMEM((4, 2, 2, ROWS, 256), BF16),
        pltpu.VMEM((2, 2, ROWS, 256), BF16),
        pltpu.VMEM((8, UNIT, NQ), F32),
        pltpu.VMEM((8, UNIT, NQ), F32),
        pltpu.VMEM((8, UNIT, NQ), BF16),
        pltpu.VMEM((2 * HD, NQ), F32),
        pltpu.VMEM((HD, NQ), F32),
        pltpu.VMEM((2, 2, ROWS, HD), BF16),
        pltpu.VMEM((ROWS, 512), BF16),
        pltpu.VMEM((HD, NQ), BF16),
        pltpu.VMEM((2, 2, 512, NQ), BF16),
        pltpu.VMEM((32, 4096), F32),
        pltpu.VMEM((2, 20, 4096), BF16),
        dma((2,)),
        pltpu.VMEM((4, 2, ROWS, 256), BF16),
        pltpu.VMEM((4, ROWS, 256), BF16),
        pltpu.VMEM((4, 2, ROWS, 256), BF16),
        pltpu.VMEM((4, ROWS, 256), BF16),
        pltpu.VMEM((2, ROWS, 256), F32),
        pltpu.VMEM((4, ROWS, 256), F32),
        pltpu.VMEM((ROWS, 256), BF16),
        pltpu.VMEM((4, ROWS, 256), BF16),
        pltpu.VMEM((ROWS, 256), BF16),
        pltpu.VMEM((4, ROWS, 256), BF16),
        pltpu.VMEM((2, 2, 4, ROWS, 256), BF16),
        pltpu.VMEM((ROWS, 512), BF16),
        pltpu.VMEM((2, 2, ROWS, HD), BF16),
        pltpu.VMEM((HD, NQ), F32),
        pltpu.VMEM((2, 2, ROWS, HD), BF16),
        pltpu.VMEM((ROWS, 512), BF16),
        pltpu.VMEM((2, 8, 2, ROWS, HD), BF16),
        pltpu.VMEM((2, 8, ROWS, HD), BF16),
        pltpu.VMEM((2, 8, ROWS, HD), BF16),
        pltpu.VMEM((8, 2, ROWS, HD), BF16),
        pltpu.VMEM((4, 80, HD), BF16),
        pltpu.VMEM((8, 2, ROWS, 256), BF16),
        pltpu.VMEM((8, 8, 128), F32),
        pltpu.VMEM((16, 8, 128), F32),
        dma,
        dma((4, 4)),
        dma((4,)),
        dma((4, 4)),
        dma((4,)),
        dma((4,)),
        dma((4,)),
        dma((4,)),
        dma((4,)),
        dma((2, 4)),
        dma((2,)),
        dma((2, 2)),
        dma,
        dma((2, 4)),
        dma,
        dma,
        dma,
        dma,
        dma,
        dma,
        dma((len(CUTS) - 1, 4)),
        dma((len(CUTS) - 1, 4)),
        dma((len(CUTS) - 1,)),
        dma((len(CUTS) - 1,)),
        dma((len(CUTS) - 1,)),
        dma((len(CUTS) - 1,)),
        dma((len(CUTS) - 1, 4)),
        dma((len(CUTS) - 1, 4)),
        dma((2, 2, 4, len(CUTS) - 1)),
        dma((2, 2, 4, len(CUTS) - 1)),
        dma((1, 4)),
        dma,
        dma((4, 2)),
        dma((4, 2)),
        dma,
        dma,
        dma((2, 4)),
        dma((2, 4)),
        dma((2, 2)),
        dma,
        dma((8,)),
        dma((8,)),
        dma((8,)),
        dma((8,)),
        dma((8,)),
        dma((8,)),
        dma((16,)),
        dma((16,)),
    ]
    dq, dk, dv, gw, ms = pl.pallas_call(
        kernel,
        out_shape=(
            jax.ShapeDtypeStruct((ROWS, 512), BF16),
            jax.ShapeDtypeStruct((ROWS, 512), F32),
            jax.ShapeDtypeStruct((ROWS, 512), F32),
            jax.ShapeDtypeStruct((512, 256), F32),
            jax.ShapeDtypeStruct((8, 128), F32),
        ),
        in_specs=[smem, smem] + [hbm] * 9,
        out_specs=(vmem,) * 5,
        scratch_shapes=scratch,
        compiler_params=pltpu.CompilerParams(
            collective_id=0, has_side_effects=True, vmem_limit_bytes=56 * 1024 * 1024
        ),
        cost_estimate=pl.CostEstimate(flops=7 * 10**9, bytes_accessed=8 * 10**6, transcendentals=1638400),
    )(frame_lengths, time_index, q, k, v, qd, kd, vd, w, noisy, vel)
    return pl.pallas_call(
        scaled,
        out_shape=tuple(jax.ShapeDtypeStruct(part.shape, BF16) for part in (dq, dk, dv, gw)),
        in_specs=[vmem] * 5,
        out_specs=(vmem,) * 4,
    )(ms, dq, dk, dv, gw)


def solution(mesh):
    in_specs = (P("seq", "tp"),) * 6 + (P("tp", None), P(("seq", "tp"), None), P(("seq", "tp"), None), P(), P())
    out_specs = (P("seq", "tp"), P("seq", "tp"), P("seq", "tp"), P("tp", "seq"))
    return jax.shard_map(
        on_device, mesh=mesh, in_specs=in_specs, out_specs=out_specs, check_vma=False
    )
```

```python
import math

import jax
import jax.numpy as jnp
from jax import lax
from jax.experimental import pallas as pl
from jax.experimental.pallas import tpu as pltpu
from jax.sharding import PartitionSpec as P

HD = 128
TSTEPS = 64
FRAMES = 16
ROWS = 160
UNIT = 320
NCHIP = 8
NQ = 640
CUTS = (0, 80, 160)
SCALE = 1.0 / math.sqrt(HD)
MESH = pl.DeviceIdType.MESH
F32 = jnp.float32
BF16 = jnp.bfloat16


def dot_nt(a, b):
    return lax.dot_general(a, b, (((1,), (1,)), ((), ())), preferred_element_type=F32)


def dot_nn(a, b):
    return lax.dot_general(a, b, (((1,), (0,)), ((), ())), preferred_element_type=F32)


def dot_tn(a, b):
    return lax.dot_general(a, b, (((0,), (0,)), ((), ())), preferred_element_type=F32)


def kernel(
    frame_ref,
    time_ref,
    q_ref,
    k_ref,
    v_ref,
    qd_ref,
    kd_ref,
    vd_ref,
    w_hbm,
    noisy_ref,
    vel_ref,
    dq_out,
    dk_out,
    dv_out,
    gw_out,
    ms_out,
    w,
    kk,
    vv,
    qq,
    sbuf,
    stbuf,
    p16,
    acc1,
    acc2,
    ublk,
    uown,
    at_own,
    at,
    negb,
    lat,
    lat_sem,
    part_a,
    part_b,
    rx_a,
    rx_b,
    sum_a,
    sum_b,
    part_a2,
    part_b2,
    rx_a2,
    rx_b2,
    cot,
    g_tx,
    g,
    dqt,
    dq_tx,
    dq_rx,
    dkv,
    sib_rx,
    dkv_tx,
    dkv_rx,
    tw_part,
    tw,
    sq_tp,
    sq_seq,
    wsem,
    kvx_send,
    kvx_recv,
    kvy_send,
    kvy_recv,
    fwx_send,
    fwx_recv,
    fwy_send,
    fwy_recv,
    q_send,
    q_recv,
    u_send,
    u_recv,
    atx_send,
    atx_recv,
    aty_send,
    aty_recv,
    at2_recv,
    atf_send,
    atf_recv,
    rsa_send,
    rsa_recv,
    rsb_send,
    rsb_recv,
    rsa2_send,
    rsa2_recv,
    rsb2_send,
    rsb2_recv,
    t_send,
    t_recv,
    g_send,
    g_recv,
    tw_send,
    twd_send,
    twd_recv,
    tw_recv,
    twg_send,
    twg_recv,
    dq_send,
    dq_recv,
    sib_send,
    sib_recv,
    dkv_send,
    dkv_recv,
    sqt_send,
    sqt_recv,
    sqs_send,
    sqs_recv,
):
    s = lax.axis_index("seq")
    t = lax.axis_index("tp")
    x = s // 4
    y = (s // 2) % 2
    c = s % 2
    m = s // 2
    yh = t // 4
    z = t % 4
    head = x
    far = (2, 1, 3)

    def ring(pos, step):
        return lax.rem(pos + step, 4)

    def seq_dev(px, py, pc):
        return (px * 4 + py * 2 + pc, t)

    def tp_dev(pyh, pz):
        return (s, pyh * 4 + pz)

    def local_copy(src, dst, sem):
        return pltpu.make_async_copy(src, dst, sem)

    def remote(src, dst, ssem, rsem, dev):
        return pltpu.make_async_remote_copy(
            src_ref=src, dst_ref=dst, send_sem=ssem, recv_sem=rsem, device_id=dev, device_id_type=MESH
        )

    def lanes(index, width):
        return pl.ds(pl.multiple_of(index * width, width), width)

    def wait_for(ref, sem):
        pltpu.make_async_copy(ref, ref, sem).wait()

    pending = []

    def launch(copy):
        copy.start()
        pending.append(copy.wait_send)

    owed = {}

    def due(name):
        owed.pop(name)()

    def finish():
        for name in list(owed):
            due(name)
        for wait in pending:
            wait()

    wload = pltpu.make_async_copy(w_hbm, w, wsem)
    wload.start()
    lat_loads = [pltpu.make_async_copy(ref, lat.at[i], lat_sem.at[i]) for i, ref in enumerate((noisy_ref, vel_ref))]
    for i, load in enumerate(lat_loads):
        load.start()
        owed["lat", i] = load.wait
    owed["w"] = wload.wait

    barrier = pltpu.get_barrier_semaphore()
    sibling = s + 1 - 2 * c
    partners = [seq_dev(x, 1 - y, c), (sibling, t), tp_dev(1 - yh, z)]
    for dx in far:
        partners += [seq_dev(ring(x, dx), y, c), seq_dev(ring(x, dx), y, 1 - c), tp_dev(yh, ring(z, dx))]
    for dev in partners:
        pl.semaphore_signal(barrier, inc=1, device_id=dev, device_id_type=MESH)
    pl.semaphore_wait(barrier, len(partners))

    kv_src = (k_ref, kd_ref, v_ref, vd_ref)
    kv_dst = ((kk, 0), (kk, 1), (vv, 0), (vv, 1))

    def kv_view(a, px, py, pc):
        buf, half = kv_dst[a]
        return buf.at[px, py, pc, :, half * HD : (half + 1) * HD]

    def kv_piece(a, px):
        return kv_src[a].at[:, lanes(px, HD)]

    def kv_all(a, py, pc):
        return kv_view(a, slice(None), py, pc)

    def kv_own(a):
        local_copy(kv_piece(a, x), kv_view(a, x, y, c), kvx_recv.at[a]).start()
        launch(
            remote(
                kv_piece(a, x), kv_view(a, x, y, c), kvy_send.at[a, 0], kvy_recv.at[a], seq_dev(x, 1 - y, c)
            )
        )

    def kv_along_x(a):
        for dx in far:
            hx = ring(x, dx)
            launch(
                remote(
                    kv_piece(a, hx), kv_view(a, x, y, c), kvx_send.at[a, dx], kvx_recv.at[a], seq_dev(hx, y, c)
                )
            )
        owed["kvx", a] = lambda: wait_for(kv_all(a, y, c), kvx_recv.at[a])
        owed["kvy", a] = lambda: wait_for(kv_all(a, 1 - y, c), kvy_recv.at[a])

    def kv_across(a):
        due(("kvx", a))
        for dx in far:
            view = kv_view(a, ring(x, dx), y, c)
            launch(remote(view, view, kvy_send.at[a, dx], kvy_recv.at[a], seq_dev(x, 1 - y, c)))
        to_sibling(a, y, fwx_send, fwx_recv, "fwx")

    def to_sibling(a, py, send, recv, name):
        view = kv_all(a, py, c)
        launch(remote(view, view, send.at[a], recv.at[a], (sibling, t)))
        owed[name, a] = lambda: wait_for(kv_all(a, py, 1 - c), recv.at[a])

    def kv_received(a):
        due(("kvy", a))
        to_sibling(a, 1 - y, fwy_send, fwy_recv, "fwy")

    def kv_complete(a):
        due(("fwx", a))
        due(("fwy", a))

    home = jnp.where((x == 1) | (x == 2), 1, 0)
    unit = x // 2

    def to_heads(src_of, dst, send, recv, slot, act):
        for dx in (2, 1, 3, 0):
            hx = ring(x, dx)
            if dx:
                copy = remote(src_of(hx), dst, send.at[slot, dx], recv, seq_dev(hx, y, home))
                copy.start() if act == "start" else copy.wait_send()
            else:

                @pl.when(home != c)
                def _():
                    copy = remote(src_of(hx), dst, send.at[slot, dx], recv, seq_dev(hx, y, home))
                    copy.start() if act == "start" else copy.wait_send()

                if act == "start":

                    @pl.when(home == c)
                    def _():
                        local_copy(src_of(hx), dst, recv).start()

    def to_owners(src, dst, send, recv, act):
        for u in range(2):
            ux = c if u == 0 else 3 - c
            for core in range(2):
                dev = ux * 4 + y * 2 + core

                @pl.when(dev != s)
                def _():
                    copy = remote(src.at[u, core], dst, send.at[u, core], recv, (dev, t))
                    copy.start() if act == "start" else copy.wait_send()

                if act == "start":

                    @pl.when(dev == s)
                    def _():
                        local_copy(src.at[u, core], dst, recv).start()

    def q_moves(act, which=(1, 0)):
        for a in which:
            ref = (qd_ref, q_ref)[a]
            to_heads(
                lambda hx, ref=ref: ref.at[:, lanes(hx, HD)],
                qq.at[unit, c, :, a * HD : (a + 1) * HD],
                q_send,
                q_recv.at[a],
                a,
                act,
            )

    kv_along_x(0)
    for a in range(4):
        kv_own(a)
    kv_along_x(1)
    q_moves("start", (1,))
    kv_along_x(2)
    q_moves("start", (0,))
    pending.append(lambda: q_moves("wait"))
    for a in range(2):
        owed["q", a] = lambda a=a: wait_for(qq.at[:, :, :, a * HD : (a + 1) * HD], q_recv.at[a])
    kv_along_x(3)

    ends = []
    total = 0
    for f in range(FRAMES):
        total = total + frame_ref[f]
        ends.append(total)
    times = [time_ref[f] for f in range(FRAMES)]

    def frame_facts(pos):
        kend = jnp.zeros(pos.shape, jnp.int32) + ends[FRAMES - 1]
        level = jnp.zeros(pos.shape, jnp.int32) + times[FRAMES - 1]
        for f in range(FRAMES - 2, -1, -1):
            inside = pos < ends[f]
            kend = jnp.where(inside, ends[f], kend)
            level = jnp.where(inside, times[f], level)
        angle = (level.astype(F32) + 0.5) * (math.pi / (2 * TSTEPS))
        return kend, jnp.cos(angle), jnp.sin(angle)

    lane = lax.broadcasted_iota(jnp.int32, (1, NQ), 1)
    chip0 = 2 * c + y
    chip1 = 2 * (3 - c) + y
    qpos = jnp.where(lane < UNIT, UNIT * chip0 + lane, UNIT * chip1 + lane - UNIT)
    kend, cosq, sinq = frame_facts(qpos)

    rpos = s * ROWS + t * 20 + lax.broadcasted_iota(jnp.int32, (20, 1), 0)
    _, cosr, sinr = frame_facts(rpos)
    for i in range(2):
        due(("lat", i))
    negb[...] = jnp.zeros_like(negb)
    negb[0:20, :] = sinr * cosr * lat[0].astype(F32) - cosr * cosr * lat[1].astype(F32)

    n0 = chip0 + 2
    n1 = jnp.minimum(chip1 + 2, 8)

    def over_keys(body, carry, between=None):
        carry = lax.fori_loop(0, n0, lambda i, st: body(i, st, 0), carry)
        if between is not None:
            between()
        return lax.fori_loop(n0, n1, lambda i, st: body(i, st, 256), carry)

    def put(row, lo, part_row):
        if lo == 0:
            return part_row
        return jnp.concatenate([row[:, :lo], part_row], axis=1)

    kv_across(0)
    kv_across(1)
    kv_across(2)
    kv_received(0)
    due(("q", 1))
    kv_complete(0)

    def chunk(buf, i):
        return buf[i // 2, i % 2].reshape(UNIT, buf.shape[-1])

    def pass1(i, top, lo):
        keys = kk[i // 2, i % 2, :, :, :HD].reshape(UNIT, HD)
        queries = qq[:, :, :, HD:].reshape(NQ, HD)[lo:]
        sc = dot_nt(keys, queries) * SCALE
        kpos = i * UNIT + lax.broadcasted_iota(jnp.int32, (UNIT, 1), 0)
        sc = jnp.where(kpos < kend[:, lo:], sc, -1e30)
        sbuf[i, :, lo:] = sc
        return put(top, lo, jnp.maximum(top[:, lo:], jnp.max(sc, axis=0, keepdims=True)))

    top = over_keys(pass1, jnp.full((1, NQ), -1e30, F32))

    kv_received(1)
    due(("q", 0))
    kv_across(3)
    kv_complete(1)

    def pass2(i, state, lo):
        den, tan = state
        st = dot_nt(chunk(kk, i), qq[...].reshape(NQ, 2 * HD)[lo:]) * SCALE
        p = jnp.exp(sbuf[i, :, lo:] - top[:, lo:])
        sbuf[i, :, lo:] = p
        stbuf[i, :, lo:] = st
        den = put(den, lo, den[:, lo:] + jnp.sum(p, axis=0, keepdims=True))
        tan = put(tan, lo, tan[:, lo:] + jnp.sum(p * st, axis=0, keepdims=True))
        return den, tan

    row0 = jnp.zeros((1, NQ), F32)
    den, tan = over_keys(pass2, (row0, row0), lambda: kv_received(2))
    inv = 1.0 / den
    mean = tan * inv
    kv_complete(2)

    acc2[...] = jnp.zeros_like(acc2)

    def pass3(i, state, lo):
        p = sbuf[i, :, lo:] * inv[:, lo:]
        p16[i, :, lo:] = p.astype(BF16)
        ds = (p * (stbuf[i, :, lo:] - mean[:, lo:])).astype(BF16)
        vals = vv[i // 2, i % 2, :, :, :HD].reshape(UNIT, HD)
        acc2[:, lo:] += dot_tn(vals, ds)
        return state

    over_keys(pass3, 0, lambda: kv_received(3))
    kv_complete(3)
    acc1[...] = jnp.zeros_like(acc1)

    def pass4(i, state, lo):
        acc1[:, lo:] += dot_tn(chunk(vv, i), p16[i, :, lo:])
        return state

    over_keys(pass4, 0)
    attn_t = acc1[0:HD].astype(BF16)
    tan_t = (acc2[...] + acc1[HD:]).astype(BF16)
    at_own[...] = attn_t
    u_t = (0.5 * cosq) * (cosq * attn_t.astype(F32) + sinq * tan_t.astype(F32))
    ublk[...] = u_t.T.astype(BF16).reshape(2, 2, ROWS, HD)
    to_owners(ublk, uown.at[:, lanes(head, HD)], u_send, u_recv, "start")
    owed["u"] = lambda: wait_for(uown, u_recv)
    pending.append(lambda: to_owners(ublk, uown.at[:, lanes(head, HD)], u_send, u_recv, "wait"))

    def at_view(py, hx):
        return at.at[py, c, lanes(hx, HD), :]

    launch(remote(at_own, at_view(y, x), aty_send, aty_recv, seq_dev(x, 1 - y, c)))
    owed["aty"] = lambda: wait_for(at_view(1 - y, x), aty_recv)

    def at_pass_on():
        due("aty")
        for dx in far:
            view = at_view(1 - y, x)
            launch(remote(view, view, atx_send.at[1, dx], at2_recv, seq_dev(ring(x, dx), y, c)))
        owed["at2"] = lambda: wait_for(at.at[1 - y, c, 0 : 3 * HD], at2_recv)

    due("w")
    due("u")
    u = uown[...]
    pick = (
        lax.broadcasted_iota(jnp.int32, (ROWS, 32), 0)
        == t * 20 + lax.broadcasted_iota(jnp.int32, (ROWS, 32), 1)
    ) & (lax.broadcasted_iota(jnp.int32, (ROWS, 32), 1) < 20)
    pick = pick.astype(F32).astype(BF16)

    def partial(pyh, pz, half):
        cols = pl.ds(pl.multiple_of((pyh * 4 + pz) * 512 + half * 256, 256), 256)
        return dot_nn(u, w[:, cols]) + dot_nn(pick, negb[:, cols].astype(BF16))

    for dz in range(4):
        part_b[dz] = partial(1 - yh, ring(z, dz), 1).astype(BF16)
    halves = [slice(lo, hi) for lo, hi in zip(CUTS[:-1], CUTS[1:])]
    pieces = range(len(halves))

    def stage(name, key, src, dst, send, recv, dev):
        copy = remote(src, dst, send.at[key], recv.at[key], dev)
        launch(copy)
        owed[(name,) + key] = copy.wait_recv

    def send_b(hf):
        rows = halves[hf]
        stage("rsb", (hf,), part_b.at[:, rows], rx_b.at[:, rows], rsb_send, rsb_recv, tp_dev(1 - yh, z))

    send_b(0)

    for dz in far:
        for e in range(2):
            part_a[dz, e] = partial(yh if e == 0 else 1 - yh, ring(z, dz), 0).astype(BF16)

    def send_a(hf):
        rows = halves[hf]
        for dz in far:
            dev = tp_dev(yh, ring(z, dz))
            stage("rsa", (hf, dz), part_a.at[dz, :, rows], rx_a.at[dz, :, rows], rsa_send, rsa_recv, dev)

    send_a(0)
    for hf in pieces[1:]:
        send_b(hf)
        send_a(hf)

    local_copy(at_own, at_view(y, x), atx_recv).start()
    for dx in far:
        launch(remote(at_own, at_view(y, x), atx_send.at[0, dx], atx_recv, seq_dev(ring(x, dx), y, c)))
    owed["atx"] = lambda: wait_for(at.at[y, c], atx_recv)

    at_pass_on()

    for dz in range(4):
        sum_b[dz] = partial(yh, ring(z, dz), 1)
    for e in range(2):
        sum_a[e] = partial(yh if e == 0 else 1 - yh, z, 0)


    def cot_copy(a, src, dst, dev, hf):
        rows = halves[hf]
        sem = (a,) + dst + (hf,)
        stage("t", sem, cot.at[(a,) + src + (rows,)], cot.at[(a,) + dst + (rows,)], t_send, t_recv, dev)

    for hf in pieces:
        rows = halves[hf]
        due(("rsb", hf))
        for dz in far:
            part_b2[dz, rows] = (sum_b[dz, rows] + rx_b[dz, rows].astype(F32)).astype(BF16)
            dev = tp_dev(yh, ring(z, dz))
            stage("rsb2", (hf, dz), part_b2.at[dz, rows], rx_b2.at[dz, rows], rsb2_send, rsb2_recv, dev)
        other = sum_a[1, rows]
        for dz in far:
            due(("rsa", hf, dz))
            other = other + rx_a[dz, 1, rows].astype(F32)
        part_a2[rows] = other.astype(BF16)
        stage("rsa2", (hf,), part_a2.at[rows], rx_a2.at[rows], rsa2_send, rsa2_recv, tp_dev(1 - yh, z))

    sq = jnp.zeros((1, 256), F32)
    for hf in pieces:
        rows = halves[hf]
        cot_a = sum_a[0, rows]
        for dz in far:
            cot_a = cot_a + rx_a[dz, 0, rows].astype(F32)
        due(("rsa2", hf))
        cot_a = cot_a + rx_a2[rows].astype(F32)
        cot[0, 0, 0, rows] = cot_a.astype(BF16)
        for dz in far:
            cot_copy(0, (0, 0), (0, dz), tp_dev(yh, ring(z, dz)), hf)
        cot_b = sum_b[0, rows] + rx_b[0, rows].astype(F32)
        for dz in far:
            due(("rsb2", hf, dz))
            cot_b = cot_b + rx_b2[dz, rows].astype(F32)
        cot[1, 0, 0, rows] = cot_b.astype(BF16)
        cot_copy(1, (0, 0), (1, 0), tp_dev(1 - yh, z), hf)
        for dz in far:
            cot_copy(1, (0, 0), (0, dz), tp_dev(yh, ring(z, dz)), hf)
        cot_copy(0, (0, 0), (1, 0), tp_dev(1 - yh, z), hf)
        sq = sq + jnp.sum(cot_a * cot_a + cot_b * cot_b, axis=0, keepdims=True)

    def sq_copy(buf, d, send, recv, dev, name):
        copy = remote(buf.at[0], buf.at[d], send.at[d], recv.at[d], dev)
        launch(copy)
        owed[name, d] = copy.wait_recv

    sq_tp[0] = jnp.zeros((8, 128), F32) + jnp.sum(sq, axis=1, keepdims=True)
    for d in range(1, 8):
        sq_copy(sq_tp, d, sqt_send, sqt_recv, (s, lax.rem(t + d, 8)), "sqt")

    def grad_part(a, dyh, dz):
        pyh = lax.rem(yh + dyh, 2)
        pz = lax.rem(z + 4 - dz, 4)
        cols = pl.ds(pl.multiple_of((pyh * 4 + pz) * 512 + a * 256, 256), 256)
        return dot_nt(cot[a, dyh, dz], w[:, cols])

    grad = grad_part(0, 0, 0) + grad_part(1, 0, 0)
    for hf in pieces:
        due(("t", 1, 1, 0, hf))
        for dz in far:
            cot_copy(1, (1, 0), (1, dz), tp_dev(yh, ring(z, dz)), hf)
        for dz in (1, 3, 2):
            due(("t", 0, 0, dz, hf))
            cot_copy(0, (0, dz), (1, dz), tp_dev(1 - yh, z), hf)
    grad = grad + grad_part(1, 1, 0)
    for dz in (1, 3, 2):
        grad = grad + grad_part(0, 0, dz)
        for hf in pieces:
            due(("t", 1, 0, dz, hf))
        grad = grad + grad_part(1, 0, dz)
    for a, dz in ((0, 0), (0, 1), (0, 3), (0, 2), (1, 1), (1, 3), (1, 2)):
        for hf in pieces:
            due(("t", a, 1, dz, hf))
        grad = grad + grad_part(a, 1, dz)
    g_tx[...] = grad.astype(BF16)

    def g_moves(act):
        to_heads(lambda hx: g_tx.at[:, lanes(hx, HD)], g.at[unit, c], g_send, g_recv, 0, act)

    g_moves("start")
    owed["g"] = lambda: wait_for(g, g_recv)
    pending.append(lambda: g_moves("wait"))

    row_half = pl.ds(pl.multiple_of(80 * (z % 2), 16), 80)
    chip_slot = y * 4 + home * 2 + unit

    def tw_source(dest):
        tt = dest // 2
        dyh = lax.rem(yh + tt // 4, 2)
        dz = lax.rem(z + 4 - tt % 4, 4)
        return cot.at[dest % 2, dyh, dz]

    def tw_send_all(act):
        for dx in (2, 1, 3, 0):
            for pc in range(2):
                dest, _ = seq_dev(ring(x, dx), 1 - y, pc)
                copy = remote(
                    tw_source(dest).at[row_half, lanes(yh, HD)],
                    tw_part.at[home * 2 + unit],
                    tw_send.at[dx, pc],
                    tw_recv,
                    (dest, t),
                )
                copy.start() if act == "start" else copy.wait_send()

    def tw_turn(act):
        @pl.when(c == z // 2)
        def _():
            tw_send_all(act)

    tw_turn("start")
    for dx in (2, 1, 3, 0):
        for e in range(2):
            dest, _ = seq_dev(ring(x, dx), y, c if e == 0 else 1 - c)
            if dx or e:
                launch(remote(tw_source(dest), tw.at[chip_slot, c], twd_send.at[dx, e], twd_recv, (dest, t)))
            else:
                local_copy(tw_source(s), tw.at[chip_slot, c], twd_recv).start()
    owed["twd"] = lambda: wait_for(tw.at[pl.ds(y * 4, 4)], twd_recv)
    owed["tw"] = lambda: wait_for(tw_part, tw_recv)
    pending.append(lambda: tw_turn("wait"))

    def tw_view(dyh, dz):
        pyh = lax.rem(yh + dyh, 2)
        pz = lax.rem(z + 4 - dz, 4)
        rows = pl.ds(pl.multiple_of(80 * (pz % 2), 16), 80)
        return tw.at[pl.ds((1 - y) * 4, 4), pz // 2, rows, lanes(pyh, HD)]

    def twg_copy(origin, slot, dev):
        view = tw_view(*origin)
        src = tw_part if origin == (0, 0) else view
        stage("twg", slot, src, view, twg_send, twg_recv, dev)

    def tw_spread():
        due("tw")
        twg_copy((0, 0), (1, 0), tp_dev(1 - yh, z))
        local_copy(tw_part, tw_view(0, 0), twg_recv.at[0, 0]).start()
        owed["twg", 0, 0] = lambda: wait_for(tw_view(0, 0), twg_recv.at[0, 0])
        for dz in far:
            twg_copy((0, 0), (0, dz), tp_dev(yh, ring(z, dz)))

    def tw_pass_on():
        due(("twg", 1, 0))
        for dz in far:
            twg_copy((1, 0), (1, dz), tp_dev(yh, ring(z, dz)))

    due("g")
    gt = g[...].reshape(NQ, HD).astype(F32).T
    dterm = jnp.sum(gt * at_own[...].astype(F32), axis=0, keepdims=True)
    dqt[...] = jnp.zeros_like(dqt)

    def back(i, lo):
        gq = g[...].reshape(NQ, HD)[lo:]
        queries = qq[...].reshape(NQ, 2 * HD)[lo:, HD:]
        keys = chunk(kk, i)[:, :HD]
        vals = chunk(vv, i)[:, :HD]
        ph = p16[i, :, lo:]
        dp = dot_nt(vals, gq)
        ds = (ph.astype(F32) * (dp - dterm[:, lo:])).astype(BF16)
        dkv[1, i] = dot_nn(ph, gq).astype(BF16).reshape(2, ROWS, HD)
        dkv[0, i] = (dot_nn(ds, queries) * SCALE).astype(BF16).reshape(2, ROWS, HD)
        dqt[:, lo:] += dot_tn(keys, ds)

    def sib_copy(i):
        return remote(
            dkv.at[:, i, 1 - c], sib_rx.at[:, i], sib_send.at[i], sib_recv.at[i], (sibling, t)
        )

    def dkv_copy(i):
        return remote(
            dkv_tx.at[:, i], dkv_rx.at[m], dkv_send.at[i], dkv_recv.at[m], seq_dev(i // 2, i % 2, c)
        )

    def both_cores(i):
        sib_copy(i).wait_recv()
        return dkv[:, i, c].astype(F32) + sib_rx[:, i].astype(F32)

    def pass_to_owner(i):
        dkv_tx[:, i] = both_cores(i).astype(BF16)
        dkv_copy(i).start()

    def back_step(k, state):
        i = lax.rem(m + 1 + k, 8)

        @pl.when(i < n0)
        def _():
            back(i, 0)

        @pl.when((i >= n0) & (i < n1))
        def _():
            back(i, 256)

        @pl.when(i >= n1)
        def _():
            dkv[:, i] = jnp.zeros((2, 2, ROWS, HD), BF16)

        sib_copy(i).start()

        @pl.when(k > 0)
        def _():
            pass_to_owner(lax.rem(m + k, 8))

        return state

    lax.fori_loop(0, 1, back_step, 0)
    tw_spread()
    lax.fori_loop(1, 6, back_step, 0)
    tw_pass_on()
    due("atx")
    due("at2")
    atf = remote(at.at[:, c], at.at[:, c], atf_send, atf_recv, (sibling, t))
    launch(atf)
    owed["atf"] = atf.wait_recv
    sqv = sq_tp[0]
    for d in range(1, 8):
        due(("sqt", d))
        sqv = sqv + sq_tp[d]
    sq_seq[0] = sqv
    for d in range(1, 16):
        sq_copy(sq_seq, d, sqs_send, sqs_recv, (lax.rem(s + d, 16), t), "sqs")

    lax.fori_loop(6, 8, back_step, 0)
    dq_tx[...] = (dqt[...] * SCALE).T.astype(BF16).reshape(2, 2, ROWS, HD)
    to_owners(dq_tx, dq_rx.at[:, lanes(head, HD)], dq_send, dq_recv, "start")
    owed["dq"] = lambda: wait_for(dq_rx, dq_recv)
    pending.append(lambda: to_owners(dq_tx, dq_rx.at[:, lanes(head, HD)], dq_send, dq_recv, "wait"))
    dkv_rx[m] = both_cores(m).astype(BF16)

    def weight_part(py):
        out = jnp.zeros((512, 256), F32)
        for e in range(2):
            rows = tw[pl.ds(py * 4 + 2 * e, 2)].reshape(NQ, 256)
            out = out + dot_nn(at[py, e], rows)
        return out

    due("twd")
    due("atf")
    gw = weight_part(y)
    for dyh in range(2):
        for dz in range(4):
            if (dyh, dz) != (1, 0):
                due(("twg", dyh, dz))
    gw = gw + weight_part(1 - y)
    gw_out[...] = gw

    sqv = sq_seq[0]
    for d in range(1, 16):
        due(("sqs", d))
        sqv = sqv + sq_seq[d]
    ms_out[...] = sqv

    due("dq")
    dq_out[...] = dq_rx[...]

    def all_dkv(k, state):
        i = lax.rem(m + 1 + k, 8)
        sib_copy(i).wait_send()

        @pl.when(k < 7)
        def _():
            dkv_copy(i).wait_send()
            remote(dkv_tx.at[:, i], dkv_rx.at[i], dkv_send.at[i], dkv_recv.at[i], (sibling, t)).wait_recv()

        return state

    lax.fori_loop(0, 8, all_dkv, 0)
    for h in range(4):
        for a, out in enumerate((dk_out, dv_out)):
            out[:, h * HD : (h + 1) * HD] = dkv_rx[2 * h, a].astype(F32) + dkv_rx[2 * h + 1, a].astype(F32)
    finish()


def scaled(ms_ref, *refs):
    scale = lax.rsqrt(ms_ref[0:1, 0:1] / (2560 * 4096) + 1e-05)
    for src, dst in zip(refs[:4], refs[4:]):
        dst[...] = (src[...].astype(F32) * scale).astype(BF16)


def on_device(q, k, v, qd, kd, vd, w, noisy, vel, time_index, frame_lengths):
    smem = pl.BlockSpec(memory_space=pltpu.SMEM)
    vmem = pl.BlockSpec(memory_space=pltpu.VMEM)
    hbm = pl.BlockSpec(memory_space=pl.ANY)
    dma = pltpu.SemaphoreType.DMA
    scratch = [
        pltpu.VMEM((512, 4096), BF16),
        pltpu.VMEM((4, 2, 2, ROWS, 256), BF16),
        pltpu.VMEM((4, 2, 2, ROWS, 256), BF16),
        pltpu.VMEM((2, 2, ROWS, 256), BF16),
        pltpu.VMEM((8, UNIT, NQ), F32),
        pltpu.VMEM((8, UNIT, NQ), F32),
        pltpu.VMEM((8, UNIT, NQ), BF16),
        pltpu.VMEM((2 * HD, NQ), F32),
        pltpu.VMEM((HD, NQ), F32),
        pltpu.VMEM((2, 2, ROWS, HD), BF16),
        pltpu.VMEM((ROWS, 512), BF16),
        pltpu.VMEM((HD, NQ), BF16),
        pltpu.VMEM((2, 2, 512, NQ), BF16),
        pltpu.VMEM((32, 4096), F32),
        pltpu.VMEM((2, 20, 4096), BF16),
        dma((2,)),
        pltpu.VMEM((4, 2, ROWS, 256), BF16),
        pltpu.VMEM((4, ROWS, 256), BF16),
        pltpu.VMEM((4, 2, ROWS, 256), BF16),
        pltpu.VMEM((4, ROWS, 256), BF16),
        pltpu.VMEM((2, ROWS, 256), F32),
        pltpu.VMEM((4, ROWS, 256), F32),
        pltpu.VMEM((ROWS, 256), BF16),
        pltpu.VMEM((4, ROWS, 256), BF16),
        pltpu.VMEM((ROWS, 256), BF16),
        pltpu.VMEM((4, ROWS, 256), BF16),
        pltpu.VMEM((2, 2, 4, ROWS, 256), BF16),
        pltpu.VMEM((ROWS, 512), BF16),
        pltpu.VMEM((2, 2, ROWS, HD), BF16),
        pltpu.VMEM((HD, NQ), F32),
        pltpu.VMEM((2, 2, ROWS, HD), BF16),
        pltpu.VMEM((ROWS, 512), BF16),
        pltpu.VMEM((2, 8, 2, ROWS, HD), BF16),
        pltpu.VMEM((2, 8, ROWS, HD), BF16),
        pltpu.VMEM((2, 8, ROWS, HD), BF16),
        pltpu.VMEM((8, 2, ROWS, HD), BF16),
        pltpu.VMEM((4, 80, HD), BF16),
        pltpu.VMEM((8, 2, ROWS, 256), BF16),
        pltpu.VMEM((8, 8, 128), F32),
        pltpu.VMEM((16, 8, 128), F32),
        dma,
        dma((4, 4)),
        dma((4,)),
        dma((4, 4)),
        dma((4,)),
        dma((4,)),
        dma((4,)),
        dma((4,)),
        dma((4,)),
        dma((2, 4)),
        dma((2,)),
        dma((2, 2)),
        dma,
        dma((2, 4)),
        dma,
        dma,
        dma,
        dma,
        dma,
        dma,
        dma((len(CUTS) - 1, 4)),
        dma((len(CUTS) - 1, 4)),
        dma((len(CUTS) - 1,)),
        dma((len(CUTS) - 1,)),
        dma((len(CUTS) - 1,)),
        dma((len(CUTS) - 1,)),
        dma((len(CUTS) - 1, 4)),
        dma((len(CUTS) - 1, 4)),
        dma((2, 2, 4, len(CUTS) - 1)),
        dma((2, 2, 4, len(CUTS) - 1)),
        dma((1, 4)),
        dma,
        dma((4, 2)),
        dma((4, 2)),
        dma,
        dma,
        dma((2, 4)),
        dma((2, 4)),
        dma((2, 2)),
        dma,
        dma((8,)),
        dma((8,)),
        dma((8,)),
        dma((8,)),
        dma((8,)),
        dma((8,)),
        dma((16,)),
        dma((16,)),
    ]
    dq, dk, dv, gw, ms = pl.pallas_call(
        kernel,
        out_shape=(
            jax.ShapeDtypeStruct((ROWS, 512), BF16),
            jax.ShapeDtypeStruct((ROWS, 512), F32),
            jax.ShapeDtypeStruct((ROWS, 512), F32),
            jax.ShapeDtypeStruct((512, 256), F32),
            jax.ShapeDtypeStruct((8, 128), F32),
        ),
        in_specs=[smem, smem] + [hbm] * 9,
        out_specs=(vmem,) * 5,
        scratch_shapes=scratch,
        compiler_params=pltpu.CompilerParams(
            collective_id=0, has_side_effects=True, vmem_limit_bytes=56 * 1024 * 1024
        ),
        cost_estimate=pl.CostEstimate(flops=7 * 10**9, bytes_accessed=8 * 10**6, transcendentals=1638400),
    )(frame_lengths, time_index, q, k, v, qd, kd, vd, w, noisy, vel)
    return pl.pallas_call(
        scaled,
        out_shape=tuple(jax.ShapeDtypeStruct(part.shape, BF16) for part in (dq, dk, dv, gw)),
        in_specs=[vmem] * 5,
        out_specs=(vmem,) * 4,
    )(ms, dq, dk, dv, gw)


def solution(mesh):
    in_specs = (P("seq", "tp"),) * 6 + (P("tp", None), P(("seq", "tp"), None), P(("seq", "tp"), None), P(), P())
    out_specs = (P("seq", "tp"), P("seq", "tp"), P("seq", "tp"), P("tp", "seq"))
    return jax.shard_map(
        on_device, mesh=mesh, in_specs=in_specs, out_specs=out_specs, check_vma=False
    )
```
